32 devices in a mesh: dp: 8 (over z, core), tensor: 4 (over y, x).
Axes of the slice: x: 2, y: 2, z: 4, core: 2. Of those that a mesh axis runs over, the one named last changes fastest.
Arguments:
- history: bfloat16 [9, 8192, 2048], P(None, 'dp', 'tensor'), may hold values from -6 to 6
- mix_in: float32 [36, 8192], P(None, 'dp'), may hold values from -2.5 to 2.5
- group_ids: int32 [8], P('dp'), may hold values from 0 to 3
- group_weight: float32 [4], replicated, may hold values from 0.3 to 3
- block_cotangent: bfloat16 [8192, 2048], P('dp', 'tensor'), may hold values from -6 to 6
- mix_cotangent: float32 [40, 8192], P(None, 'dp'), may hold values from -6 to 6
- qkv_weight: bfloat16 [3, 2048, 2048], P(None, 'dp', 'tensor'), may hold values from -0.125 to 0.125
- out_weight: bfloat16 [2048, 2048], P('tensor', 'dp'), may hold values from -2 to 2
- up_weight: bfloat16 [2048, 8192], P('dp', 'tensor'), may hold values from -0.125 to 0.125
- down_weight: bfloat16 [8192, 2048], P('tensor', 'dp'), may hold values from -0.0625 to 0.0625
- norm_gain: bfloat16 [4, 2048], P(None, 'dp'), may hold values from 0.5 to 1.5
- norm_bias: bfloat16 [4, 2048], P(None, 'dp'), may hold values from -2.5 to 2.5
- mix_weight: bfloat16 [2048, 40], P('dp'), may hold values from -0.125 to 0.125
- next_weight: bfloat16 [40, 40], replicated, may hold values from -1 to 1
Outputs:
- block_out: bfloat16 [8192, 2048], P('dp', 'tensor')
- next_mix: float32 [40, 8192], P(None, 'dp')
- history_grad: float32 [9, 8192, 2048], P(None, 'dp', 'tensor')
- mix_grad: float32 [36, 8192], P(None, 'dp')
- qkv_grad: float32 [3, 2048, 2048], P(None, 'dp', 'tensor')
- out_grad: float32 [2048, 2048], P('tensor', 'dp')
- up_grad: float32 [2048, 8192], P('dp', 'tensor')
- down_grad: float32 [8192, 2048], P('tensor', 'dp')
- gain_grad: float32 [4, 2048], P(None, 'dp')
- bias_grad: float32 [4, 2048], P(None, 'dp')
- mix_proj_grad: float32 [2048, 40], P('dp')
- next_proj_grad: float32 [40, 40], replicated
The draws below stay inside these ranges and needn't reach their ends.
All inputs are finite; a program needn't handle non-finite values.
Results may differ from the reference program's by a relative error of at most 0.024.
Values may be sent and summed in bfloat16 or wider, within the bound.
No kernel may reach another device: no remote copies, remote signals or barrier semaphores. Data moves between devices by JAX's collectives and lax.ppermute only.
A program may use at most 256 MiB of HBM per device.

```python
import math
import jax
import jax.numpy as jnp
from jax import lax

D = 2048
HEADS = 16
HEAD_DIM = 128
FF = 8192
ROT = 32
STREAMS = 4
ENTRIES = 9
GROUPS = 4
LENGTH = 1024
SEQS = 8
TOKENS = 8192
MIX_IN = 36
MIX_OUT = 40


def with_ends(array, rng, smallest, largest):
    place = [jax.random.randint(jax.random.fold_in(rng, axis), (), 0, length) for axis, length in enumerate(array.shape)]
    longest = array.shape.index(max(array.shape))
    next_to = place[:longest] + [(place[longest] + 1) % array.shape[longest]] + place[longest + 1:]
    return array.at[tuple(place)].set(smallest).at[tuple(next_to)].set(largest)


def shard_levels(own_key, dims, split, least, top_value):
    level, own = 1.0, jax.random.fold_in(own_key, 6)
    for dim, parts in split:
        draws = jnp.exp(jax.random.uniform(jax.random.fold_in(own, dim), (parts,), jnp.float32, least / len(split), top_value / len(split)))
        level = level * jnp.repeat(draws, dims[dim] // parts).reshape([-1 if axis == dim else 1 for axis in range(len(dims))])
    return level


def gaussian(stream_key, dims, scale, bound, shards=(), kind=jnp.bfloat16):
    level = shard_levels(stream_key, dims, shards, -0.22, 0.18) if shards else 1.0
    array = jax.random.normal(stream_key, dims, jnp.float32) * scale * level
    return jnp.minimum(jnp.maximum(array, -bound), bound).astype(kind)


def setup_inputs(seed: int = 0) -> dict:
    splits = jax.random.split(jax.random.key(seed), 15)
    return {
        "history": gaussian(splits[0], (ENTRIES, TOKENS, D), 1.0, 6.0, ((1, 8), (2, 4))),
        "mix_in": gaussian(splits[1], (MIX_IN, TOKENS), 0.35, 2.5, ((1, 8),), jnp.float32),
        "group_ids": with_ends(jax.random.randint(splits[2], (SEQS,), 0, GROUPS), jax.random.fold_in(splits[2], 1), 0, GROUPS - 1).astype(jnp.int32),
        "group_weight": jnp.clip(jnp.exp(jax.random.uniform(splits[3], (GROUPS,), jnp.float32, math.log(0.3), math.log(3.0))), 0.3, 3.0),
        "block_cotangent": gaussian(splits[4], (TOKENS, D), 1.0, 6.0, ((0, 8), (1, 4))),
        "mix_cotangent": gaussian(splits[5], (MIX_OUT, TOKENS), 1.0, 6.0, ((1, 8),), jnp.float32),
        "qkv_weight": gaussian(splits[6], (3, D, D), D ** -0.5, 0.125, ((1, 8), (2, 4))),
        "out_weight": gaussian(splits[7], (D, D), (max(D // 256, 1)) ** -0.5, 2.0, ((0, 4), (1, 8))),
        "up_weight": gaussian(splits[8], (D, FF), D ** -0.5, 0.125, ((0, 8), (1, 4))),
        "down_weight": gaussian(splits[9], (FF, D), FF ** -0.5, 0.0625, ((0, 4), (1, 8))),
        "norm_gain": jnp.clip(1.0 + 0.1 * jax.random.normal(splits[10], (STREAMS, D), jnp.float32), 0.5, 1.5).astype(jnp.bfloat16),
        "norm_bias": gaussian(splits[11], (STREAMS, D), 0.3, 2.5, ((1, 8),)),
        "mix_weight": gaussian(splits[12], (D, MIX_OUT), D ** -0.5, 0.125, ((0, 8),)),
        "next_weight": gaussian(splits[13], (MIX_OUT, MIX_OUT), MIX_OUT ** -0.5, 1.0),
    }


ln_eps = 1e-05
rms_eps = 1e-06
big_negative = -1e+30

@jax.custom_vjp
def low(v):
    return lax.optimization_barrier(v.astype(jnp.bfloat16)).astype(jnp.float32)

@jax.custom_vjp
def low_back(v):
    return v

def low_keep(v):
    return (low(v), None)

def low_pass(kept, grad):
    return (grad,)

def back_keep(v):
    return (v, None)

def back_low(kept, grad):
    return (low(grad),)
low.defvjp(low_keep, low_pass)
low_back.defvjp(back_keep, back_low)

def matmul_high(left, right):
    return jnp.dot(left, right, precision=lax.Precision.HIGHEST, preferred_element_type=jnp.float32)

def layer_norm(values, gain, shift):
    center = lax.optimization_barrier(jnp.mean(values, axis=-1, keepdims=True))
    offset = values - center
    spread = lax.optimization_barrier(jnp.mean(offset * offset, axis=-1, keepdims=True))
    return offset * lax.rsqrt(spread + ln_eps) * gain + shift

def rotary_tables(count):
    places = (jnp.arange(count, dtype=jnp.int32) % LENGTH).astype(jnp.float32)
    freqs = jnp.power(10000.0, -jnp.arange(0, ROT, 2).astype(jnp.float32) / ROT)
    angles = places[:, None] * freqs[None, :]
    return (jnp.cos(angles), jnp.sin(angles))

def rotate(values, cosine, sine):
    halfway = ROT // 2
    first_half = values[..., :halfway]
    second_half = values[..., halfway:ROT]
    cos_wide = cosine[:, None, :]
    sin_wide = sine[:, None, :]
    return jnp.concatenate([first_half * cos_wide - second_half * sin_wide, second_half * cos_wide + first_half * sin_wide, values[..., ROT:]], axis=-1)

def attend(queries, key_heads, value_heads):
    block_rows = min(512, LENGTH)
    count = LENGTH // block_rows
    score_scale = HEAD_DIM ** (-0.5)
    blocks = queries.reshape(count, block_rows, HEADS, HEAD_DIM)
    key_place = jnp.arange(LENGTH, dtype=jnp.int32)

    def one_block(pair):
        block, first = pair
        scores = jnp.einsum('qhd,khd->hqk', block, key_heads, precision=lax.Precision.HIGHEST) * score_scale
        scores = low_back(scores)
        query_place = first + jnp.arange(block_rows, dtype=jnp.int32)
        allowed = key_place[None, :] <= query_place[:, None]
        scores = jnp.where(allowed[None], scores, big_negative)
        summit = lax.optimization_barrier(jnp.max(scores, axis=-1, keepdims=True))
        exponent = jnp.exp(scores - summit)
        probs = exponent / lax.optimization_barrier(jnp.sum(exponent, axis=-1, keepdims=True))
        return jnp.einsum('hqk,khd->qhd', low(probs), value_heads, precision=lax.Precision.HIGHEST)
    starts = jnp.arange(count, dtype=jnp.int32) * block_rows
    return lax.map(jax.checkpoint(one_block), (blocks, starts)).reshape(LENGTH, HEADS * HEAD_DIM)

def forward(history, mix_in, qkv_weight, out_weight, up_weight, down_weight, norm_gain, norm_bias, mix_weight, next_weight, cosine, sine):
    coeffs = mix_in.reshape(STREAMS, ENTRIES, LENGTH)
    streams = jnp.einsum('cet,etd->ctd', coeffs, history, precision=lax.Precision.HIGHEST)
    normed = low(layer_norm(streams, norm_gain[:, None, :], norm_bias[:, None, :]))
    q_lin = low_back(matmul_high(normed[0], qkv_weight[0])).reshape(LENGTH, HEADS, HEAD_DIM)
    k_lin = low_back(matmul_high(normed[1], qkv_weight[1])).reshape(LENGTH, HEADS, HEAD_DIM)
    queries = low(rotate(q_lin, cosine, sine))
    key_heads = low(rotate(k_lin, cosine, sine))
    value_heads = low(low_back(matmul_high(normed[2], qkv_weight[2]))).reshape(LENGTH, HEADS, HEAD_DIM)
    attended = low(low_back(attend(queries, key_heads, value_heads)))
    hidden_pre = low_back(matmul_high(normed[3], up_weight))
    hidden = low(jax.nn.gelu(hidden_pre, approximate=False))
    branch = low_back(matmul_high(attended, out_weight) + matmul_high(hidden, down_weight))
    block = low(streams[3] + branch)
    square = lax.optimization_barrier(jnp.mean(block * block, axis=-1, keepdims=True))
    scaled = low(block * lax.rsqrt(square + rms_eps))
    pre_mix = low_back(matmul_high(scaled, mix_weight))
    mix_hidden = low(jax.nn.gelu(pre_mix, approximate=False))
    next_mix = low_back(matmul_high(mix_hidden, next_weight))
    return (block, next_mix.T)

def reference(history, mix_in, group_ids, group_weight, block_cotangent, mix_cotangent, qkv_weight, out_weight, up_weight, down_weight, norm_gain, norm_bias, mix_weight, next_weight):
    weights = tuple((item.astype(jnp.float32) for item in (qkv_weight, out_weight, up_weight, down_weight, norm_gain, norm_bias, mix_weight, next_weight)))
    cosine, sine = rotary_tables(LENGTH)
    token_scale = group_weight[group_ids]

    def one_sequence(totals, index):
        first = index * LENGTH
        hist_seq = lax.dynamic_slice_in_dim(history, first, LENGTH, 1).astype(jnp.float32)
        mix_seq = lax.dynamic_slice_in_dim(mix_in, first, LENGTH, 1)
        factor = token_scale[index]
        block_seed = lax.dynamic_slice_in_dim(block_cotangent, first, LENGTH, 0).astype(jnp.float32) * factor
        mix_seed = lax.dynamic_slice_in_dim(mix_cotangent, first, LENGTH, 1) * factor

        def run_layer(hist_arg, mix_arg, *params):
            return forward(hist_arg, mix_arg, *params, cosine, sine)
        outputs, pull = jax.vjp(run_layer, hist_seq, mix_seq, *weights)
        grads = pull((block_seed, mix_seed))
        totals = tuple((total + grad for total, grad in zip(totals, grads[2:])))
        return (totals, (outputs[0].astype(jnp.bfloat16), outputs[1], grads[0], grads[1]))
    zeros = tuple((jnp.zeros(item.shape, jnp.float32) for item in weights))
    totals, stacked = lax.scan(one_sequence, zeros, jnp.arange(SEQS, dtype=jnp.int32))
    blocks, mixes, hist_grads, mix_grads = stacked
    block_out = blocks.reshape(TOKENS, D)
    next_mix = jnp.transpose(mixes, (1, 0, 2)).reshape(MIX_OUT, TOKENS)
    history_grad = jnp.transpose(hist_grads, (1, 0, 2, 3)).reshape(ENTRIES, TOKENS, D)
    mix_grad = jnp.transpose(mix_grads, (1, 0, 2)).reshape(MIX_IN, TOKENS)
    return (block_out, next_mix, history_grad, mix_grad, totals[0], totals[1], totals[2], totals[3], totals[4], totals[5], totals[6], totals[7])
```

```python
import jax
import jax.numpy as jnp
from jax import lax
from jax.sharding import PartitionSpec as P

HEAD_DIM = 128
ROT = 32
STREAMS = 4
ENTRIES = 9
LENGTH = 1024


ln_eps = 1e-05
rms_eps = 1e-06
big_negative = -1e30
root_half = 0.7071067811865476
inv_root_tau = 0.3989422804014327


def gelu_exact(values):
    return jax.nn.gelu(values, approximate=False)


def gelu_slope(values):
    return (
        0.5 * (1.0 + lax.erf(values * root_half))
        + values * jnp.exp(-0.5 * values * values) * inv_root_tau
    )


def rotary_tables(count):
    places = (jnp.arange(count, dtype=jnp.int32) % LENGTH).astype(jnp.float32)
    freqs = jnp.power(10000.0, -jnp.arange(0, ROT, 2).astype(jnp.float32) / ROT)
    angles = places[:, None] * freqs[None, :]
    return (jnp.cos(angles), jnp.sin(angles))


def rotate(values, cosine, sine):
    halfway = ROT // 2
    first_half = values[..., :halfway]
    second_half = values[..., halfway:ROT]
    cos_wide = cosine[:, None, :]
    sin_wide = sine[:, None, :]
    return jnp.concatenate(
        [
            first_half * cos_wide - second_half * sin_wide,
            second_half * cos_wide + first_half * sin_wide,
            values[..., ROT:],
        ],
        axis=-1,
    )


def local_dot(left, right):
    return jnp.dot(left, right, preferred_element_type=jnp.float32)


def contract_rows(left, right):
    return lax.dot_general(
        left, right, (((0,), (0,)), ((), ())), preferred_element_type=jnp.float32
    )


def contract_cols(left, right):
    return lax.dot_general(
        left, right, (((1,), (1,)), ((), ())), preferred_element_type=jnp.float32
    )


def masked_scores(queries, key_heads, block_start, block_stop):
    score_scale = queries.shape[2] ** (-0.5)
    scores = (
        jnp.einsum(
            "qhd,khd->hqk",
            queries[block_start:block_stop],
            key_heads[:block_stop],
            preferred_element_type=jnp.float32,
        )
        * score_scale
    )
    allowed = (
        jnp.arange(block_stop)[None, :]
        <= (block_start + jnp.arange(block_stop - block_start))[:, None]
    )
    return jnp.where(allowed[None], scores, big_negative)


def attention_forward(queries, key_heads, value_heads):
    length = queries.shape[0]
    block_rows = min(512, length)
    outputs = []
    totals = []
    for number in range(length // block_rows):
        block_start = number * block_rows
        block_stop = block_start + block_rows
        scores = masked_scores(queries, key_heads, block_start, block_stop)
        summit = jnp.max(scores, axis=-1, keepdims=True)
        exponent = jnp.exp(scores - summit)
        partition = jnp.sum(exponent, axis=-1, keepdims=True)
        weights_low = (exponent / partition).astype(jnp.bfloat16)
        outputs.append(
            jnp.einsum(
                "hqk,khd->qhd",
                weights_low,
                value_heads[:block_stop],
                preferred_element_type=jnp.float32,
            )
        )
        totals.append(summit + jnp.log(partition))
    return (jnp.concatenate(outputs, 0).astype(jnp.bfloat16), totals)


def attention_backward(queries, key_heads, value_heads, grad_out, totals):
    length = queries.shape[0]
    block_rows = min(512, length)
    score_scale = queries.shape[2] ** (-0.5)
    key_grad = jnp.zeros(key_heads.shape, jnp.float32)
    value_grad = jnp.zeros(value_heads.shape, jnp.float32)
    query_grads = []
    for number in range(length // block_rows):
        block_start = number * block_rows
        block_stop = block_start + block_rows
        scores = masked_scores(queries, key_heads, block_start, block_stop)
        probs = jnp.exp(scores - totals[number])
        probs_low = probs.astype(jnp.bfloat16)
        grad_rows = grad_out[block_start:block_stop]
        prob_grad = jnp.einsum(
            "qhd,khd->hqk", grad_rows, value_heads[:block_stop], preferred_element_type=jnp.float32
        )
        value_grad = value_grad.at[:block_stop].add(
            jnp.einsum("hqk,qhd->khd", probs_low, grad_rows, preferred_element_type=jnp.float32)
        )
        center = jnp.sum(probs * prob_grad, axis=-1, keepdims=True)
        score_grad = (probs * (prob_grad - center)).astype(jnp.bfloat16)
        query_grads.append(
            jnp.einsum(
                "hqk,khd->qhd",
                score_grad,
                key_heads[:block_stop],
                preferred_element_type=jnp.float32,
            )
            * score_scale
        )
        key_grad = key_grad.at[:block_stop].add(
            jnp.einsum(
                "hqk,qhd->khd",
                score_grad,
                queries[block_start:block_stop],
                preferred_element_type=jnp.float32,
            )
            * score_scale
        )
    return (jnp.concatenate(query_grads, 0), key_grad, value_grad)


def swap(values, axis, bit):
    count = lax.axis_size(axis)
    return lax.ppermute(values, axis, [(i, i ^ bit) for i in range(count)])


def axis_bits(axis):
    count = lax.axis_size(axis)
    return [1 << b for b in range(count.bit_length() - 1)]


def butterfly_sum(values, axis):
    for bit in axis_bits(axis):
        values = values + swap(values, axis, bit)
    return values


def gather_pieces(own):
    bits = axis_bits("tensor")
    half = own.shape[0] // 2
    if len(bits) == 2:
        one = swap(own, "tensor", 1)
        two = swap(own, "tensor", 2)
        top = swap(one[:half], "tensor", 2)
        bottom = swap(two[half:], "tensor", 1)
        return {0: own, 1: one, 2: two, 3: jnp.concatenate([top, bottom], 0)}
    halves = []
    for part, order in ((own[:half], bits), (own[half:], bits[::-1])):
        held = {0: part}
        for bit in order:
            keys = list(held)
            got = swap(jnp.stack([held[k] for k in keys]), "tensor", bit)
            for number, k in enumerate(keys):
                held[k ^ bit] = got[number]
        halves.append(held)
    return {k: jnp.concatenate([halves[0][k], halves[1][k]], 0) for k in halves[0]}


def gather_columns(own):
    place = lax.axis_index("tensor")
    width = own.shape[1]
    pieces = gather_pieces(own)
    whole = jnp.zeros((own.shape[0], width * len(pieces)), own.dtype)
    for key, piece in pieces.items():
        whole = lax.dynamic_update_slice_in_dim(whole, piece, (place ^ key) * width, 1)
    return whole


def scatter_columns(partial):
    place = lax.axis_index("tensor")
    count = lax.axis_size("tensor")
    width = partial.shape[1] // count
    half = partial.shape[0] // 2
    bits = axis_bits("tensor")
    sums = []
    for number, order in enumerate((bits, bits[::-1])):
        rows = partial[number * half : (number + 1) * half]
        held = {
            k: lax.dynamic_slice_in_dim(rows, (place ^ k) * width, width, 1) for k in range(count)
        }
        for bit in order:
            sent = [k for k in held if k & bit]
            got = swap(jnp.stack([held[k] for k in sent]).astype(jnp.bfloat16), "tensor", bit)
            for spot, k in enumerate(sent):
                held[k ^ bit] = held[k ^ bit].astype(jnp.float32) + got[spot].astype(jnp.float32)
                del held[k]
        sums.append(held[0])
    return jnp.concatenate(sums, 0)


def per_device(
    history,
    mix_in,
    group_ids,
    group_weight,
    block_cotangent,
    mix_cotangent,
    qkv_weight,
    out_weight,
    up_weight,
    down_weight,
    norm_gain,
    norm_bias,
    mix_weight,
    next_weight,
):
    tensor_count = lax.axis_size("tensor")
    tensor_place = lax.axis_index("tensor")
    dp_place = lax.axis_index("dp")
    tokens = history.shape[1]
    width_own = history.shape[2]
    width_all = width_own * tensor_count
    column_start = tensor_place * width_own
    share = norm_gain.shape[1]
    mix_out = mix_weight.shape[1]

    cot_full = gather_columns(block_cotangent)
    smalls = jnp.concatenate([norm_gain.T, norm_bias.T, mix_weight], 1)
    smalls = lax.all_gather(smalls, "dp", axis=0, tiled=True)
    gain_flat = smalls[:, :STREAMS].T.astype(jnp.float32)
    bias_flat = smalls[:, STREAMS : 2 * STREAMS].T.astype(jnp.float32)
    mix_full = smalls[:, 2 * STREAMS :]
    qkv_full = lax.all_gather(qkv_weight, "dp", axis=1, tiled=True)
    up_full = lax.all_gather(up_weight, "dp", axis=0, tiled=True)
    down_full = lax.all_gather(down_weight, "dp", axis=1, tiled=True)
    out_full = lax.all_gather(out_weight, "dp", axis=1, tiled=True)
    heads_own = qkv_full.shape[2] // HEAD_DIM
    coeffs = mix_in.reshape(STREAMS, ENTRIES, tokens)
    streams_own = jnp.zeros((STREAMS, tokens, width_own), jnp.float32)
    for entry in range(ENTRIES):
        streams_own = (
            streams_own + coeffs[:, entry, :, None] * history[entry].astype(jnp.float32)[None]
        )
    gain_own = lax.dynamic_slice_in_dim(gain_flat, column_start, width_own, 1)[:, None, :]
    bias_own = lax.dynamic_slice_in_dim(bias_flat, column_start, width_own, 1)[:, None, :]
    residual_own = streams_own[3]
    stats = butterfly_sum(
        jnp.concatenate(
            [jnp.sum(streams_own, axis=-1), jnp.sum(streams_own * streams_own, axis=-1)], 0
        ),
        "tensor",
    )
    center = stats[:STREAMS, :, None] / width_all
    inv_spread = lax.rsqrt(stats[STREAMS:, :, None] / width_all - center * center + ln_eps)
    unit_own = (streams_own - center) * inv_spread
    normed_own = (unit_own * gain_own + bias_own).astype(jnp.bfloat16)
    normed = [gather_columns(normed_own[c]) for c in range(STREAMS)]
    cosine, sine = rotary_tables(tokens)
    q_lin = local_dot(normed[0], qkv_full[0]).reshape(tokens, heads_own, HEAD_DIM)
    k_lin = local_dot(normed[1], qkv_full[1]).reshape(tokens, heads_own, HEAD_DIM)
    q_rot, query_pull = jax.vjp(lambda values: rotate(values, cosine, sine), q_lin)
    k_rot, key_pull = jax.vjp(lambda values: rotate(values, cosine, sine), k_lin)
    queries = q_rot.astype(jnp.bfloat16)
    key_heads = k_rot.astype(jnp.bfloat16)
    value_heads = (
        local_dot(normed[2], qkv_full[2])
        .astype(jnp.bfloat16)
        .reshape(tokens, heads_own, HEAD_DIM)
    )
    result, totals = attention_forward(queries, key_heads, value_heads)
    attended = result.reshape(tokens, heads_own * HEAD_DIM)
    hidden_pre = local_dot(normed[3], up_full)
    hidden = gelu_exact(hidden_pre).astype(jnp.bfloat16)
    partial_branch = local_dot(attended, out_full) + local_dot(hidden, down_full)
    branch_own = scatter_columns(partial_branch.astype(jnp.bfloat16))
    block_own = (residual_own + branch_own).astype(jnp.bfloat16)
    block_full = gather_columns(block_own)
    block_wide = block_full.astype(jnp.float32)
    root_inv = lax.rsqrt(jnp.mean(block_wide * block_wide, axis=-1, keepdims=True) + rms_eps)
    scaled = (block_wide * root_inv).astype(jnp.bfloat16)
    pre_mix = local_dot(scaled, mix_full)
    mix_hidden = gelu_exact(pre_mix).astype(jnp.bfloat16)
    next_mix = local_dot(mix_hidden, next_weight).T
    member = (group_ids[:, None] == jnp.arange(group_weight.shape[0])[None, :]).astype(jnp.float32)
    seq_scale = jnp.sum(member * group_weight[None, :], axis=1)
    token_scale = jnp.repeat(seq_scale, LENGTH)
    mix_seed = (mix_cotangent * token_scale[None, :]).T.astype(jnp.bfloat16)
    next_part = contract_rows(mix_hidden, mix_seed)
    mix_hidden_grad = contract_cols(mix_seed, next_weight)
    pre_mix_grad = (mix_hidden_grad * gelu_slope(pre_mix)).astype(jnp.bfloat16)
    mix_part = contract_rows(pre_mix_grad, scaled)
    scaled_grad = contract_cols(pre_mix_grad, mix_full)
    block_grad = (
        root_inv * scaled_grad
        - block_wide
        * root_inv
        * root_inv
        * root_inv
        * jnp.mean(scaled_grad * block_wide, axis=-1, keepdims=True)
        + cot_full.astype(jnp.float32) * token_scale[:, None]
    )
    branch_grad = block_grad.astype(jnp.bfloat16)
    block_grad_own = lax.dynamic_slice_in_dim(block_grad, column_start, width_own, 1)
    down_part = contract_rows(hidden, branch_grad)
    down_grad = lax.psum_scatter(
        down_part.astype(jnp.bfloat16), "dp", scatter_dimension=1, tiled=True
    ).astype(jnp.float32)
    hidden_grad = contract_cols(branch_grad, down_full)
    hidden_pre_grad = (hidden_grad * gelu_slope(hidden_pre)).astype(jnp.bfloat16)
    up_part = contract_rows(normed[3], hidden_pre_grad)
    up_grad = lax.psum_scatter(
        up_part.astype(jnp.bfloat16), "dp", scatter_dimension=0, tiled=True
    ).astype(jnp.float32)
    normed_grads = [None] * STREAMS
    normed_grads[3] = scatter_columns(
        contract_cols(hidden_pre_grad, up_full).astype(jnp.bfloat16)
    )
    out_part = contract_rows(attended, branch_grad)
    out_grad = lax.psum_scatter(
        out_part.astype(jnp.bfloat16), "dp", scatter_dimension=1, tiled=True
    ).astype(jnp.float32)
    attended_grad = (
        contract_cols(branch_grad, out_full)
        .astype(jnp.bfloat16)
        .reshape(tokens, heads_own, HEAD_DIM)
    )
    q_grad, k_grad, v_grad = attention_backward(
        queries, key_heads, value_heads, attended_grad, totals
    )
    lin_grads = [
        query_pull(q_grad)[0].astype(jnp.bfloat16).reshape(tokens, heads_own * HEAD_DIM),
        key_pull(k_grad)[0].astype(jnp.bfloat16).reshape(tokens, heads_own * HEAD_DIM),
        v_grad.astype(jnp.bfloat16).reshape(tokens, heads_own * HEAD_DIM),
    ]
    for c in range(3):
        normed_grads[c] = scatter_columns(
            contract_cols(lin_grads[c], qkv_full[c]).astype(jnp.bfloat16)
        )
    qkv_part = jnp.stack(
        [contract_rows(normed[c], lin_grads[c]).astype(jnp.bfloat16) for c in range(3)], 0
    )
    qkv_grad = lax.psum_scatter(qkv_part, "dp", scatter_dimension=1, tiled=True).astype(jnp.float32)
    normed_grad_own = jnp.stack(normed_grads, 0)
    gain_scaled = normed_grad_own * gain_own
    sums = butterfly_sum(
        jnp.concatenate(
            [jnp.sum(gain_scaled, axis=-1), jnp.sum(gain_scaled * unit_own, axis=-1)], 0
        ),
        "tensor",
    )
    sum_plain = sums[:STREAMS, :, None]
    sum_unit = sums[STREAMS:, :, None]
    stream_grad = inv_spread * (
        gain_scaled - sum_plain / width_all - unit_own * (sum_unit / width_all)
    )
    stream_grad = stream_grad.at[3].add(block_grad_own)
    entry_grads = []
    entry_mixes = []
    for entry in range(ENTRIES):
        entry_grads.append(jnp.sum(coeffs[:, entry, :, None] * stream_grad, axis=0))
        entry_mixes.append(jnp.sum(stream_grad * history[entry].astype(jnp.float32)[None], axis=-1))
    history_grad = jnp.stack(entry_grads, 0)
    mix_grad = butterfly_sum(
        jnp.stack(entry_mixes, 1).reshape(STREAMS * ENTRIES, tokens), "tensor"
    )
    norm_part = butterfly_sum(
        jnp.concatenate(
            [jnp.sum(normed_grad_own * unit_own, axis=1), jnp.sum(normed_grad_own, axis=1)], 0
        ),
        "dp",
    )
    norm_whole = lax.dynamic_slice_in_dim(gather_columns(norm_part), dp_place * share, share, 1)
    gain_grad = norm_whole[:STREAMS]
    bias_grad = norm_whole[STREAMS:]
    next_row = jnp.pad(next_part, ((0, 0), (0, width_all - next_part.shape[1])))
    mix_sums = butterfly_sum(jnp.concatenate([mix_part, next_row], 0), "dp")
    mix_proj_grad = lax.dynamic_slice_in_dim(mix_sums[:mix_out], dp_place * share, share, 1).T
    next_proj_grad = mix_sums[mix_out:, : next_part.shape[1]]
    return (
        block_own,
        next_mix,
        history_grad,
        mix_grad,
        qkv_grad,
        out_grad,
        up_grad,
        down_grad,
        gain_grad,
        bias_grad,
        mix_proj_grad,
        next_proj_grad,
    )


def solution(mesh):
    placed = (
        P(None, "dp", "tensor"),
        P(None, "dp"),
        P("dp"),
        P(),
        P("dp", "tensor"),
        P(None, "dp"),
        P(None, "dp", "tensor"),
        P("tensor", "dp"),
        P("dp", "tensor"),
        P("tensor", "dp"),
        P(None, "dp"),
        P(None, "dp"),
        P("dp", None),
        P(),
    )
    return jax.shard_map(
        per_device,
        mesh=mesh,
        in_specs=placed,
        out_specs=(
            P("dp", "tensor"),
            P(None, "dp"),
            P(None, "dp", "tensor"),
            P(None, "dp"),
            P(None, "dp", "tensor"),
            P("tensor", "dp"),
            P("dp", "tensor"),
            P("tensor", "dp"),
            P(None, "dp"),
            P(None, "dp"),
            P("dp", None),
            P(),
        ),
        check_vma=False,
    )
```

```python
import functools

import jax
import jax.numpy as jnp
import numpy as np
from jax import lax
from jax.experimental import pallas as pl
from jax.experimental.pallas import tpu as pltpu
from jax.sharding import PartitionSpec as P

HEAD_DIM = 128
ROT = 32
STREAMS = 4
ENTRIES = 9
LENGTH = 1024
LANES = 128

ln_eps = 1e-05
rms_eps = 1e-06
big_negative = -1e30
root_half = 0.7071067811865476
inv_root_tau = 0.3989422804014327
F32 = jnp.float32
BF16 = jnp.bfloat16
VMEM_BYTES = 56 * 1024 * 1024

NN = (((1,), (0,)), ((), ()))
NT = (((1,), (1,)), ((), ()))
TN = (((0,), (0,)), ((), ()))


def mul(left, right, dims=NN):
    return lax.dot_general(left, right, dims, preferred_element_type=F32)


def kernel_call(body, grid, place, ins, outs, name, flops=0, scratch=()):
    moved = sum(a.size * a.dtype.itemsize for a, _, _ in ins)
    moved += sum(int(np.prod(s)) * jnp.dtype(d).itemsize for s, d, _, _ in outs)
    call = pl.pallas_call(
        body,
        out_shape=[jax.ShapeDtypeStruct(s, d) for s, d, _, _ in outs],
        grid_spec=pltpu.PrefetchScalarGridSpec(
            num_scalar_prefetch=1,
            grid=grid,
            in_specs=[pl.BlockSpec(b, m) for _, b, m in ins],
            out_specs=[pl.BlockSpec(b, m) for _, _, b, m in outs],
            scratch_shapes=[pltpu.VMEM(shape, dtype) for shape, dtype in scratch],
        ),
        compiler_params=pltpu.CompilerParams(
            vmem_limit_bytes=VMEM_BYTES,
            dimension_semantics=("arbitrary",) * len(grid),
        ),
        cost_estimate=pl.CostEstimate(
            flops=int(flops), bytes_accessed=int(moved), transcendentals=0
        ),
        name=name,
    )
    return call(place, *[a for a, _, _ in ins])


def const(*zeros):
    return lambda *_: zeros


def group_parts(refs, shape):
    groups, spot = [], 0
    for parts in shape:
        groups.append(refs[spot : spot + parts])
        spot += parts
    return groups, refs[spot:]


def joined(parts):
    if len(parts) == 1:
        return parts[0][...]
    return jnp.concatenate([part[...] for part in parts], 0)


def normal_parts(x):
    size = jnp.abs(x) * root_half
    lower = 1.0 + 0.3275911 * size
    t = 1.0 / lower
    poly = t * (
        0.254829592
        + t * (-0.284496736 + t * (1.421413741 + t * (-1.453152027 + t * 1.061405429)))
    )
    bell = jnp.exp(-0.5 * x * x)
    tail = 0.5 * poly * bell
    cumulative = jnp.where(x < 0, tail, 1.0 - tail)
    return cumulative, bell * inv_root_tau


def lanes_to_rows(columns, rows):
    lane = lax.broadcasted_iota(jnp.int32, (columns[0].shape[0], LANES), 1)
    wide = jnp.zeros((columns[0].shape[0], LANES), F32)
    for number, column in enumerate(columns):
        wide = jnp.where(lane == number, column, wide)
    return wide.T[:rows]


def mix_kernel(place, hist, coef, streams, stats):
    totals = [None] * STREAMS
    for e in range(ENTRIES):
        entry = hist[e].astype(F32)
        for c in range(STREAMS):
            k = c * ENTRIES + e
            term = coef[:, k : k + 1] * entry
            totals[c] = term if totals[c] is None else totals[c] + term
    columns = []
    for c in range(STREAMS):
        streams[c] = totals[c]
        columns.append(jnp.sum(totals[c], axis=1, keepdims=True))
    for c in range(STREAMS):
        columns.append(jnp.sum(totals[c] * totals[c], axis=1, keepdims=True))
    stats[...] = lanes_to_rows(columns, 2 * STREAMS)


def rows_to_lanes(rows):
    tall = jnp.concatenate([rows, jnp.zeros((LANES - rows.shape[0], LANES), F32)], 0)
    return tall.T


def center_and_spread(stats, width_all):
    turned = rows_to_lanes(stats)
    centers, spreads = [], []
    for c in range(STREAMS):
        center = turned[:, c : c + 1] / width_all
        square = turned[:, STREAMS + c : STREAMS + c + 1] / width_all
        centers.append(center)
        spreads.append(lax.rsqrt(square - center * center + ln_eps))
    return centers, spreads


def norm_kernel(width_all, place, streams, stats, gain, bias, first, last):
    centers, spreads = center_and_spread(stats[...], width_all)
    for c in range(STREAMS):
        unit = (streams[c] - centers[c]) * spreads[c]
        normed = (unit * gain[c : c + 1] + bias[c : c + 1]).astype(BF16)
        if c < STREAMS - 1:
            first[c] = normed
        else:
            last[...] = normed


def spread_kernel(width_all, place, streams, stats, hist, out):
    centers, spreads = center_and_spread(stats[...], width_all)
    units = [(streams[c] - centers[c]) * spreads[c] for c in range(STREAMS)]
    columns = []
    entries = [hist[e].astype(F32) for e in range(ENTRIES)]
    for c in range(STREAMS):
        for e in range(ENTRIES):
            columns.append(jnp.sum(units[c] * entries[e], axis=1, keepdims=True))
    for e in range(ENTRIES):
        columns.append(jnp.sum(entries[e], axis=1, keepdims=True))
    out[...] = lanes_to_rows(columns, out.shape[0])


def turn(x, cosine, ahead, behind):
    half = ROT // 2
    return x * cosine + pltpu.roll(x, half, 1) * ahead + pltpu.roll(x, LANES - half, 1) * behind


def qkv_kernel(shape, place, *refs):
    pieces, refs = group_parts(refs, shape)
    count = len(shape)
    weights, (cosine, ahead, behind, out) = refs[:count], refs[count:]
    total = mul(joined(pieces[0]), weights[0][...])
    for r in range(1, count):
        total += mul(joined(pieces[r]), weights[r][...])
    c = pl.program_id(0)

    @pl.when(c < 2)
    def _():
        for h in range(total.shape[1] // HEAD_DIM):
            spot = slice(h * HEAD_DIM, (h + 1) * HEAD_DIM)
            turned = turn(total[:, spot], cosine[...], ahead[...], behind[...])
            out[:, spot] = turned.astype(BF16)

    @pl.when(c == 2)
    def _():
        out[...] = total.astype(BF16)


ROWS = 256


def attend_kernel(place, q, k, v, out):
    scale = HEAD_DIM**-0.5
    for number in range(q.shape[0] // ROWS):
        start, stop = number * ROWS, (number + 1) * ROWS
        scores = mul(q[start:stop], k[:stop], NT) * scale
        row = lax.broadcasted_iota(jnp.int32, scores.shape, 0) + start
        col = lax.broadcasted_iota(jnp.int32, scores.shape, 1)
        scores = jnp.where(col <= row, scores, big_negative)
        summit = jnp.max(scores, axis=1, keepdims=True)
        exponent = jnp.exp(scores - summit)
        part = jnp.sum(exponent, axis=1, keepdims=True)
        probs = (exponent * (1.0 / part)).astype(BF16)
        out[start:stop] = mul(probs, v[:stop]).astype(BF16)


def attend_back_kernel(place, q, k, v, grad, cosine, ahead, behind, out, dk, dv):
    scale = HEAD_DIM**-0.5
    dk[...] = jnp.zeros_like(dk)
    dv[...] = jnp.zeros_like(dv)
    for number in range(q.shape[0] // ROWS):
        start, stop = number * ROWS, (number + 1) * ROWS
        here = slice(start, stop)
        scores = mul(k[:stop], q[here], NT) * scale
        row = lax.broadcasted_iota(jnp.int32, scores.shape, 0)
        col = lax.broadcasted_iota(jnp.int32, scores.shape, 1) + start
        scores = jnp.where(row <= col, scores, big_negative)
        summit = jnp.max(scores, axis=0, keepdims=True)
        exponent = jnp.exp(scores - summit)
        part = jnp.sum(exponent, axis=0, keepdims=True)
        probs = exponent * (1.0 / part)
        prob_grad = mul(v[:stop], grad[here], NT)
        dv[:stop] += mul(probs.astype(BF16), grad[here])
        center = jnp.sum(probs * prob_grad, axis=0, keepdims=True)
        score_grad = (probs * (prob_grad - center)).astype(BF16)
        dk[:stop] += mul(score_grad, q[here])
        query_grad = mul(score_grad, k[:stop], TN) * scale
        out[0, here] = turn(
            query_grad, cosine[here], -ahead[here], -behind[here]
        ).astype(BF16)
    out[1] = turn(dk[...] * scale, cosine[...], -ahead[...], -behind[...]).astype(BF16)
    out[2] = dv[...].astype(BF16)


def part_rows(parts, start, rows):
    for part in parts:
        if start < part.shape[0]:
            return part[start : start + rows]
        start -= part.shape[0]


def up_kernel(shape, place, *refs):
    pieces, refs = group_parts(refs, shape)
    count = len(shape)
    weights, (hidden, slope) = refs[:count], refs[count:]
    for m in range(hidden.shape[0] // ROWS):
        here = slice(m * ROWS, (m + 1) * ROWS)
        total = mul(part_rows(pieces[0], m * ROWS, ROWS), weights[0][...])
        for r in range(1, count):
            total += mul(part_rows(pieces[r], m * ROWS, ROWS), weights[r][...])
        cumulative, density = normal_parts(total)
        hidden[here] = (total * cumulative).astype(BF16)
        slope[here] = (cumulative + total * density).astype(BF16)


def down_kernel(place, hidden, attended, down, out, branch):
    for m in range(hidden.shape[0] // ROWS):
        here = slice(m * ROWS, (m + 1) * ROWS)
        branch[here] = (
            mul(hidden[here], down[...]) + mul(attended[here], out[...])
        ).astype(BF16)


def spans(pieces, rows):
    ins = []
    for parts in pieces:
        before = 0
        for part in parts:
            steps = part.shape[0] // rows

            def block_map(i, p, before=before, steps=steps):
                return (jnp.clip(i - before, 0, steps - 1), 0)

            ins.append((part, (rows, part.shape[1]), block_map))
            before += steps
    return ins


def pick(parts, steps):
    value, before = parts[0][...], 0
    for number in range(1, len(parts)):
        before += steps[number - 1]
        value = jnp.where(pl.program_id(0) < before, value, parts[number][...])
    return value


def middle_kernel(block_steps, cot_steps, width_all, place, *refs):
    block, refs = group_parts(refs, [len(steps) for steps in block_steps])
    cot, refs = group_parts(refs, [len(steps) for steps in cot_steps])
    count = len(block)
    block = [pick(parts, steps) for parts, steps in zip(block, block_steps)]
    cot = [pick(parts, steps) for parts, steps in zip(cot, cot_steps)]
    weights = refs[:count]
    next_weight, seed, factor = refs[count : 3 + count]
    branch_grad, block_grad, next_mix, next_part, mix_part = refs[3 + count :]
    width = block[0].shape[1]

    @pl.when(pl.program_id(0) == 0)
    def _():
        next_part[...] = jnp.zeros_like(next_part)
        mix_part[...] = jnp.zeros_like(mix_part)

    raw = mul(block[0], weights[0][...])
    for r in range(1, count):
        raw += mul(block[r], weights[r][...])
    square = 0.0
    for r in range(count):
        wide = block[r].astype(F32)
        square += jnp.sum(wide * wide, axis=1, keepdims=True)
    root_inv = lax.rsqrt(square / width_all + rms_eps)
    pre_mix = raw * root_inv
    cumulative, density = normal_parts(pre_mix)
    mix_hidden = (pre_mix * cumulative).astype(BF16)
    next_mix[...] = mul(next_weight[...], mix_hidden, (((0,), (1,)), ((), ())))
    next_part[...] += mul(mix_hidden, seed[...], TN)
    hidden_grad = mul(seed[...], next_weight[...], NT)
    pre_grad = (hidden_grad * (cumulative + pre_mix * density)).astype(BF16)
    inner = jnp.sum(pre_grad.astype(F32) * raw, axis=1, keepdims=True) / width_all
    coef = root_inv * root_inv * root_inv * inner
    for r in range(count):
        offset = pl.multiple_of((place[0] ^ r) * width, LANES)
        wide = block[r].astype(F32)
        scaled = (wide * root_inv).astype(BF16)
        mix_part[:, pl.ds(offset, width)] += mul(pre_grad, scaled, TN)
        scaled_grad = mul(pre_grad, weights[r][...], NT)
        total = (
            root_inv * scaled_grad - wide * coef + cot[r].astype(F32) * factor[...]
        )
        branch_grad[:, pl.ds(offset, width)] = total.astype(BF16)
        if r == 0:
            block_grad[...] = total


def down_grad_kernel(hidden_steps, place, hidden, attended, branch_grad, out):
    def work(left):
        turned = left.T
        for m in range(out.shape[1] // 512):
            here = slice(m * 512, (m + 1) * 512)
            out[:, here] = mul(turned, branch_grad[:, here]).astype(BF16)

    j = pl.program_id(0)

    @pl.when(j < hidden_steps)
    def _():
        work(hidden[...])

    @pl.when(j == hidden_steps)
    def _():
        work(attended[...])


def hidden_grad_kernel(place, branch_grad, weight, slope, hidden_grad):
    for m in range(branch_grad.shape[0] // ROWS):
        here = slice(m * ROWS, (m + 1) * ROWS)
        total = mul(branch_grad[here], weight[...], NT)
        hidden_grad[here] = (total * slope[here].astype(F32)).astype(BF16)


def back_kernel(place, grad, weight, out):
    for m in range(grad.shape[0] // ROWS):
        here = slice(m * ROWS, (m + 1) * ROWS)
        out[here] = mul(grad[here], weight[...], NT).astype(BF16)


def weight_grad_kernel(shape, hidden_steps, place, *refs):
    last, refs = group_parts(refs, shape)
    first, refs = group_parts(refs, shape)
    hidden_grad, lin_grad, out, turned = refs
    j, r = pl.program_id(0), pl.program_id(1)
    for k in range(len(shape)):

        @pl.when((j == 0) & (r == k))
        def _():
            turned[k] = joined(last[k]).T

        @pl.when((j >= hidden_steps) & (r == k))
        def _():
            out[...] = mul(joined(first[k]), lin_grad[...], TN).astype(BF16)

    @pl.when(j < hidden_steps)
    def _():
        out[...] = mul(turned[r], hidden_grad[...]).astype(BF16)


def sums_kernel(
    width_all, place, first, last, streams, stats, gain, hist, block_grad, out, norm_part
):
    @pl.when(pl.program_id(0) == 0)
    def _():
        norm_part[...] = jnp.zeros_like(norm_part)

    centers, spreads = center_and_spread(stats[...], width_all)
    terms, plain, other = [], [], []
    for c in range(STREAMS):
        unit = (streams[c] - centers[c]) * spreads[c]
        grad = first[c] if c < STREAMS - 1 else last[...]
        times = grad * unit
        norm_part[c : c + 1] += jnp.sum(times, axis=0, keepdims=True)
        norm_part[STREAMS + c : STREAMS + c + 1] += jnp.sum(grad, axis=0, keepdims=True)
        scaled = grad * gain[c : c + 1]
        plain.append(jnp.sum(scaled, axis=1, keepdims=True))
        other.append(jnp.sum(scaled * unit, axis=1, keepdims=True))
        term = scaled * spreads[c]
        terms.append(term + block_grad[...] if c == STREAMS - 1 else term)
    columns = [None] * (STREAMS * ENTRIES)
    for e in range(ENTRIES):
        entry = hist[e].astype(F32)
        for c in range(STREAMS):
            columns[c * ENTRIES + e] = jnp.sum(terms[c] * entry, axis=1, keepdims=True)
    out[...] = lanes_to_rows(columns + plain + other, out.shape[0])


def history_kernel(
    width_all, place, first, last, streams, stats, gain, sums, coef, block_grad, out
):
    centers, spreads = center_and_spread(stats[...], width_all)
    turned = rows_to_lanes(sums[...])
    grads = []
    for c in range(STREAMS):
        unit = (streams[c] - centers[c]) * spreads[c]
        grad = first[c] if c < STREAMS - 1 else last[...]
        plain = turned[:, c : c + 1] / width_all
        other = turned[:, STREAMS + c : STREAMS + c + 1] / width_all
        value = spreads[c] * (grad * gain[c : c + 1] - plain - unit * other)
        grads.append(value + block_grad[...] if c == STREAMS - 1 else value)
    for e in range(ENTRIES):
        total = coef[:, e : e + 1] * grads[0]
        for c in range(1, STREAMS):
            k = c * ENTRIES + e
            total += coef[:, k : k + 1] * grads[c]
        out[e] = total


def swap(values, axis, bit):
    count = lax.axis_size(axis)
    return lax.ppermute(values, axis, [(i, i ^ bit) for i in range(count)])


def after(value, *earlier):
    return lax.optimization_barrier((value, earlier))[0]


def axis_bits(axis):
    count = lax.axis_size(axis)
    return [1 << b for b in range(count.bit_length() - 1)]


def butterfly_sum(values, axis):
    for bit in axis_bits(axis):
        values = values + swap(values, axis, bit)
    return values


def gather_start(own):
    bits = axis_bits("tensor")
    if len(bits) == 2:
        return own, [swap(own, "tensor", bit) for bit in bits]
    return own, []


def gather_finish(state):
    own, arrived = state
    bits = axis_bits("tensor")
    half = own.shape[-2] // 2
    if len(bits) == 2:
        one, two = arrived
        top = swap(one[..., :half, :], "tensor", 2)
        bottom = swap(two[..., half:, :], "tensor", 1)
        return [[own], [one], [two], [top, bottom]]
    halves = []
    for part, order in ((own[..., :half, :], bits), (own[..., half:, :], bits[::-1])):
        held = {0: part}
        for bit in order:
            keys = list(held)
            got = swap(jnp.stack([held[k] for k in keys]), "tensor", bit)
            for number, k in enumerate(keys):
                held[k ^ bit] = got[number]
        halves.append(held)
    return [[halves[0][k], halves[1][k]] for k in sorted(halves[0])]


def gather_pieces(own):
    return gather_finish(gather_start(own))


def scatter_start(pieces):
    half = pieces.shape[-2] // 2
    bits = axis_bits("tensor")
    states = []
    for number, order in enumerate((bits, bits[::-1])):
        rows = pieces[..., number * half : (number + 1) * half, :]
        held = {k: rows[k] for k in range(pieces.shape[0])}
        states.append((order, held, *scatter_send(held, order[0])))
    return states


def scatter_send(held, bit):
    sent = [k for k in held if k & bit]
    return sent, swap(jnp.stack([held[k] for k in sent]).astype(BF16), "tensor", bit)


def scatter_arrived(states):
    return [state[3] for state in states]


def scatter_finish(states):
    sums = []
    for order, held, sent, got in states:
        for number, bit in enumerate(order):
            if number:
                sent, got = scatter_send(held, bit)
            for spot, k in enumerate(sent):
                held[k ^ bit] = held[k ^ bit].astype(F32) + got[spot].astype(F32)
                del held[k]
        sums.append(held[0])
    return jnp.concatenate(sums, -2)


def scatter_pieces(pieces):
    return scatter_finish(scatter_start(pieces))


def per_device(
    history,
    mix_in,
    group_ids,
    group_weight,
    block_cotangent,
    mix_cotangent,
    qkv_weight,
    out_weight,
    up_weight,
    down_weight,
    norm_gain,
    norm_bias,
    mix_weight,
    next_weight,
):
    count = lax.axis_size("tensor")
    tensor_place = lax.axis_index("tensor")
    dp_place = lax.axis_index("dp")
    tokens, width = history.shape[1:]
    width_all = width * count
    share = norm_gain.shape[1]
    mix_out = mix_weight.shape[1]
    heads_width = qkv_weight.shape[2]
    heads = heads_width // HEAD_DIM
    hidden_width = up_weight.shape[1]
    hidden_steps = hidden_width // heads_width
    place = jnp.stack([tensor_place, dp_place]).astype(jnp.int32)
    call = functools.partial(kernel_call, place=place)

    def other(r, *rest):
        return lambda *g: (g[-1][0] ^ r,) + rest

    cot_state = gather_start(block_cotangent)

    smalls = jnp.concatenate([norm_gain.T, norm_bias.T, mix_weight], 1)
    smalls = lax.all_gather(smalls, "dp", axis=0, tiled=True)
    mix_full = smalls[:, 2 * STREAMS :]
    norm_own = lax.dynamic_slice_in_dim(
        smalls[:, : 2 * STREAMS].astype(F32), tensor_place * width, width, 0
    ).T
    gain_own, bias_own = norm_own[:STREAMS], norm_own[STREAMS:]
    qkv_full = lax.all_gather(qkv_weight, "dp", axis=1, tiled=True)
    up_full = lax.all_gather(up_weight, "dp", axis=0, tiled=True)
    both_full = lax.all_gather(
        jnp.concatenate([down_weight, out_weight], 0), "dp", axis=1, tiled=True
    )

    coef = mix_in.T
    token_steps = tokens // LANES
    hist_in = (history, (ENTRIES, LANES, width), lambda i, p: (0, i, 0))
    coef_in = (coef, (LANES, coef.shape[1]), lambda i, p: (i, 0))
    wide_map = lambda i, p: (0, i, 0)
    row_map = lambda i, p: (0, i)
    streams, stats = call(
        mix_kernel,
        (token_steps,),
        ins=[hist_in, coef_in],
        outs=[
            ((STREAMS, tokens, width), F32, (STREAMS, LANES, width), wide_map),
            ((2 * STREAMS, tokens), F32, (2 * STREAMS, LANES), row_map),
        ],
        name="mix",
        flops=2 * STREAMS * history.size,
    )
    stats = butterfly_sum(after(stats, *cot_state[1]), "tensor")
    cot_pieces = gather_finish(cot_state)
    streams_in = (streams, (STREAMS, LANES, width), wide_map)
    stats_in = (stats, (2 * STREAMS, LANES), row_map)
    gain_in = (gain_own, (STREAMS, width), const(0, 0))
    normed_first, normed_last = call(
        functools.partial(norm_kernel, width_all),
        (token_steps,),
        ins=[streams_in, stats_in, gain_in, (bias_own, (STREAMS, width), const(0, 0))],
        outs=[
            ((STREAMS - 1, tokens, width), BF16, (STREAMS - 1, LANES, width), wide_map),
            ((tokens, width), BF16, (LANES, width), lambda i, p: (i, 0)),
        ],
        name="norm",
    )
    streams_in = (after(streams, normed_last), *streams_in[1:])
    (fixed_part,) = call(
        functools.partial(spread_kernel, width_all),
        (token_steps,),
        ins=[streams_in, stats_in, hist_in],
        outs=[((48, tokens), F32, (48, LANES), row_map)],
        name="spread",
    )
    fixed_sums = butterfly_sum(fixed_part, "tensor")

    first_own, first_arrived = gather_start(normed_first)
    first_arrived = [after(arrived, fixed_part) for arrived in first_arrived]
    first_pieces = gather_finish((first_own, first_arrived))
    last_pieces = gather_pieces(normed_last)
    first_pieces = after(first_pieces, cot_pieces, fixed_sums)

    places = (jnp.arange(tokens, dtype=jnp.int32) % LENGTH).astype(F32)
    freqs = jnp.power(10000.0, -jnp.arange(0, ROT, 2).astype(F32) / ROT)
    angles = places[:, None] * freqs[None, :]
    cosine, sine = jnp.cos(angles), jnp.sin(angles)
    rest = jnp.zeros((tokens, HEAD_DIM - ROT), F32)
    blank = jnp.zeros_like(sine)
    tables = [
        jnp.concatenate([cosine, cosine, rest + 1.0], 1),
        jnp.concatenate([blank, sine, rest], 1),
        jnp.concatenate([-sine, blank, rest], 1),
    ]
    table_ins = [(t, (tokens, HEAD_DIM), const(0, 0)) for t in tables]

    (qkv,) = call(
        functools.partial(qkv_kernel, [len(parts) for parts in first_pieces]),
        (3,),
        ins=[
            (part, (None, *part.shape[1:]), lambda c, p: (c, 0, 0))
            for parts in first_pieces
            for part in parts
        ]
        + [
            (qkv_full, (None, width, heads_width), lambda c, p, r=r: (c, p[0] ^ r, 0))
            for r in range(count)
        ]
        + table_ins,
        outs=[((3, tokens, heads_width), BF16, (None, tokens, heads_width), lambda c, p: (c, 0, 0))],
        name="qkv",
        flops=6 * tokens * width_all * heads_width,
    )
    head_ins = [
        (qkv, (None, tokens, HEAD_DIM), lambda h, p, c=c: (c, 0, h)) for c in range(3)
    ]
    (attended,) = call(
        attend_kernel,
        (heads,),
        ins=head_ins,
        outs=[((tokens, heads_width), BF16, (tokens, HEAD_DIM), lambda h, p: (0, h))],
        name="attend",
        flops=4 * tokens * tokens * heads_width,
    )
    step = min(512, hidden_width)
    hidden, slope = call(
        functools.partial(up_kernel, [len(parts) for parts in last_pieces]),
        (hidden_width // step,),
        ins=[(part, part.shape, const(0, 0)) for parts in last_pieces for part in parts]
        + [(up_full, (width, step), lambda j, p, r=r: (p[0] ^ r, j)) for r in range(count)],
        outs=[((tokens, hidden_width), BF16, (tokens, step), lambda j, p: (0, j))] * 2,
        name="up",
        flops=2 * tokens * width_all * hidden_width,
    )
    member = (group_ids[:, None] == jnp.arange(group_weight.shape[0])[None, :]).astype(F32)
    seq_scale = jnp.sum(member * group_weight[None, :], axis=1)
    seed = (mix_cotangent * jnp.repeat(seq_scale, LENGTH)[None, :]).T.astype(BF16)
    factor = jnp.repeat(seq_scale, LENGTH)[:, None]
    seed, factor, mix_full = lax.optimization_barrier((seed, factor, mix_full))
    hidden = after(hidden, seed, factor, mix_full)
    chunks = 1
    rows = tokens // chunks
    block_owns, block_states, held = [], [], hidden
    for number in range(chunks):
        (branch_pieces,) = call(
            down_kernel,
            (count,),
            ins=[
                (held, (rows, hidden_width), const(number, 0)),
                (attended, (rows, heads_width), const(number, 0)),
                (both_full, (hidden_width, width), lambda r, p: (0, p[0] ^ r)),
                (both_full, (heads_width, width), lambda r, p: (hidden_steps, p[0] ^ r)),
            ],
            outs=[((count, rows, width), BF16, (None, rows, width), lambda r, p: (r, 0, 0))],
            name="down",
            flops=2 * rows * width_all * (hidden_width + heads_width),
        )
        held = after(held, branch_pieces)
        block_states.append(scatter_start(branch_pieces))
    for number in range(chunks):
        residual = streams[STREAMS - 1, number * rows : (number + 1) * rows]
        if number:
            residual = after(residual, *block_states[number - 1][1])
        total = residual + scatter_finish(block_states[number])
        block_owns.append(lax.optimization_barrier(total.astype(BF16)))
        block_states[number] = gather_start(block_owns[number])
    block_chunks = [gather_finish(state) for state in block_states]
    block_own = jnp.concatenate(block_owns, 0)
    block_pieces = [[part for chunk in block_chunks for part in chunk[r]] for r in range(count)]

    mid = min(256, tokens)
    branch_grad, block_grad, next_mix, next_part, mix_part = call(
        functools.partial(
            middle_kernel,
            [[part.shape[0] // mid for part in parts] for parts in block_pieces],
            [[part.shape[0] // mid for part in parts] for parts in cot_pieces],
            width_all,
        ),
        (tokens // mid,),
        ins=spans(block_pieces, mid)
        + spans(cot_pieces, mid)
        + [(mix_full, (width, mix_out), other(r, 0)) for r in range(count)]
        + [
            (next_weight, next_weight.shape, const(0, 0)),
            (seed, (mid, mix_out), lambda i, p: (i, 0)),
            (factor, (mid, 1), lambda i, p: (i, 0)),
        ],
        outs=[
            ((tokens, width_all), BF16, (mid, width_all), lambda i, p: (i, 0)),
            ((tokens, width), F32, (mid, width), lambda i, p: (i, 0)),
            ((mix_out, tokens), F32, (mix_out, mid), row_map),
            ((mix_out, mix_out), F32, (mix_out, mix_out), const(0, 0)),
            ((mix_out, width_all), F32, (mix_out, width_all), const(0, 0)),
        ],
        name="middle",
        flops=6 * tokens * width_all * mix_out,
    )

    last_step = hidden_steps - 1
    mix_rows = -(-mix_out // 16) * 16
    branch_in = (branch_grad, (tokens, width_all), const(0, 0))
    (both_part,) = call(
        functools.partial(down_grad_kernel, hidden_steps),
        (hidden_steps + 1,),
        ins=[
            (hidden, (tokens, heads_width), lambda j, p: (0, jnp.minimum(j, last_step))),
            (attended, (tokens, heads_width), const(0, 0)),
            branch_in,
        ],
        outs=[
            (
                (hidden_width + heads_width + mix_rows, width_all),
                BF16,
                (heads_width, width_all),
                lambda j, p: (j, 0),
            )
        ],
        name="down_grad",
        flops=2 * tokens * width_all * (hidden_width + heads_width),
    )
    both_part = lax.dynamic_update_slice_in_dim(
        both_part,
        jnp.pad(mix_part, ((0, mix_rows - mix_out), (0, 0))).astype(BF16),
        hidden_width + heads_width,
        0,
    )
    branch_grad = after(branch_grad, both_part)
    branch_in = (branch_grad, (tokens, width_all), const(0, 0))
    (attended_grad,) = call(
        back_kernel,
        (1,),
        ins=[
            branch_in,
            (both_full, (heads_width, width_all), const(hidden_steps, 0)),
        ],
        outs=[((tokens, heads_width), BF16, (tokens, heads_width), const(0, 0))],
        name="attended_grad",
        flops=2 * tokens * width_all * heads_width,
    )
    next_bits = axis_bits("dp")
    next_sum = next_part + swap(next_part, "dp", next_bits[0])
    lin_grads = pl.pallas_call(
        attend_back_kernel,
        out_shape=jax.ShapeDtypeStruct((3, tokens, heads_width), BF16),
        grid_spec=pltpu.PrefetchScalarGridSpec(
            num_scalar_prefetch=1,
            grid=(heads,),
            in_specs=[pl.BlockSpec(b, m) for _, b, m in head_ins]
            + [pl.BlockSpec((tokens, HEAD_DIM), lambda h, p: (0, h))]
            + [pl.BlockSpec(b, m) for _, b, m in table_ins],
            out_specs=pl.BlockSpec((3, tokens, HEAD_DIM), lambda h, p: (0, 0, h)),
            scratch_shapes=[pltpu.VMEM((tokens, HEAD_DIM), F32)] * 2,
        ),
        compiler_params=pltpu.CompilerParams(vmem_limit_bytes=VMEM_BYTES),
        cost_estimate=pl.CostEstimate(
            flops=10 * tokens * tokens * heads_width,
            bytes_accessed=8 * tokens * heads_width * 2,
            transcendentals=heads * tokens * tokens,
        ),
        name="attend_back",
    )(place, qkv, qkv, qkv, attended_grad, *tables)
    def qkv_back(grads, begin, end):
        return call(
            back_kernel,
            (end - begin, count),
            ins=[
                (grads, (None, tokens, heads_width), lambda c, r, p: (c + begin, 0, 0)),
                (qkv_full, (None, width, heads_width), lambda c, r, p: (c + begin, p[0] ^ r, 0)),
            ],
            outs=[
                (
                    (count, end - begin, tokens, width),
                    BF16,
                    (None, None, tokens, width),
                    lambda c, r, p: (r, c, 0, 0),
                )
            ],
            name="qkv_back",
            flops=2 * (end - begin) * tokens * width_all * heads_width,
        )[0]

    grads_a = qkv_back(lin_grads, 0, 1)
    states_a = scatter_start(grads_a)
    lin_grads = after(lin_grads, grads_a)
    grads_b = qkv_back(lin_grads, 1, 3)
    states_b = scatter_start(grads_b)
    branch_grad = after(branch_grad, grads_b, next_sum)
    branch_in = (branch_grad, (tokens, width_all), const(0, 0))
    (hidden_grad,) = call(
        hidden_grad_kernel,
        (hidden_steps,),
        ins=[
            branch_in,
            (both_full, (heads_width, width_all), lambda j, p: (j, 0)),
            (slope, (tokens, heads_width), lambda j, p: (0, j)),
        ],
        outs=[((tokens, hidden_width), BF16, (tokens, heads_width), lambda j, p: (0, j))],
        name="hidden_grad",
        flops=2 * tokens * width_all * hidden_width,
    )
    hidden_grad = after(hidden_grad, *scatter_arrived(states_a))
    grad_a = scatter_finish(states_a)
    (last_grads,) = call(
        back_kernel,
        (count,),
        ins=[
            (hidden_grad, (tokens, hidden_width), const(0, 0)),
            (up_full, (width, hidden_width), lambda r, p: (p[0] ^ r, 0)),
        ],
        outs=[((count, tokens, width), BF16, (None, tokens, width), lambda r, p: (r, 0, 0))],
        name="up_back",
        flops=2 * tokens * width_all * hidden_width,
    )
    last_states = scatter_start(last_grads)
    hidden_grad = after(hidden_grad, last_grads)
    for bit in next_bits[1:]:
        next_sum = next_sum + swap(next_sum, "dp", bit)
    all_steps = hidden_steps + 3
    lin_step = lambda j: jnp.maximum(j - hidden_steps, 0)
    (wide_part,) = call(
        functools.partial(
            weight_grad_kernel, [len(parts) for parts in last_pieces], hidden_steps
        ),
        (all_steps, count),
        ins=[(part, part.shape, const(0, 0)) for parts in last_pieces for part in parts]
        + [
            (part, (None, *part.shape[1:]), lambda j, r, p: (lin_step(j), 0, 0))
            for parts in first_pieces
            for part in parts
        ]
        + [
            (
                hidden_grad,
                (tokens, heads_width),
                lambda j, r, p: (0, jnp.minimum(j, hidden_steps - 1)),
            ),
            (lin_grads, (None, tokens, heads_width), lambda j, r, p: (lin_step(j), 0, 0)),
        ],
        outs=[
            (
                (width_all, all_steps * heads_width),
                BF16,
                (width, heads_width),
                lambda j, r, p: (p[0] ^ r, j),
            )
        ],
        name="weight_grad",
        flops=2 * tokens * width_all * (hidden_width + 3 * heads_width),
        scratch=[((count, width, tokens), BF16)],
    )
    wide_part = after(
        wide_part, grad_a, *scatter_arrived(states_b), *scatter_arrived(last_states)
    )
    grad_b = scatter_finish(states_b)
    last_grad = scatter_finish(last_states)
    first_grad = jnp.concatenate([grad_a, grad_b], 0)
    both_grad = lax.psum_scatter(both_part, "dp", scatter_dimension=1, tiled=True).astype(F32)
    out_end = hidden_width + heads_width
    down_grad, out_grad = both_grad[:hidden_width], both_grad[hidden_width:out_end]
    mix_proj_grad = both_grad[out_end : out_end + mix_out].T
    wide_grad = lax.psum_scatter(wide_part, "dp", scatter_dimension=0, tiled=True).astype(F32)
    up_grad = wide_grad[:, :hidden_width]
    qkv_grad = jnp.stack(
        [
            wide_grad[:, hidden_width + c * heads_width : hidden_width + (c + 1) * heads_width]
            for c in range(3)
        ]
    )

    grad_ins = [
        (first_grad, (STREAMS - 1, LANES, width), wide_map),
        (last_grad, (LANES, width), lambda i, p: (i, 0)),
        streams_in,
        stats_in,
        gain_in,
    ]
    block_grad_in = (block_grad, (LANES, width), lambda i, p: (i, 0))
    sums, norm_part = call(
        functools.partial(sums_kernel, width_all),
        (token_steps,),
        ins=grad_ins + [hist_in, block_grad_in],
        outs=[
            ((48, tokens), F32, (48, LANES), row_map),
            ((2 * STREAMS, width), F32, (2 * STREAMS, width), const(0, 0)),
        ],
        name="sums",
    )
    sums = butterfly_sum(sums, "tensor")
    pairs = STREAMS * ENTRIES
    feature_sums = sums[pairs : pairs + 2 * STREAMS]
    (history_grad,) = call(
        functools.partial(history_kernel, width_all),
        (token_steps,),
        ins=grad_ins
        + [(feature_sums, (2 * STREAMS, LANES), row_map), coef_in, block_grad_in],
        outs=[((ENTRIES, tokens, width), F32, (ENTRIES, LANES, width), wide_map)],
        name="history",
    )
    center = stats[:STREAMS] / width_all
    spread = lax.rsqrt(stats[STREAMS:] / width_all - center * center + ln_eps)
    mix_grad = (
        sums[:pairs].reshape(STREAMS, ENTRIES, tokens)
        - (spread * feature_sums[:STREAMS] / width_all)[:, None]
        * fixed_sums[None, pairs : pairs + ENTRIES]
        - (spread * feature_sums[STREAMS:] / width_all)[:, None]
        * fixed_sums[:pairs].reshape(STREAMS, ENTRIES, tokens)
    ).reshape(pairs, tokens)

    norm_part = butterfly_sum(after(norm_part, sums), "dp")
    norm_whole = lax.dynamic_update_slice_in_dim(
        jnp.zeros((2 * STREAMS, width_all), F32), norm_part, tensor_place * width, 1
    )
    norm_whole = butterfly_sum(norm_whole, "tensor")
    norm_whole = lax.dynamic_slice_in_dim(norm_whole, dp_place * share, share, 1)
    next_proj_grad = next_sum
    return (
        block_own,
        next_mix,
        history_grad,
        mix_grad,
        qkv_grad,
        out_grad,
        up_grad,
        down_grad,
        norm_whole[:STREAMS],
        norm_whole[STREAMS:],
        mix_proj_grad,
        next_proj_grad,
    )


def solution(mesh):
    placed = (
        P(None, "dp", "tensor"),
        P(None, "dp"),
        P("dp"),
        P(),
        P("dp", "tensor"),
        P(None, "dp"),
        P(None, "dp", "tensor"),
        P("tensor", "dp"),
        P("dp", "tensor"),
        P("tensor", "dp"),
        P(None, "dp"),
        P(None, "dp"),
        P("dp", None),
        P(),
    )
    return jax.shard_map(
        per_device,
        mesh=mesh,
        in_specs=placed,
        out_specs=(
            P("dp", "tensor"),
            P(None, "dp"),
            P(None, "dp", "tensor"),
            P(None, "dp"),
            P(None, "dp", "tensor"),
            P("tensor", "dp"),
            P("dp", "tensor"),
            P("tensor", "dp"),
            P(None, "dp"),
            P(None, "dp"),
            P("dp", None),
            P(),
        ),
        check_vma=False,
    )
```

```python
import functools

import jax
import jax.numpy as jnp
import numpy as np
from jax import lax
from jax.experimental import pallas as pl
from jax.experimental.pallas import tpu as pltpu
from jax.sharding import PartitionSpec as P

HEAD_DIM = 128
ROT = 32
STREAMS = 4
ENTRIES = 9
LENGTH = 1024
LANES = 128

ln_eps = 1e-05
rms_eps = 1e-06
big_negative = -1e30
root_half = 0.7071067811865476
inv_root_tau = 0.3989422804014327
F32 = jnp.float32
BF16 = jnp.bfloat16
VMEM_BYTES = 56 * 1024 * 1024

NN = (((1,), (0,)), ((), ()))
NT = (((1,), (1,)), ((), ()))
TN = (((0,), (0,)), ((), ()))


def mul(left, right, dims=NN):
    return lax.dot_general(left, right, dims, preferred_element_type=F32)


def kernel_call(body, grid, place, ins, outs, name, flops=0, scratch=()):
    moved = sum(a.size * a.dtype.itemsize for a, _, _ in ins)
    moved += sum(int(np.prod(s)) * jnp.dtype(d).itemsize for s, d, _, _ in outs)
    call = pl.pallas_call(
        body,
        out_shape=[jax.ShapeDtypeStruct(s, d) for s, d, _, _ in outs],
        grid_spec=pltpu.PrefetchScalarGridSpec(
            num_scalar_prefetch=1,
            grid=grid,
            in_specs=[pl.BlockSpec(b, m) for _, b, m in ins],
            out_specs=[pl.BlockSpec(b, m) for _, _, b, m in outs],
            scratch_shapes=[pltpu.VMEM(shape, dtype) for shape, dtype in scratch],
        ),
        compiler_params=pltpu.CompilerParams(
            vmem_limit_bytes=VMEM_BYTES,
            dimension_semantics=("arbitrary",) * len(grid),
        ),
        cost_estimate=pl.CostEstimate(
            flops=int(flops), bytes_accessed=int(moved), transcendentals=0
        ),
        name=name,
    )
    return call(place, *[a for a, _, _ in ins])


def const(*zeros):
    return lambda *_: zeros


def group_parts(refs, shape):
    groups, spot = [], 0
    for parts in shape:
        groups.append(refs[spot : spot + parts])
        spot += parts
    return groups, refs[spot:]


def joined(parts):
    if len(parts) == 1:
        return parts[0][...]
    return jnp.concatenate([part[...] for part in parts], 0)


def normal_parts(x):
    size = jnp.abs(x) * root_half
    lower = 1.0 + 0.3275911 * size
    t = 1.0 / lower
    poly = t * (
        0.254829592
        + t * (-0.284496736 + t * (1.421413741 + t * (-1.453152027 + t * 1.061405429)))
    )
    bell = jnp.exp(-0.5 * x * x)
    tail = 0.5 * poly * bell
    cumulative = jnp.where(x < 0, tail, 1.0 - tail)
    return cumulative, bell * inv_root_tau


def lanes_to_rows(columns, rows):
    lane = lax.broadcasted_iota(jnp.int32, (columns[0].shape[0], LANES), 1)
    wide = jnp.zeros((columns[0].shape[0], LANES), F32)
    for number, column in enumerate(columns):
        wide = jnp.where(lane == number, column, wide)
    return wide.T[:rows]


def mix_kernel(place, hist, coef, streams, stats):
    totals = [None] * STREAMS
    for e in range(ENTRIES):
        entry = hist[e].astype(F32)
        for c in range(STREAMS):
            k = c * ENTRIES + e
            term = coef[:, k : k + 1] * entry
            totals[c] = term if totals[c] is None else totals[c] + term
    columns = []
    for c in range(STREAMS):
        streams[c] = totals[c]
        columns.append(jnp.sum(totals[c], axis=1, keepdims=True))
    for c in range(STREAMS):
        columns.append(jnp.sum(totals[c] * totals[c], axis=1, keepdims=True))
    stats[...] = lanes_to_rows(columns, 2 * STREAMS)


def rows_to_lanes(rows):
    tall = jnp.concatenate([rows, jnp.zeros((LANES - rows.shape[0], LANES), F32)], 0)
    return tall.T


def center_and_spread(stats, width_all):
    turned = rows_to_lanes(stats)
    centers, spreads = [], []
    for c in range(STREAMS):
        center = turned[:, c : c + 1] / width_all
        square = turned[:, STREAMS + c : STREAMS + c + 1] / width_all
        centers.append(center)
        spreads.append(lax.rsqrt(square - center * center + ln_eps))
    return centers, spreads


def norm_kernel(width_all, place, streams, stats, gain, bias, first, last):
    centers, spreads = center_and_spread(stats[...], width_all)
    for c in range(STREAMS):
        unit = (streams[c] - centers[c]) * spreads[c]
        normed = (unit * gain[c : c + 1] + bias[c : c + 1]).astype(BF16)
        if c < STREAMS - 1:
            first[c] = normed
        else:
            last[...] = normed


def spread_kernel(width_all, place, streams, stats, hist, out):
    centers, spreads = center_and_spread(stats[...], width_all)
    units = [(streams[c] - centers[c]) * spreads[c] for c in range(STREAMS)]
    columns = []
    entries = [hist[e].astype(F32) for e in range(ENTRIES)]
    for c in range(STREAMS):
        for e in range(ENTRIES):
            columns.append(jnp.sum(units[c] * entries[e], axis=1, keepdims=True))
    for e in range(ENTRIES):
        columns.append(jnp.sum(entries[e], axis=1, keepdims=True))
    out[...] = lanes_to_rows(columns, out.shape[0])


def turn(x, cosine, ahead, behind):
    half = ROT // 2
    return x * cosine + pltpu.roll(x, half, 1) * ahead + pltpu.roll(x, LANES - half, 1) * behind


def qkv_kernel(shape, place, *refs):
    pieces, refs = group_parts(refs, shape)
    count = len(shape)
    weights, (cosine, ahead, behind, out) = refs[:count], refs[count:]
    total = mul(joined(pieces[0]), weights[0][...])
    for r in range(1, count):
        total += mul(joined(pieces[r]), weights[r][...])
    c = pl.program_id(0)

    @pl.when(c < 2)
    def _():
        for h in range(total.shape[1] // HEAD_DIM):
            spot = slice(h * HEAD_DIM, (h + 1) * HEAD_DIM)
            turned = turn(total[:, spot], cosine[...], ahead[...], behind[...])
            out[:, spot] = turned.astype(BF16)

    @pl.when(c == 2)
    def _():
        out[...] = total.astype(BF16)


ROWS = 256


def attend_kernel(place, q, k, v, out):
    scale = HEAD_DIM**-0.5
    for number in range(q.shape[0] // ROWS):
        start, stop = number * ROWS, (number + 1) * ROWS
        scores = mul(q[start:stop], k[:stop], NT) * scale
        row = lax.broadcasted_iota(jnp.int32, scores.shape, 0) + start
        col = lax.broadcasted_iota(jnp.int32, scores.shape, 1)
        scores = jnp.where(col <= row, scores, big_negative)
        summit = jnp.max(scores, axis=1, keepdims=True)
        exponent = jnp.exp(scores - summit)
        part = jnp.sum(exponent, axis=1, keepdims=True)
        probs = (exponent * (1.0 / part)).astype(BF16)
        out[start:stop] = mul(probs, v[:stop]).astype(BF16)


def attend_back_kernel(place, q, k, v, grad, cosine, ahead, behind, out, dk, dv):
    scale = HEAD_DIM**-0.5
    dk[...] = jnp.zeros_like(dk)
    dv[...] = jnp.zeros_like(dv)
    for number in range(q.shape[0] // ROWS):
        start, stop = number * ROWS, (number + 1) * ROWS
        here = slice(start, stop)
        scores = mul(k[:stop], q[here], NT) * scale
        row = lax.broadcasted_iota(jnp.int32, scores.shape, 0)
        col = lax.broadcasted_iota(jnp.int32, scores.shape, 1) + start
        scores = jnp.where(row <= col, scores, big_negative)
        summit = jnp.max(scores, axis=0, keepdims=True)
        exponent = jnp.exp(scores - summit)
        part = jnp.sum(exponent, axis=0, keepdims=True)
        probs = exponent * (1.0 / part)
        prob_grad = mul(v[:stop], grad[here], NT)
        dv[:stop] += mul(probs.astype(BF16), grad[here])
        center = jnp.sum(probs * prob_grad, axis=0, keepdims=True)
        score_grad = (probs * (prob_grad - center)).astype(BF16)
        dk[:stop] += mul(score_grad, q[here])
        query_grad = mul(score_grad, k[:stop], TN) * scale
        out[0, here] = turn(
            query_grad, cosine[here], -ahead[here], -behind[here]
        ).astype(BF16)
    out[1] = turn(dk[...] * scale, cosine[...], -ahead[...], -behind[...]).astype(BF16)
    out[2] = dv[...].astype(BF16)


def part_rows(parts, start, rows):
    for part in parts:
        if start < part.shape[0]:
            return part[start : start + rows]
        start -= part.shape[0]


def up_kernel(shape, place, *refs):
    pieces, refs = group_parts(refs, shape)
    count = len(shape)
    weights, (hidden, slope) = refs[:count], refs[count:]
    for m in range(hidden.shape[0] // ROWS):
        here = slice(m * ROWS, (m + 1) * ROWS)
        total = mul(part_rows(pieces[0], m * ROWS, ROWS), weights[0][...])
        for r in range(1, count):
            total += mul(part_rows(pieces[r], m * ROWS, ROWS), weights[r][...])
        cumulative, density = normal_parts(total)
        hidden[here] = (total * cumulative).astype(BF16)
        slope[here] = (cumulative + total * density).astype(BF16)


def down_kernel(place, hidden, attended, down, out, branch):
    for m in range(hidden.shape[0] // ROWS):
        here = slice(m * ROWS, (m + 1) * ROWS)
        branch[here] = (
            mul(hidden[here], down[...]) + mul(attended[here], out[...])
        ).astype(BF16)


def spans(pieces, rows):
    ins = []
    for parts in pieces:
        before = 0
        for part in parts:
            steps = part.shape[0] // rows

            def block_map(i, p, before=before, steps=steps):
                return (jnp.clip(i - before, 0, steps - 1), 0)

            ins.append((part, (rows, part.shape[1]), block_map))
            before += steps
    return ins


def pick(parts, steps):
    value, before = parts[0][...], 0
    for number in range(1, len(parts)):
        before += steps[number - 1]
        value = jnp.where(pl.program_id(0) < before, value, parts[number][...])
    return value


def middle_kernel(block_steps, cot_steps, width_all, place, *refs):
    block, refs = group_parts(refs, [len(steps) for steps in block_steps])
    cot, refs = group_parts(refs, [len(steps) for steps in cot_steps])
    count = len(block)
    block = [pick(parts, steps) for parts, steps in zip(block, block_steps)]
    cot = [pick(parts, steps) for parts, steps in zip(cot, cot_steps)]
    weights = refs[:count]
    next_weight, seed, factor = refs[count : 3 + count]
    branch_grad, block_grad, next_mix, next_part, mix_part = refs[3 + count :]
    width = block[0].shape[1]

    @pl.when(pl.program_id(0) == 0)
    def _():
        next_part[...] = jnp.zeros_like(next_part)
        mix_part[...] = jnp.zeros_like(mix_part)

    raw = mul(block[0], weights[0][...])
    for r in range(1, count):
        raw += mul(block[r], weights[r][...])
    square = 0.0
    for r in range(count):
        wide = block[r].astype(F32)
        square += jnp.sum(wide * wide, axis=1, keepdims=True)
    root_inv = lax.rsqrt(square / width_all + rms_eps)
    pre_mix = raw * root_inv
    cumulative, density = normal_parts(pre_mix)
    mix_hidden = (pre_mix * cumulative).astype(BF16)
    next_mix[...] = mul(next_weight[...], mix_hidden, (((0,), (1,)), ((), ())))
    next_part[...] += mul(mix_hidden, seed[...], TN)
    hidden_grad = mul(seed[...], next_weight[...], NT)
    pre_grad = (hidden_grad * (cumulative + pre_mix * density)).astype(BF16)
    inner = jnp.sum(pre_grad.astype(F32) * raw, axis=1, keepdims=True) / width_all
    coef = root_inv * root_inv * root_inv * inner
    for r in range(count):
        offset = pl.multiple_of((place[0] ^ r) * width, LANES)
        wide = block[r].astype(F32)
        scaled = (wide * root_inv).astype(BF16)
        mix_part[:, pl.ds(offset, width)] += mul(pre_grad, scaled, TN)
        scaled_grad = mul(pre_grad, weights[r][...], NT)
        total = (
            root_inv * scaled_grad - wide * coef + cot[r].astype(F32) * factor[...]
        )
        branch_grad[:, pl.ds(offset, width)] = total.astype(BF16)
        if r == 0:
            block_grad[...] = total


def down_grad_kernel(hidden_steps, place, hidden, attended, branch_grad, out):
    def work(left):
        turned = left.T
        for m in range(out.shape[1] // 512):
            here = slice(m * 512, (m + 1) * 512)
            out[:, here] = mul(turned, branch_grad[:, here]).astype(BF16)

    j = pl.program_id(0)

    @pl.when(j < hidden_steps)
    def _():
        work(hidden[...])

    @pl.when(j == hidden_steps)
    def _():
        work(attended[...])


def hidden_grad_kernel(place, branch_grad, weight, slope, hidden_grad):
    for m in range(branch_grad.shape[0] // ROWS):
        here = slice(m * ROWS, (m + 1) * ROWS)
        total = mul(branch_grad[here], weight[...], NT)
        hidden_grad[here] = (total * slope[here].astype(F32)).astype(BF16)


def back_kernel(place, grad, weight, out):
    for m in range(grad.shape[0] // ROWS):
        here = slice(m * ROWS, (m + 1) * ROWS)
        out[here] = mul(grad[here], weight[...], NT).astype(BF16)


def weight_grad_kernel(shape, hidden_steps, place, *refs):
    last, refs = group_parts(refs, shape)
    first, refs = group_parts(refs, shape)
    hidden_grad, lin_grad, out, turned = refs
    j, r = pl.program_id(0), pl.program_id(1)
    for k in range(len(shape)):

        @pl.when((j == 0) & (r == k))
        def _():
            turned[k] = joined(last[k]).T

        @pl.when((j >= hidden_steps) & (r == k))
        def _():
            out[...] = mul(joined(first[k]), lin_grad[...], TN).astype(BF16)

    @pl.when(j < hidden_steps)
    def _():
        out[...] = mul(turned[r], hidden_grad[...]).astype(BF16)


def sums_kernel(
    width_all, place, first, last, streams, stats, gain, hist, block_grad, out, norm_part
):
    @pl.when(pl.program_id(0) == 0)
    def _():
        norm_part[...] = jnp.zeros_like(norm_part)

    centers, spreads = center_and_spread(stats[...], width_all)
    terms, plain, other = [], [], []
    for c in range(STREAMS):
        unit = (streams[c] - centers[c]) * spreads[c]
        grad = first[c] if c < STREAMS - 1 else last[...]
        times = grad * unit
        norm_part[c : c + 1] += jnp.sum(times, axis=0, keepdims=True)
        norm_part[STREAMS + c : STREAMS + c + 1] += jnp.sum(grad, axis=0, keepdims=True)
        scaled = grad * gain[c : c + 1]
        plain.append(jnp.sum(scaled, axis=1, keepdims=True))
        other.append(jnp.sum(scaled * unit, axis=1, keepdims=True))
        term = scaled * spreads[c]
        terms.append(term + block_grad[...] if c == STREAMS - 1 else term)
    columns = [None] * (STREAMS * ENTRIES)
    for e in range(ENTRIES):
        entry = hist[e].astype(F32)
        for c in range(STREAMS):
            columns[c * ENTRIES + e] = jnp.sum(terms[c] * entry, axis=1, keepdims=True)
    out[...] = lanes_to_rows(columns + plain + other, out.shape[0])


def history_kernel(
    width_all, place, first, last, streams, stats, gain, sums, coef, block_grad, out
):
    centers, spreads = center_and_spread(stats[...], width_all)
    turned = rows_to_lanes(sums[...])
    grads = []
    for c in range(STREAMS):
        unit = (streams[c] - centers[c]) * spreads[c]
        grad = first[c] if c < STREAMS - 1 else last[...]
        plain = turned[:, c : c + 1] / width_all
        other = turned[:, STREAMS + c : STREAMS + c + 1] / width_all
        value = spreads[c] * (grad * gain[c : c + 1] - plain - unit * other)
        grads.append(value + block_grad[...] if c == STREAMS - 1 else value)
    for e in range(ENTRIES):
        total = coef[:, e : e + 1] * grads[0]
        for c in range(1, STREAMS):
            k = c * ENTRIES + e
            total += coef[:, k : k + 1] * grads[c]
        out[e] = total


def swap(values, axis, bit):
    count = lax.axis_size(axis)
    return lax.ppermute(values, axis, [(i, i ^ bit) for i in range(count)])


def after(value, *earlier):
    return lax.optimization_barrier((value, earlier))[0]


def axis_bits(axis):
    count = lax.axis_size(axis)
    return [1 << b for b in range(count.bit_length() - 1)]


def butterfly_sum(values, axis):
    for bit in axis_bits(axis):
        values = values + swap(values, axis, bit)
    return values


def gather_start(own):
    bits = axis_bits("tensor")
    if len(bits) == 2:
        return own, [swap(own, "tensor", bit) for bit in bits]
    return own, []


def gather_finish(state):
    own, arrived = state
    bits = axis_bits("tensor")
    half = own.shape[-2] // 2
    if len(bits) == 2:
        one, two = arrived
        top = swap(one[..., :half, :], "tensor", 2)
        bottom = swap(two[..., half:, :], "tensor", 1)
        return [[own], [one], [two], [top, bottom]]
    halves = []
    for part, order in ((own[..., :half, :], bits), (own[..., half:, :], bits[::-1])):
        held = {0: part}
        for bit in order:
            keys = list(held)
            got = swap(jnp.stack([held[k] for k in keys]), "tensor", bit)
            for number, k in enumerate(keys):
                held[k ^ bit] = got[number]
        halves.append(held)
    return [[halves[0][k], halves[1][k]] for k in sorted(halves[0])]


def gather_pieces(own):
    return gather_finish(gather_start(own))


def scatter_start(pieces):
    half = pieces.shape[-2] // 2
    bits = axis_bits("tensor")
    states = []
    for number, order in enumerate((bits, bits[::-1])):
        rows = pieces[..., number * half : (number + 1) * half, :]
        held = {k: rows[k] for k in range(pieces.shape[0])}
        states.append([held, *scatter_send(held, order[0])])
    return states


def scatter_send(held, bit):
    sent = [k for k in held if k & bit]
    return sent, swap(jnp.stack([held[k] for k in sent]).astype(BF16), "tensor", bit), bit


def scatter_add(held, sent, got, bit):
    for spot, k in enumerate(sent):
        held[k ^ bit] = held[k ^ bit].astype(F32) + got[spot].astype(F32)
        del held[k]


def scatter_arrived(states):
    return [state[2] for state in states]


def together(states):
    arrived = lax.optimization_barrier(tuple(scatter_arrived(states)))
    for state, got in zip(states, arrived):
        state[2] = got
    return states


def scatter_second(states):
    bits = axis_bits("tensor")
    later = []
    for (held, sent, got, first), order in zip(states, (bits, bits[::-1])):
        held = dict(held)
        scatter_add(held, sent, got, first)
        for bit in order[1:-1]:
            sent, got, _ = scatter_send(held, bit)
            scatter_add(held, sent, got, bit)
        later.append([held, *scatter_send(held, order[-1])])
    return later


def scatter_end(states):
    sums = []
    for held, sent, got, bit in states:
        held = dict(held)
        scatter_add(held, sent, got, bit)
        sums.append(held[0])
    return jnp.concatenate(sums, -2)


def per_device(
    history,
    mix_in,
    group_ids,
    group_weight,
    block_cotangent,
    mix_cotangent,
    qkv_weight,
    out_weight,
    up_weight,
    down_weight,
    norm_gain,
    norm_bias,
    mix_weight,
    next_weight,
):
    count = lax.axis_size("tensor")
    tensor_place = lax.axis_index("tensor")
    dp_place = lax.axis_index("dp")
    tokens, width = history.shape[1:]
    width_all = width * count
    share = norm_gain.shape[1]
    mix_out = mix_weight.shape[1]
    heads_width = qkv_weight.shape[2]
    heads = heads_width // HEAD_DIM
    hidden_width = up_weight.shape[1]
    hidden_steps = hidden_width // heads_width
    place = jnp.stack([tensor_place, dp_place]).astype(jnp.int32)
    call = functools.partial(kernel_call, place=place)

    def other(r, *rest):
        return lambda *g: (g[-1][0] ^ r,) + rest

    cot_state = gather_start(block_cotangent)

    smalls = jnp.concatenate([norm_gain.T, norm_bias.T, mix_weight], 1)
    smalls = lax.all_gather(smalls, "dp", axis=0, tiled=True)
    mix_full = smalls[:, 2 * STREAMS :]
    norm_own = lax.dynamic_slice_in_dim(
        smalls[:, : 2 * STREAMS].astype(F32), tensor_place * width, width, 0
    ).T
    gain_own, bias_own = norm_own[:STREAMS], norm_own[STREAMS:]
    qkv_full = lax.all_gather(qkv_weight, "dp", axis=1, tiled=True)
    up_full = lax.all_gather(up_weight, "dp", axis=0, tiled=True)
    both_full = lax.all_gather(
        jnp.concatenate([down_weight, out_weight], 0), "dp", axis=1, tiled=True
    )

    coef = mix_in.T
    token_steps = tokens // LANES
    hist_in = (history, (ENTRIES, LANES, width), lambda i, p: (0, i, 0))
    coef_in = (coef, (LANES, coef.shape[1]), lambda i, p: (i, 0))
    wide_map = lambda i, p: (0, i, 0)
    row_map = lambda i, p: (0, i)
    streams, stats = call(
        mix_kernel,
        (token_steps,),
        ins=[hist_in, coef_in],
        outs=[
            ((STREAMS, tokens, width), F32, (STREAMS, LANES, width), wide_map),
            ((2 * STREAMS, tokens), F32, (2 * STREAMS, LANES), row_map),
        ],
        name="mix",
        flops=2 * STREAMS * history.size,
    )
    stats = butterfly_sum(after(stats, *cot_state[1]), "tensor")
    cot_pieces = gather_finish(cot_state)
    streams_in = (streams, (STREAMS, LANES, width), wide_map)
    stats_in = (stats, (2 * STREAMS, LANES), row_map)
    gain_in = (gain_own, (STREAMS, width), const(0, 0))
    normed_first, normed_last = call(
        functools.partial(norm_kernel, width_all),
        (token_steps,),
        ins=[streams_in, stats_in, gain_in, (bias_own, (STREAMS, width), const(0, 0))],
        outs=[
            ((STREAMS - 1, tokens, width), BF16, (STREAMS - 1, LANES, width), wide_map),
            ((tokens, width), BF16, (LANES, width), lambda i, p: (i, 0)),
        ],
        name="norm",
    )
    streams_in = (after(streams, normed_last), *streams_in[1:])
    (fixed_part,) = call(
        functools.partial(spread_kernel, width_all),
        (token_steps,),
        ins=[streams_in, stats_in, hist_in],
        outs=[((48, tokens), F32, (48, LANES), row_map)],
        name="spread",
    )

    first_own, first_arrived = gather_start(normed_first)
    first_arrived = [after(arrived, fixed_part) for arrived in first_arrived]
    first_pieces = gather_finish((first_own, first_arrived))
    last_pieces = gather_pieces(normed_last)
    first_pieces = after(first_pieces, cot_pieces)

    places = (jnp.arange(tokens, dtype=jnp.int32) % LENGTH).astype(F32)
    freqs = jnp.power(10000.0, -jnp.arange(0, ROT, 2).astype(F32) / ROT)
    angles = places[:, None] * freqs[None, :]
    cosine, sine = jnp.cos(angles), jnp.sin(angles)
    rest = jnp.zeros((tokens, HEAD_DIM - ROT), F32)
    blank = jnp.zeros_like(sine)
    tables = [
        jnp.concatenate([cosine, cosine, rest + 1.0], 1),
        jnp.concatenate([blank, sine, rest], 1),
        jnp.concatenate([-sine, blank, rest], 1),
    ]
    table_ins = [(t, (tokens, HEAD_DIM), const(0, 0)) for t in tables]

    (qkv,) = call(
        functools.partial(qkv_kernel, [len(parts) for parts in first_pieces]),
        (3,),
        ins=[
            (part, (None, *part.shape[1:]), lambda c, p: (c, 0, 0))
            for parts in first_pieces
            for part in parts
        ]
        + [
            (qkv_full, (None, width, heads_width), lambda c, p, r=r: (c, p[0] ^ r, 0))
            for r in range(count)
        ]
        + table_ins,
        outs=[((3, tokens, heads_width), BF16, (None, tokens, heads_width), lambda c, p: (c, 0, 0))],
        name="qkv",
        flops=6 * tokens * width_all * heads_width,
    )
    head_ins = [
        (qkv, (None, tokens, HEAD_DIM), lambda h, p, c=c: (c, 0, h)) for c in range(3)
    ]
    (attended,) = call(
        attend_kernel,
        (heads,),
        ins=head_ins,
        outs=[((tokens, heads_width), BF16, (tokens, HEAD_DIM), lambda h, p: (0, h))],
        name="attend",
        flops=4 * tokens * tokens * heads_width,
    )
    step = min(512, hidden_width)
    hidden, slope = call(
        functools.partial(up_kernel, [len(parts) for parts in last_pieces]),
        (hidden_width // step,),
        ins=[(part, part.shape, const(0, 0)) for parts in last_pieces for part in parts]
        + [(up_full, (width, step), lambda j, p, r=r: (p[0] ^ r, j)) for r in range(count)],
        outs=[((tokens, hidden_width), BF16, (tokens, step), lambda j, p: (0, j))] * 2,
        name="up",
        flops=2 * tokens * width_all * hidden_width,
    )
    member = (group_ids[:, None] == jnp.arange(group_weight.shape[0])[None, :]).astype(F32)
    seq_scale = jnp.sum(member * group_weight[None, :], axis=1)
    seed = (mix_cotangent * jnp.repeat(seq_scale, LENGTH)[None, :]).T.astype(BF16)
    factor = jnp.repeat(seq_scale, LENGTH)[:, None]
    seed, factor, mix_full = lax.optimization_barrier((seed, factor, mix_full))
    hidden = after(hidden, seed, factor, mix_full)
    chunks = 1
    rows = tokens // chunks
    block_owns, block_states, held = [], [], hidden
    for number in range(chunks):
        (branch_pieces,) = call(
            down_kernel,
            (count,),
            ins=[
                (held, (rows, hidden_width), const(number, 0)),
                (attended, (rows, heads_width), const(number, 0)),
                (both_full, (hidden_width, width), lambda r, p: (0, p[0] ^ r)),
                (both_full, (heads_width, width), lambda r, p: (hidden_steps, p[0] ^ r)),
            ],
            outs=[((count, rows, width), BF16, (None, rows, width), lambda r, p: (r, 0, 0))],
            name="down",
            flops=2 * rows * width_all * (hidden_width + heads_width),
        )
        held = after(held, branch_pieces)
        block_states.append(scatter_start(branch_pieces))
    for number in range(chunks):
        residual = streams[STREAMS - 1, number * rows : (number + 1) * rows]
        if number:
            residual = after(residual, *block_states[number - 1][1])
        total = residual + scatter_end(together(scatter_second(together(block_states[number]))))
        block_owns.append(lax.optimization_barrier(total.astype(BF16)))
        block_states[number] = gather_start(block_owns[number])
    block_chunks = [gather_finish(state) for state in block_states]
    block_own = jnp.concatenate(block_owns, 0)
    block_pieces = [[part for chunk in block_chunks for part in chunk[r]] for r in range(count)]

    mid = min(256, tokens)
    branch_grad, block_grad, next_mix, next_part, mix_part = call(
        functools.partial(
            middle_kernel,
            [[part.shape[0] // mid for part in parts] for parts in block_pieces],
            [[part.shape[0] // mid for part in parts] for parts in cot_pieces],
            width_all,
        ),
        (tokens // mid,),
        ins=spans(block_pieces, mid)
        + spans(cot_pieces, mid)
        + [(mix_full, (width, mix_out), other(r, 0)) for r in range(count)]
        + [
            (next_weight, next_weight.shape, const(0, 0)),
            (seed, (mid, mix_out), lambda i, p: (i, 0)),
            (factor, (mid, 1), lambda i, p: (i, 0)),
        ],
        outs=[
            ((tokens, width_all), BF16, (mid, width_all), lambda i, p: (i, 0)),
            ((tokens, width), F32, (mid, width), lambda i, p: (i, 0)),
            ((mix_out, tokens), F32, (mix_out, mid), row_map),
            ((mix_out, mix_out), F32, (mix_out, mix_out), const(0, 0)),
            ((mix_out, width_all), F32, (mix_out, width_all), const(0, 0)),
        ],
        name="middle",
        flops=6 * tokens * width_all * mix_out,
    )

    last_step = hidden_steps - 1
    mix_rows = -(-mix_out // 16) * 16
    branch_in = (branch_grad, (tokens, width_all), const(0, 0))
    (both_part,) = call(
        functools.partial(down_grad_kernel, hidden_steps),
        (hidden_steps + 1,),
        ins=[
            (hidden, (tokens, heads_width), lambda j, p: (0, jnp.minimum(j, last_step))),
            (attended, (tokens, heads_width), const(0, 0)),
            branch_in,
        ],
        outs=[
            (
                (hidden_width + heads_width + mix_rows, width_all),
                BF16,
                (heads_width, width_all),
                lambda j, p: (j, 0),
            )
        ],
        name="down_grad",
        flops=2 * tokens * width_all * (hidden_width + heads_width),
    )
    both_part = lax.dynamic_update_slice_in_dim(
        both_part,
        jnp.pad(mix_part, ((0, mix_rows - mix_out), (0, 0))).astype(BF16),
        hidden_width + heads_width,
        0,
    )
    branch_grad = after(branch_grad, both_part)
    branch_in = (branch_grad, (tokens, width_all), const(0, 0))
    tensor_bits = axis_bits("tensor")
    fixed_sums = after(fixed_part, branch_pieces)
    fixed_sums = fixed_sums + swap(fixed_sums, "tensor", tensor_bits[0])
    branch_grad = after(branch_grad, fixed_sums)
    branch_in = (branch_grad, (tokens, width_all), const(0, 0))
    (attended_grad,) = call(
        back_kernel,
        (tokens // ROWS,),
        ins=[
            (branch_grad, (ROWS, width_all), lambda i, p: (i, 0)),
            (both_full, (heads_width, width_all), const(hidden_steps, 0)),
        ],
        outs=[((tokens, heads_width), BF16, (ROWS, heads_width), lambda i, p: (i, 0))],
        name="attended_grad",
        flops=2 * tokens * width_all * heads_width,
    )
    for bit in tensor_bits[1:]:
        fixed_sums = fixed_sums + swap(fixed_sums, "tensor", bit)
    next_bits = axis_bits("dp")
    next_sum = next_part + swap(next_part, "dp", next_bits[0])
    lin_grads = pl.pallas_call(
        attend_back_kernel,
        out_shape=jax.ShapeDtypeStruct((3, tokens, heads_width), BF16),
        grid_spec=pltpu.PrefetchScalarGridSpec(
            num_scalar_prefetch=1,
            grid=(heads,),
            in_specs=[pl.BlockSpec(b, m) for _, b, m in head_ins]
            + [pl.BlockSpec((tokens, HEAD_DIM), lambda h, p: (0, h))]
            + [pl.BlockSpec(b, m) for _, b, m in table_ins],
            out_specs=pl.BlockSpec((3, tokens, HEAD_DIM), lambda h, p: (0, 0, h)),
            scratch_shapes=[pltpu.VMEM((tokens, HEAD_DIM), F32)] * 2,
        ),
        compiler_params=pltpu.CompilerParams(vmem_limit_bytes=VMEM_BYTES),
        cost_estimate=pl.CostEstimate(
            flops=10 * tokens * tokens * heads_width,
            bytes_accessed=8 * tokens * heads_width * 2,
            transcendentals=heads * tokens * tokens,
        ),
        name="attend_back",
    )(place, qkv, qkv, qkv, attended_grad, *tables)
    def qkv_back(grads, begin, end):
        return call(
            back_kernel,
            (end - begin, count),
            ins=[
                (grads, (None, tokens, heads_width), lambda c, r, p: (c + begin, 0, 0)),
                (qkv_full, (None, width, heads_width), lambda c, r, p: (c + begin, p[0] ^ r, 0)),
            ],
            outs=[
                (
                    (count, end - begin, tokens, width),
                    BF16,
                    (None, None, tokens, width),
                    lambda c, r, p: (r, c, 0, 0),
                )
            ],
            name="qkv_back",
            flops=2 * (end - begin) * tokens * width_all * heads_width,
        )[0]

    grads_a = qkv_back(lin_grads, 0, 1)
    states_a = scatter_start(grads_a)
    lin_grads = after(lin_grads, grads_a)
    grads_b = qkv_back(lin_grads, 1, 3)
    states_b = scatter_start(grads_b)
    branch_grad = after(branch_grad, grads_b, next_sum, fixed_sums)
    branch_in = (branch_grad, (tokens, width_all), const(0, 0))
    (hidden_grad,) = call(
        hidden_grad_kernel,
        (hidden_steps,),
        ins=[
            branch_in,
            (both_full, (heads_width, width_all), lambda j, p: (j, 0)),
            (slope, (tokens, heads_width), lambda j, p: (0, j)),
        ],
        outs=[((tokens, hidden_width), BF16, (tokens, heads_width), lambda j, p: (0, j))],
        name="hidden_grad",
        flops=2 * tokens * width_all * hidden_width,
    )
    hidden_grad = after(hidden_grad, *scatter_arrived(states_a))
    (last_grads,) = call(
        back_kernel,
        (count,),
        ins=[
            (hidden_grad, (tokens, hidden_width), const(0, 0)),
            (up_full, (width, hidden_width), lambda r, p: (p[0] ^ r, 0)),
        ],
        outs=[((count, tokens, width), BF16, (None, tokens, width), lambda r, p: (r, 0, 0))],
        name="up_back",
        flops=2 * tokens * width_all * hidden_width,
    )
    last_states = scatter_start(last_grads)
    hidden_grad = after(hidden_grad, last_grads)
    for bit in next_bits[1:]:
        next_sum = next_sum + swap(next_sum, "dp", bit)
    all_steps = hidden_steps + 3
    lin_step = lambda j: jnp.maximum(j - hidden_steps, 0)
    (wide_part,) = call(
        functools.partial(
            weight_grad_kernel, [len(parts) for parts in last_pieces], hidden_steps
        ),
        (all_steps, count),
        ins=[(part, part.shape, const(0, 0)) for parts in last_pieces for part in parts]
        + [
            (part, (None, *part.shape[1:]), lambda j, r, p: (lin_step(j), 0, 0))
            for parts in first_pieces
            for part in parts
        ]
        + [
            (
                hidden_grad,
                (tokens, heads_width),
                lambda j, r, p: (0, jnp.minimum(j, hidden_steps - 1)),
            ),
            (lin_grads, (None, tokens, heads_width), lambda j, r, p: (lin_step(j), 0, 0)),
        ],
        outs=[
            (
                (width_all, all_steps * heads_width),
                BF16,
                (width, heads_width),
                lambda j, r, p: (p[0] ^ r, j),
            )
        ],
        name="weight_grad",
        flops=2 * tokens * width_all * (hidden_width + 3 * heads_width),
        scratch=[((count, width, tokens), BF16)],
    )
    wide_part = after(
        wide_part,
        *scatter_arrived(states_b),
        *scatter_arrived(last_states),
    )
    together(states_b + last_states)
    later = [scatter_second(states) for states in (states_a, states_b, last_states)]
    together([state for states in later for state in states])
    first_grad = jnp.concatenate([scatter_end(later[0]), scatter_end(later[1])], 0)
    last_grad = scatter_end(later[2])
    both_grad = lax.psum_scatter(both_part, "dp", scatter_dimension=1, tiled=True).astype(F32)
    out_end = hidden_width + heads_width
    down_grad, out_grad = both_grad[:hidden_width], both_grad[hidden_width:out_end]
    mix_proj_grad = both_grad[out_end : out_end + mix_out].T
    wide_grad = lax.psum_scatter(wide_part, "dp", scatter_dimension=0, tiled=True).astype(F32)
    up_grad = wide_grad[:, :hidden_width]
    qkv_grad = jnp.stack(
        [
            wide_grad[:, hidden_width + c * heads_width : hidden_width + (c + 1) * heads_width]
            for c in range(3)
        ]
    )

    grad_ins = [
        (first_grad, (STREAMS - 1, LANES, width), wide_map),
        (last_grad, (LANES, width), lambda i, p: (i, 0)),
        streams_in,
        stats_in,
        gain_in,
    ]
    grad_ins[0] = (after(first_grad, next_sum), *grad_ins[0][1:])
    block_grad_in = (block_grad, (LANES, width), lambda i, p: (i, 0))
    sums, norm_part = call(
        functools.partial(sums_kernel, width_all),
        (token_steps,),
        ins=grad_ins + [hist_in, block_grad_in],
        outs=[
            ((48, tokens), F32, (48, LANES), row_map),
            ((2 * STREAMS, width), F32, (2 * STREAMS, width), const(0, 0)),
        ],
        name="sums",
    )
    dp_bits = axis_bits("dp")
    sums = sums + swap(sums, "tensor", tensor_bits[0])
    norm_part = norm_part + swap(norm_part, "dp", dp_bits[0])
    sums, norm_part = lax.optimization_barrier((sums, norm_part))
    for bit in tensor_bits[1:]:
        sums = sums + swap(sums, "tensor", bit)
    norm_part = norm_part + swap(norm_part, "dp", dp_bits[1])
    sums, norm_part = lax.optimization_barrier((sums, norm_part))
    pairs = STREAMS * ENTRIES
    feature_sums = sums[pairs : pairs + 2 * STREAMS]
    (history_grad,) = call(
        functools.partial(history_kernel, width_all),
        (token_steps,),
        ins=grad_ins
        + [(feature_sums, (2 * STREAMS, LANES), row_map), coef_in, block_grad_in],
        outs=[((ENTRIES, tokens, width), F32, (ENTRIES, LANES, width), wide_map)],
        name="history",
    )
    center = stats[:STREAMS] / width_all
    spread = lax.rsqrt(stats[STREAMS:] / width_all - center * center + ln_eps)
    mix_grad = (
        sums[:pairs].reshape(STREAMS, ENTRIES, tokens)
        - (spread * feature_sums[:STREAMS] / width_all)[:, None]
        * fixed_sums[None, pairs : pairs + ENTRIES]
        - (spread * feature_sums[STREAMS:] / width_all)[:, None]
        * fixed_sums[:pairs].reshape(STREAMS, ENTRIES, tokens)
    ).reshape(pairs, tokens)

    for bit in dp_bits[2:]:
        norm_part = norm_part + swap(norm_part, "dp", bit)
    norm_whole = lax.dynamic_update_slice_in_dim(
        jnp.zeros((2 * STREAMS, width_all), F32), norm_part, tensor_place * width, 1
    )
    norm_whole = butterfly_sum(norm_whole, "tensor")
    norm_whole = lax.dynamic_slice_in_dim(norm_whole, dp_place * share, share, 1)
    next_proj_grad = next_sum
    return (
        block_own,
        next_mix,
        history_grad,
        mix_grad,
        qkv_grad,
        out_grad,
        up_grad,
        down_grad,
        norm_whole[:STREAMS],
        norm_whole[STREAMS:],
        mix_proj_grad,
        next_proj_grad,
    )


def solution(mesh):
    placed = (
        P(None, "dp", "tensor"),
        P(None, "dp"),
        P("dp"),
        P(),
        P("dp", "tensor"),
        P(None, "dp"),
        P(None, "dp", "tensor"),
        P("tensor", "dp"),
        P("dp", "tensor"),
        P("tensor", "dp"),
        P(None, "dp"),
        P(None, "dp"),
        P("dp", None),
        P(),
    )
    return jax.shard_map(
        per_device,
        mesh=mesh,
        in_specs=placed,
        out_specs=(
            P("dp", "tensor"),
            P(None, "dp"),
            P(None, "dp", "tensor"),
            P(None, "dp"),
            P(None, "dp", "tensor"),
            P("tensor", "dp"),
            P("dp", "tensor"),
            P("tensor", "dp"),
            P(None, "dp"),
            P(None, "dp"),
            P("dp", None),
            P(),
        ),
        check_vma=False,
    )
```

```python
import functools

import jax
import jax.numpy as jnp
import numpy as np
from jax import lax
from jax.experimental import pallas as pl
from jax.experimental.pallas import tpu as pltpu
from jax.sharding import PartitionSpec as P

HEAD_DIM = 128
ROT = 32
STREAMS = 4
ENTRIES = 9
LENGTH = 1024
LANES = 128

ln_eps = 1e-05
rms_eps = 1e-06
big_negative = -1e30
root_half = 0.7071067811865476
inv_root_tau = 0.3989422804014327
F32 = jnp.float32
BF16 = jnp.bfloat16
VMEM_BYTES = 56 * 1024 * 1024

NN = (((1,), (0,)), ((), ()))
NT = (((1,), (1,)), ((), ()))
TN = (((0,), (0,)), ((), ()))


def mul(left, right, dims=NN):
    return lax.dot_general(left, right, dims, preferred_element_type=F32)


def kernel_call(body, grid, place, ins, outs, name, flops=0, scratch=()):
    moved = sum(a.size * a.dtype.itemsize for a, _, _ in ins)
    moved += sum(int(np.prod(s)) * jnp.dtype(d).itemsize for s, d, _, _ in outs)
    call = pl.pallas_call(
        body,
        out_shape=[jax.ShapeDtypeStruct(s, d) for s, d, _, _ in outs],
        grid_spec=pltpu.PrefetchScalarGridSpec(
            num_scalar_prefetch=1,
            grid=grid,
            in_specs=[pl.BlockSpec(b, m) for _, b, m in ins],
            out_specs=[pl.BlockSpec(b, m) for _, _, b, m in outs],
            scratch_shapes=[pltpu.VMEM(shape, dtype) for shape, dtype in scratch],
        ),
        compiler_params=pltpu.CompilerParams(
            vmem_limit_bytes=VMEM_BYTES,
            dimension_semantics=("arbitrary",) * len(grid),
        ),
        cost_estimate=pl.CostEstimate(
            flops=int(flops), bytes_accessed=int(moved), transcendentals=0
        ),
        name=name,
    )
    return call(place, *[a for a, _, _ in ins])


def const(*zeros):
    return lambda *_: zeros


def group_parts(refs, shape):
    groups, spot = [], 0
    for parts in shape:
        groups.append(refs[spot : spot + parts])
        spot += parts
    return groups, refs[spot:]


def joined(parts):
    if len(parts) == 1:
        return parts[0][...]
    return jnp.concatenate([part[...] for part in parts], 0)


def normal_parts(x):
    size = jnp.abs(x) * root_half
    lower = 1.0 + 0.3275911 * size
    t = 1.0 / lower
    poly = t * (
        0.254829592
        + t * (-0.284496736 + t * (1.421413741 + t * (-1.453152027 + t * 1.061405429)))
    )
    bell = jnp.exp(-0.5 * x * x)
    tail = 0.5 * poly * bell
    cumulative = jnp.where(x < 0, tail, 1.0 - tail)
    return cumulative, bell * inv_root_tau


def lanes_to_rows(columns, rows):
    lane = lax.broadcasted_iota(jnp.int32, (columns[0].shape[0], LANES), 1)
    wide = jnp.zeros((columns[0].shape[0], LANES), F32)
    for number, column in enumerate(columns):
        wide = jnp.where(lane == number, column, wide)
    return wide.T[:rows]


def mix_kernel(place, hist, coef, streams, stats):
    totals = [None] * STREAMS
    for e in range(ENTRIES):
        entry = hist[e].astype(F32)
        for c in range(STREAMS):
            k = c * ENTRIES + e
            term = coef[:, k : k + 1] * entry
            totals[c] = term if totals[c] is None else totals[c] + term
    columns = []
    for c in range(STREAMS):
        streams[c] = totals[c]
        columns.append(jnp.sum(totals[c], axis=1, keepdims=True))
    for c in range(STREAMS):
        columns.append(jnp.sum(totals[c] * totals[c], axis=1, keepdims=True))
    stats[...] = lanes_to_rows(columns, 2 * STREAMS)


def rows_to_lanes(rows):
    tall = jnp.concatenate([rows, jnp.zeros((LANES - rows.shape[0], LANES), F32)], 0)
    return tall.T


def center_and_spread(stats, width_all):
    turned = rows_to_lanes(stats)
    centers, spreads = [], []
    for c in range(STREAMS):
        center = turned[:, c : c + 1] / width_all
        square = turned[:, STREAMS + c : STREAMS + c + 1] / width_all
        centers.append(center)
        spreads.append(lax.rsqrt(square - center * center + ln_eps))
    return centers, spreads


def norm_kernel(width_all, place, streams, stats, gain, bias, first, last):
    centers, spreads = center_and_spread(stats[...], width_all)
    for c in range(STREAMS):
        unit = (streams[c] - centers[c]) * spreads[c]
        normed = (unit * gain[c : c + 1] + bias[c : c + 1]).astype(BF16)
        if c < STREAMS - 1:
            first[c] = normed
        else:
            last[...] = normed


def spread_kernel(width_all, place, streams, stats, hist, out):
    centers, spreads = center_and_spread(stats[...], width_all)
    units = [(streams[c] - centers[c]) * spreads[c] for c in range(STREAMS)]
    columns = []
    entries = [hist[e].astype(F32) for e in range(ENTRIES)]
    for c in range(STREAMS):
        for e in range(ENTRIES):
            columns.append(jnp.sum(units[c] * entries[e], axis=1, keepdims=True))
    for e in range(ENTRIES):
        columns.append(jnp.sum(entries[e], axis=1, keepdims=True))
    out[...] = lanes_to_rows(columns, out.shape[0])


def turn(x, cosine, ahead, behind):
    half = ROT // 2
    return x * cosine + pltpu.roll(x, half, 1) * ahead + pltpu.roll(x, LANES - half, 1) * behind


def qkv_kernel(shape, place, *refs):
    pieces, refs = group_parts(refs, shape)
    count = len(shape)
    weights, (cosine, ahead, behind, out) = refs[:count], refs[count:]
    total = mul(joined(pieces[0]), weights[0][...])
    for r in range(1, count):
        total += mul(joined(pieces[r]), weights[r][...])
    c = pl.program_id(0)

    @pl.when(c < 2)
    def _():
        for h in range(total.shape[1] // HEAD_DIM):
            spot = slice(h * HEAD_DIM, (h + 1) * HEAD_DIM)
            turned = turn(total[:, spot], cosine[...], ahead[...], behind[...])
            out[:, spot] = turned.astype(BF16)

    @pl.when(c == 2)
    def _():
        out[...] = total.astype(BF16)


ROWS = 256


def attend_kernel(place, q, k, v, out):
    scale = HEAD_DIM**-0.5
    for number in range(q.shape[0] // ROWS):
        start, stop = number * ROWS, (number + 1) * ROWS
        scores = mul(q[start:stop], k[:stop], NT) * scale
        row = lax.broadcasted_iota(jnp.int32, scores.shape, 0) + start
        col = lax.broadcasted_iota(jnp.int32, scores.shape, 1)
        scores = jnp.where(col <= row, scores, big_negative)
        summit = jnp.max(scores, axis=1, keepdims=True)
        exponent = jnp.exp(scores - summit)
        part = jnp.sum(exponent, axis=1, keepdims=True)
        probs = (exponent * (1.0 / part)).astype(BF16)
        out[start:stop] = mul(probs, v[:stop]).astype(BF16)


def attend_back_kernel(place, q, k, v, grad, cosine, ahead, behind, out, dk, dv):
    scale = HEAD_DIM**-0.5
    dk[...] = jnp.zeros_like(dk)
    dv[...] = jnp.zeros_like(dv)
    for number in range(q.shape[0] // ROWS):
        start, stop = number * ROWS, (number + 1) * ROWS
        here = slice(start, stop)
        scores = mul(k[:stop], q[here], NT) * scale
        row = lax.broadcasted_iota(jnp.int32, scores.shape, 0)
        col = lax.broadcasted_iota(jnp.int32, scores.shape, 1) + start
        scores = jnp.where(row <= col, scores, big_negative)
        summit = jnp.max(scores, axis=0, keepdims=True)
        exponent = jnp.exp(scores - summit)
        part = jnp.sum(exponent, axis=0, keepdims=True)
        probs = exponent * (1.0 / part)
        prob_grad = mul(v[:stop], grad[here], NT)
        dv[:stop] += mul(probs.astype(BF16), grad[here])
        center = jnp.sum(probs * prob_grad, axis=0, keepdims=True)
        score_grad = (probs * (prob_grad - center)).astype(BF16)
        dk[:stop] += mul(score_grad, q[here])
        query_grad = mul(score_grad, k[:stop], TN) * scale
        out[0, here] = turn(
            query_grad, cosine[here], -ahead[here], -behind[here]
        ).astype(BF16)
    out[1] = turn(dk[...] * scale, cosine[...], -ahead[...], -behind[...]).astype(BF16)
    out[2] = dv[...].astype(BF16)


def part_rows(parts, start, rows):
    for part in parts:
        if start < part.shape[0]:
            return part[start : start + rows]
        start -= part.shape[0]


def up_kernel(shape, place, *refs):
    pieces, refs = group_parts(refs, shape)
    count = len(shape)
    weights, (hidden, slope) = refs[:count], refs[count:]
    for m in range(hidden.shape[0] // ROWS):
        here = slice(m * ROWS, (m + 1) * ROWS)
        total = mul(part_rows(pieces[0], m * ROWS, ROWS), weights[0][...])
        for r in range(1, count):
            total += mul(part_rows(pieces[r], m * ROWS, ROWS), weights[r][...])
        cumulative, density = normal_parts(total)
        hidden[here] = (total * cumulative).astype(BF16)
        slope[here] = (cumulative + total * density).astype(BF16)


def down_kernel(place, hidden, attended, down, out, branch):
    for m in range(hidden.shape[0] // ROWS):
        here = slice(m * ROWS, (m + 1) * ROWS)
        branch[here] = (
            mul(hidden[here], down[...]) + mul(attended[here], out[...])
        ).astype(BF16)


def spans(pieces, rows):
    ins = []
    for parts in pieces:
        before = 0
        for part in parts:
            steps = part.shape[0] // rows

            def block_map(i, p, before=before, steps=steps):
                return (jnp.clip(i - before, 0, steps - 1), 0)

            ins.append((part, (rows, part.shape[1]), block_map))
            before += steps
    return ins


def pick(parts, steps):
    value, before = parts[0][...], 0
    for number in range(1, len(parts)):
        before += steps[number - 1]
        value = jnp.where(pl.program_id(0) < before, value, parts[number][...])
    return value


def middle_kernel(block_steps, cot_steps, width_all, place, *refs):
    block, refs = group_parts(refs, [len(steps) for steps in block_steps])
    cot, refs = group_parts(refs, [len(steps) for steps in cot_steps])
    count = len(block)
    block = [pick(parts, steps) for parts, steps in zip(block, block_steps)]
    cot = [pick(parts, steps) for parts, steps in zip(cot, cot_steps)]
    weights = refs[:count]
    next_weight, seed, factor = refs[count : 3 + count]
    branch_grad, block_grad, next_mix, next_part, mix_part = refs[3 + count :]
    width = block[0].shape[1]

    @pl.when(pl.program_id(0) == 0)
    def _():
        next_part[...] = jnp.zeros_like(next_part)
        mix_part[...] = jnp.zeros_like(mix_part)

    raw = mul(block[0], weights[0][...])
    for r in range(1, count):
        raw += mul(block[r], weights[r][...])
    square = 0.0
    for r in range(count):
        wide = block[r].astype(F32)
        square += jnp.sum(wide * wide, axis=1, keepdims=True)
    root_inv = lax.rsqrt(square / width_all + rms_eps)
    pre_mix = raw * root_inv
    cumulative, density = normal_parts(pre_mix)
    mix_hidden = (pre_mix * cumulative).astype(BF16)
    next_mix[...] = mul(next_weight[...], mix_hidden, (((0,), (1,)), ((), ())))
    next_part[...] += mul(mix_hidden, seed[...], TN)
    hidden_grad = mul(seed[...], next_weight[...], NT)
    pre_grad = (hidden_grad * (cumulative + pre_mix * density)).astype(BF16)
    inner = jnp.sum(pre_grad.astype(F32) * raw, axis=1, keepdims=True) / width_all
    coef = root_inv * root_inv * root_inv * inner
    for r in range(count):
        offset = pl.multiple_of((place[0] ^ r) * width, LANES)
        wide = block[r].astype(F32)
        scaled = (wide * root_inv).astype(BF16)
        mix_part[:, pl.ds(offset, width)] += mul(pre_grad, scaled, TN)
        scaled_grad = mul(pre_grad, weights[r][...], NT)
        total = (
            root_inv * scaled_grad - wide * coef + cot[r].astype(F32) * factor[...]
        )
        branch_grad[:, pl.ds(offset, width)] = total.astype(BF16)
        if r == 0:
            block_grad[...] = total


def down_grad_kernel(hidden_steps, place, hidden, attended, branch_grad, out):
    def work(left):
        turned = left.T
        for m in range(out.shape[1] // 512):
            here = slice(m * 512, (m + 1) * 512)
            out[:, here] = mul(turned, branch_grad[:, here]).astype(BF16)

    j = pl.program_id(0)

    @pl.when(j < hidden_steps)
    def _():
        work(hidden[...])

    @pl.when(j == hidden_steps)
    def _():
        work(attended[...])


def hidden_grad_kernel(place, branch_grad, weight, slope, hidden_grad):
    for m in range(branch_grad.shape[0] // ROWS):
        here = slice(m * ROWS, (m + 1) * ROWS)
        total = mul(branch_grad[here], weight[...], NT)
        hidden_grad[here] = (total * slope[here].astype(F32)).astype(BF16)


def back_kernel(place, grad, weight, out):
    for m in range(grad.shape[0] // ROWS):
        here = slice(m * ROWS, (m + 1) * ROWS)
        out[here] = mul(grad[here], weight[...], NT).astype(BF16)


def weight_grad_kernel(shape, hidden_steps, place, *refs):
    last, refs = group_parts(refs, shape)
    first, refs = group_parts(refs, shape)
    hidden_grad, lin_grad, out, turned = refs
    j, r = pl.program_id(0), pl.program_id(1)
    for k in range(len(shape)):

        @pl.when((j == 0) & (r == k))
        def _():
            turned[k] = joined(last[k]).T

        @pl.when((j >= hidden_steps) & (r == k))
        def _():
            out[...] = mul(joined(first[k]), lin_grad[...], TN).astype(BF16)

    @pl.when(j < hidden_steps)
    def _():
        out[...] = mul(turned[r], hidden_grad[...]).astype(BF16)


def sums_kernel(
    width_all, place, first, last, streams, stats, gain, hist, block_grad, out, norm_part
):
    @pl.when(pl.program_id(0) == 0)
    def _():
        norm_part[...] = jnp.zeros_like(norm_part)

    centers, spreads = center_and_spread(stats[...], width_all)
    terms, plain, other = [], [], []
    for c in range(STREAMS):
        unit = (streams[c] - centers[c]) * spreads[c]
        grad = first[c] if c < STREAMS - 1 else last[...]
        times = grad * unit
        norm_part[c : c + 1] += jnp.sum(times, axis=0, keepdims=True)
        norm_part[STREAMS + c : STREAMS + c + 1] += jnp.sum(grad, axis=0, keepdims=True)
        scaled = grad * gain[c : c + 1]
        plain.append(jnp.sum(scaled, axis=1, keepdims=True))
        other.append(jnp.sum(scaled * unit, axis=1, keepdims=True))
        term = scaled * spreads[c]
        terms.append(term + block_grad[...] if c == STREAMS - 1 else term)
    columns = [None] * (STREAMS * ENTRIES)
    for e in range(ENTRIES):
        entry = hist[e].astype(F32)
        for c in range(STREAMS):
            columns[c * ENTRIES + e] = jnp.sum(terms[c] * entry, axis=1, keepdims=True)
    out[...] = lanes_to_rows(columns + plain + other, out.shape[0])


def history_kernel(
    width_all, place, first, last, streams, stats, gain, sums, coef, block_grad, out
):
    centers, spreads = center_and_spread(stats[...], width_all)
    turned = rows_to_lanes(sums[...])
    grads = []
    for c in range(STREAMS):
        unit = (streams[c] - centers[c]) * spreads[c]
        grad = first[c] if c < STREAMS - 1 else last[...]
        plain = turned[:, c : c + 1] / width_all
        other = turned[:, STREAMS + c : STREAMS + c + 1] / width_all
        value = spreads[c] * (grad * gain[c : c + 1] - plain - unit * other)
        grads.append(value + block_grad[...] if c == STREAMS - 1 else value)
    for e in range(ENTRIES):
        total = coef[:, e : e + 1] * grads[0]
        for c in range(1, STREAMS):
            k = c * ENTRIES + e
            total += coef[:, k : k + 1] * grads[c]
        out[e] = total


def swap(values, axis, bit):
    count = lax.axis_size(axis)
    return lax.ppermute(values, axis, [(i, i ^ bit) for i in range(count)])


def after(value, *earlier):
    return lax.optimization_barrier((value, earlier))[0]


def axis_bits(axis):
    count = lax.axis_size(axis)
    return [1 << b for b in range(count.bit_length() - 1)]


def butterfly_sum(values, axis):
    for bit in axis_bits(axis):
        values = values + swap(values, axis, bit)
    return values


def gather_start(own):
    bits = axis_bits("tensor")
    if len(bits) == 2:
        return own, [swap(own, "tensor", bit) for bit in bits]
    return own, []


def gather_finish(state):
    own, arrived = state
    bits = axis_bits("tensor")
    half = own.shape[-2] // 2
    if len(bits) == 2:
        one, two = arrived
        top = swap(one[..., :half, :], "tensor", 2)
        bottom = swap(two[..., half:, :], "tensor", 1)
        return [[own], [one], [two], [top, bottom]]
    halves = []
    for part, order in ((own[..., :half, :], bits), (own[..., half:, :], bits[::-1])):
        held = {0: part}
        for bit in order:
            keys = list(held)
            got = swap(jnp.stack([held[k] for k in keys]), "tensor", bit)
            for number, k in enumerate(keys):
                held[k ^ bit] = got[number]
        halves.append(held)
    return [[halves[0][k], halves[1][k]] for k in sorted(halves[0])]


def gather_pieces(own):
    return gather_finish(gather_start(own))


def scatter_start(pieces):
    half = pieces.shape[-2] // 2
    bits = axis_bits("tensor")
    states = []
    for number, order in enumerate((bits, bits[::-1])):
        rows = pieces[..., number * half : (number + 1) * half, :]
        held = {k: rows[k] for k in range(pieces.shape[0])}
        states.append([held, *scatter_send(held, order[0])])
    return states


def scatter_send(held, bit):
    sent = [k for k in held if k & bit]
    return sent, swap(jnp.stack([held[k] for k in sent]).astype(BF16), "tensor", bit), bit


def scatter_add(held, sent, got, bit):
    for spot, k in enumerate(sent):
        held[k ^ bit] = held[k ^ bit].astype(F32) + got[spot].astype(F32)
        del held[k]


def scatter_arrived(states):
    return [state[2] for state in states]


def together(states):
    arrived = lax.optimization_barrier(tuple(scatter_arrived(states)))
    for state, got in zip(states, arrived):
        state[2] = got
    return states


def scatter_second(states):
    bits = axis_bits("tensor")
    later = []
    for (held, sent, got, first), order in zip(states, (bits, bits[::-1])):
        held = dict(held)
        scatter_add(held, sent, got, first)
        for bit in order[1:-1]:
            sent, got, _ = scatter_send(held, bit)
            scatter_add(held, sent, got, bit)
        later.append([held, *scatter_send(held, order[-1])])
    return later


def scatter_end(states):
    sums = []
    for held, sent, got, bit in states:
        held = dict(held)
        scatter_add(held, sent, got, bit)
        sums.append(held[0])
    return jnp.concatenate(sums, -2)


def per_device(
    history,
    mix_in,
    group_ids,
    group_weight,
    block_cotangent,
    mix_cotangent,
    qkv_weight,
    out_weight,
    up_weight,
    down_weight,
    norm_gain,
    norm_bias,
    mix_weight,
    next_weight,
):
    count = lax.axis_size("tensor")
    tensor_place = lax.axis_index("tensor")
    dp_place = lax.axis_index("dp")
    tokens, width = history.shape[1:]
    width_all = width * count
    share = norm_gain.shape[1]
    mix_out = mix_weight.shape[1]
    heads_width = qkv_weight.shape[2]
    heads = heads_width // HEAD_DIM
    hidden_width = up_weight.shape[1]
    hidden_steps = hidden_width // heads_width
    place = jnp.stack([tensor_place, dp_place]).astype(jnp.int32)
    call = functools.partial(kernel_call, place=place)

    def other(r, *rest):
        return lambda *g: (g[-1][0] ^ r,) + rest

    cot_state = gather_start(block_cotangent)

    smalls = jnp.concatenate([norm_gain.T, norm_bias.T, mix_weight], 1)
    smalls = lax.all_gather(smalls, "dp", axis=0, tiled=True)
    mix_full = smalls[:, 2 * STREAMS :]
    norm_own = lax.dynamic_slice_in_dim(
        smalls[:, : 2 * STREAMS].astype(F32), tensor_place * width, width, 0
    ).T
    gain_own, bias_own = norm_own[:STREAMS], norm_own[STREAMS:]
    wide_full = lax.all_gather(
        jnp.concatenate([up_weight, *qkv_weight], 1), "dp", axis=0, tiled=True
    )
    both_full = lax.all_gather(
        jnp.concatenate([down_weight, out_weight], 0), "dp", axis=1, tiled=True
    )

    coef = mix_in.T
    token_steps = tokens // LANES
    hist_in = (history, (ENTRIES, LANES, width), lambda i, p: (0, i, 0))
    coef_in = (coef, (LANES, coef.shape[1]), lambda i, p: (i, 0))
    wide_map = lambda i, p: (0, i, 0)
    row_map = lambda i, p: (0, i)
    streams, stats = call(
        mix_kernel,
        (token_steps,),
        ins=[hist_in, coef_in],
        outs=[
            ((STREAMS, tokens, width), F32, (STREAMS, LANES, width), wide_map),
            ((2 * STREAMS, tokens), F32, (2 * STREAMS, LANES), row_map),
        ],
        name="mix",
        flops=2 * STREAMS * history.size,
    )
    stats = butterfly_sum(after(stats, *cot_state[1]), "tensor")
    cot_pieces = gather_finish(cot_state)
    streams_in = (streams, (STREAMS, LANES, width), wide_map)
    stats_in = (stats, (2 * STREAMS, LANES), row_map)
    gain_in = (gain_own, (STREAMS, width), const(0, 0))
    normed_first, normed_last = call(
        functools.partial(norm_kernel, width_all),
        (token_steps,),
        ins=[streams_in, stats_in, gain_in, (bias_own, (STREAMS, width), const(0, 0))],
        outs=[
            ((STREAMS - 1, tokens, width), BF16, (STREAMS - 1, LANES, width), wide_map),
            ((tokens, width), BF16, (LANES, width), lambda i, p: (i, 0)),
        ],
        name="norm",
    )
    streams_in = (after(streams, normed_last), *streams_in[1:])
    (fixed_part,) = call(
        functools.partial(spread_kernel, width_all),
        (token_steps,),
        ins=[streams_in, stats_in, hist_in],
        outs=[((48, tokens), F32, (48, LANES), row_map)],
        name="spread",
    )

    first_own, first_arrived = gather_start(normed_first)
    first_arrived = [after(arrived, fixed_part) for arrived in first_arrived]
    first_pieces = gather_finish((first_own, first_arrived))
    last_own, last_arrived = gather_start(
        after(normed_last, *[part for parts in first_pieces[1:] for part in parts])
    )

    places = (jnp.arange(tokens, dtype=jnp.int32) % LENGTH).astype(F32)
    freqs = jnp.power(10000.0, -jnp.arange(0, ROT, 2).astype(F32) / ROT)
    angles = places[:, None] * freqs[None, :]
    cosine, sine = jnp.cos(angles), jnp.sin(angles)
    rest = jnp.zeros((tokens, HEAD_DIM - ROT), F32)
    blank = jnp.zeros_like(sine)
    tables = [
        jnp.concatenate([cosine, cosine, rest + 1.0], 1),
        jnp.concatenate([blank, sine, rest], 1),
        jnp.concatenate([-sine, blank, rest], 1),
    ]
    table_ins = [(t, (tokens, HEAD_DIM), const(0, 0)) for t in tables]

    (qkv,) = call(
        functools.partial(qkv_kernel, [len(parts) for parts in first_pieces]),
        (3,),
        ins=[
            (part, (None, *part.shape[1:]), lambda c, p: (c, 0, 0))
            for parts in first_pieces
            for part in parts
        ]
        + [
            (wide_full, (width, heads_width), lambda c, p, r=r: (p[0] ^ r, hidden_steps + c))
            for r in range(count)
        ]
        + table_ins,
        outs=[((3, tokens, heads_width), BF16, (None, tokens, heads_width), lambda c, p: (c, 0, 0))],
        name="qkv",
        flops=6 * tokens * width_all * heads_width,
    )
    head_ins = [
        (qkv, (None, tokens, HEAD_DIM), lambda h, p, c=c: (c, 0, h)) for c in range(3)
    ]
    (attended,) = call(
        attend_kernel,
        (heads,),
        ins=head_ins,
        outs=[((tokens, heads_width), BF16, (tokens, HEAD_DIM), lambda h, p: (0, h))],
        name="attend",
        flops=4 * tokens * tokens * heads_width,
    )
    last_pieces = gather_finish((last_own, [after(arrived, qkv) for arrived in last_arrived]))
    last_pieces[0] = [after(part, attended) for part in last_pieces[0]]
    step = min(512, hidden_width)
    hidden, slope = call(
        functools.partial(up_kernel, [len(parts) for parts in last_pieces]),
        (hidden_width // step,),
        ins=[(part, part.shape, const(0, 0)) for parts in last_pieces for part in parts]
        + [(wide_full, (width, step), lambda j, p, r=r: (p[0] ^ r, j)) for r in range(count)],
        outs=[((tokens, hidden_width), BF16, (tokens, step), lambda j, p: (0, j))] * 2,
        name="up",
        flops=2 * tokens * width_all * hidden_width,
    )
    member = (group_ids[:, None] == jnp.arange(group_weight.shape[0])[None, :]).astype(F32)
    seq_scale = jnp.sum(member * group_weight[None, :], axis=1)
    seed = (mix_cotangent * jnp.repeat(seq_scale, LENGTH)[None, :]).T.astype(BF16)
    factor = jnp.repeat(seq_scale, LENGTH)[:, None]
    seed, factor, mix_full = lax.optimization_barrier((seed, factor, mix_full))
    hidden = after(hidden, seed, factor, mix_full, cot_pieces)
    chunks = 1
    rows = tokens // chunks
    block_owns, block_states, held = [], [], hidden
    for number in range(chunks):
        (branch_pieces,) = call(
            down_kernel,
            (count,),
            ins=[
                (held, (rows, hidden_width), const(number, 0)),
                (attended, (rows, heads_width), const(number, 0)),
                (both_full, (hidden_width, width), lambda r, p: (0, p[0] ^ r)),
                (both_full, (heads_width, width), lambda r, p: (hidden_steps, p[0] ^ r)),
            ],
            outs=[((count, rows, width), BF16, (None, rows, width), lambda r, p: (r, 0, 0))],
            name="down",
            flops=2 * rows * width_all * (hidden_width + heads_width),
        )
        held = after(held, branch_pieces)
        block_states.append(scatter_start(branch_pieces))
    for number in range(chunks):
        residual = streams[STREAMS - 1, number * rows : (number + 1) * rows]
        if number:
            residual = after(residual, *block_states[number - 1][1])
        total = residual + scatter_end(together(scatter_second(together(block_states[number]))))
        block_owns.append(lax.optimization_barrier(total.astype(BF16)))
        block_states[number] = gather_start(block_owns[number])
    block_chunks = [gather_finish(state) for state in block_states]
    block_own = jnp.concatenate(block_owns, 0)
    block_pieces = [[part for chunk in block_chunks for part in chunk[r]] for r in range(count)]

    mid = min(256, tokens)
    branch_grad, block_grad, next_mix, next_part, mix_part = call(
        functools.partial(
            middle_kernel,
            [[part.shape[0] // mid for part in parts] for parts in block_pieces],
            [[part.shape[0] // mid for part in parts] for parts in cot_pieces],
            width_all,
        ),
        (tokens // mid,),
        ins=spans(block_pieces, mid)
        + spans(cot_pieces, mid)
        + [(mix_full, (width, mix_out), other(r, 0)) for r in range(count)]
        + [
            (next_weight, next_weight.shape, const(0, 0)),
            (seed, (mid, mix_out), lambda i, p: (i, 0)),
            (factor, (mid, 1), lambda i, p: (i, 0)),
        ],
        outs=[
            ((tokens, width_all), BF16, (mid, width_all), lambda i, p: (i, 0)),
            ((tokens, width), F32, (mid, width), lambda i, p: (i, 0)),
            ((mix_out, tokens), F32, (mix_out, mid), row_map),
            ((mix_out, mix_out), F32, (mix_out, mix_out), const(0, 0)),
            ((mix_out, width_all), F32, (mix_out, width_all), const(0, 0)),
        ],
        name="middle",
        flops=6 * tokens * width_all * mix_out,
    )

    last_step = hidden_steps - 1
    mix_rows = -(-mix_out // 16) * 16
    branch_in = (branch_grad, (tokens, width_all), const(0, 0))
    (both_part,) = call(
        functools.partial(down_grad_kernel, hidden_steps),
        (hidden_steps + 1,),
        ins=[
            (hidden, (tokens, heads_width), lambda j, p: (0, jnp.minimum(j, last_step))),
            (attended, (tokens, heads_width), const(0, 0)),
            branch_in,
        ],
        outs=[
            (
                (hidden_width + heads_width + mix_rows, width_all),
                BF16,
                (heads_width, width_all),
                lambda j, p: (j, 0),
            )
        ],
        name="down_grad",
        flops=2 * tokens * width_all * (hidden_width + heads_width),
    )
    both_part = lax.dynamic_update_slice_in_dim(
        both_part,
        jnp.pad(mix_part, ((0, mix_rows - mix_out), (0, 0))).astype(BF16),
        hidden_width + heads_width,
        0,
    )
    branch_grad = after(branch_grad, both_part)
    branch_in = (branch_grad, (tokens, width_all), const(0, 0))
    tensor_bits = axis_bits("tensor")
    (attended_grad,) = call(
        back_kernel,
        (tokens // ROWS,),
        ins=[
            (branch_grad, (ROWS, width_all), lambda i, p: (i, 0)),
            (both_full, (heads_width, width_all), const(hidden_steps, 0)),
        ],
        outs=[((tokens, heads_width), BF16, (ROWS, heads_width), lambda i, p: (i, 0))],
        name="attended_grad",
        flops=2 * tokens * width_all * heads_width,
    )
    lin_grads = pl.pallas_call(
        attend_back_kernel,
        out_shape=jax.ShapeDtypeStruct((3, tokens, heads_width), BF16),
        grid_spec=pltpu.PrefetchScalarGridSpec(
            num_scalar_prefetch=1,
            grid=(heads,),
            in_specs=[pl.BlockSpec(b, m) for _, b, m in head_ins]
            + [pl.BlockSpec((tokens, HEAD_DIM), lambda h, p: (0, h))]
            + [pl.BlockSpec(b, m) for _, b, m in table_ins],
            out_specs=pl.BlockSpec((3, tokens, HEAD_DIM), lambda h, p: (0, 0, h)),
            scratch_shapes=[pltpu.VMEM((tokens, HEAD_DIM), F32)] * 2,
        ),
        compiler_params=pltpu.CompilerParams(vmem_limit_bytes=VMEM_BYTES),
        cost_estimate=pl.CostEstimate(
            flops=10 * tokens * tokens * heads_width,
            bytes_accessed=8 * tokens * heads_width * 2,
            transcendentals=heads * tokens * tokens,
        ),
        name="attend_back",
    )(place, qkv, qkv, qkv, attended_grad, *tables)
    def qkv_back(grads, begin, end):
        return call(
            back_kernel,
            (end - begin, count),
            ins=[
                (grads, (None, tokens, heads_width), lambda c, r, p: (c + begin, 0, 0)),
                (
                    wide_full,
                    (width, heads_width),
                    lambda c, r, p: (p[0] ^ r, hidden_steps + c + begin),
                ),
            ],
            outs=[
                (
                    (count, end - begin, tokens, width),
                    BF16,
                    (None, None, tokens, width),
                    lambda c, r, p: (r, c, 0, 0),
                )
            ],
            name="qkv_back",
            flops=2 * (end - begin) * tokens * width_all * heads_width,
        )[0]

    grads_a = qkv_back(lin_grads, 0, 1)
    states_a = scatter_start(grads_a)
    lin_grads = after(lin_grads, grads_a)
    grads_b = qkv_back(lin_grads, 1, 3)
    states_b = scatter_start(grads_b)
    branch_grad = after(branch_grad, grads_b)
    branch_in = (branch_grad, (tokens, width_all), const(0, 0))
    (hidden_grad,) = call(
        hidden_grad_kernel,
        (hidden_steps,),
        ins=[
            branch_in,
            (both_full, (heads_width, width_all), lambda j, p: (j, 0)),
            (slope, (tokens, heads_width), lambda j, p: (0, j)),
        ],
        outs=[((tokens, hidden_width), BF16, (tokens, heads_width), lambda j, p: (0, j))],
        name="hidden_grad",
        flops=2 * tokens * width_all * hidden_width,
    )
    hidden_grad = after(hidden_grad, *scatter_arrived(states_a))
    (last_grads,) = call(
        back_kernel,
        (count,),
        ins=[
            (hidden_grad, (tokens, hidden_width), const(0, 0)),
            (wide_full, (width, hidden_width), lambda r, p: (p[0] ^ r, 0)),
        ],
        outs=[((count, tokens, width), BF16, (None, tokens, width), lambda r, p: (r, 0, 0))],
        name="up_back",
        flops=2 * tokens * width_all * hidden_width,
    )
    last_states = scatter_start(last_grads)
    next_bits = axis_bits("dp")
    fixed_got = swap(after(fixed_part, hidden_grad), "tensor", tensor_bits[0])
    next_got = swap(after(next_part, hidden_grad), "dp", next_bits[0])
    hidden_grad = after(hidden_grad, last_grads)
    all_steps = hidden_steps + 3
    lin_step = lambda j: jnp.maximum(j - hidden_steps, 0)
    (wide_part,) = call(
        functools.partial(
            weight_grad_kernel, [len(parts) for parts in last_pieces], hidden_steps
        ),
        (all_steps, count),
        ins=[(part, part.shape, const(0, 0)) for parts in last_pieces for part in parts]
        + [
            (part, (None, *part.shape[1:]), lambda j, r, p: (lin_step(j), 0, 0))
            for parts in first_pieces
            for part in parts
        ]
        + [
            (
                hidden_grad,
                (tokens, heads_width),
                lambda j, r, p: (0, jnp.minimum(j, hidden_steps - 1)),
            ),
            (lin_grads, (None, tokens, heads_width), lambda j, r, p: (lin_step(j), 0, 0)),
        ],
        outs=[
            (
                (width_all, all_steps * heads_width),
                BF16,
                (width, heads_width),
                lambda j, r, p: (p[0] ^ r, j),
            )
        ],
        name="weight_grad",
        flops=2 * tokens * width_all * (hidden_width + 3 * heads_width),
        scratch=[((count, width, tokens), BF16)],
    )
    wide_part = after(
        wide_part,
        fixed_got,
        next_got,
        *scatter_arrived(states_b),
        *scatter_arrived(last_states),
    )
    fixed_sums = fixed_part + fixed_got
    for bit in tensor_bits[1:]:
        fixed_sums = fixed_sums + swap(fixed_sums, "tensor", bit)
    next_sum = next_part + next_got
    next_sum = next_sum + swap(next_sum, "dp", next_bits[1])
    together(states_b + last_states)
    later = [scatter_second(states) for states in (states_a, states_b, last_states)]
    together([state for states in later for state in states] + [[None, None, next_sum]])
    first_grad = jnp.concatenate([scatter_end(later[0]), scatter_end(later[1])], 0)
    last_grad = scatter_end(later[2])
    both_grad = lax.psum_scatter(both_part, "dp", scatter_dimension=1, tiled=True).astype(F32)
    out_end = hidden_width + heads_width
    down_grad, out_grad = both_grad[:hidden_width], both_grad[hidden_width:out_end]
    mix_proj_grad = both_grad[out_end : out_end + mix_out].T
    wide_grad = lax.psum_scatter(wide_part, "dp", scatter_dimension=0, tiled=True).astype(F32)
    up_grad = wide_grad[:, :hidden_width]
    qkv_grad = jnp.stack(
        [
            wide_grad[:, hidden_width + c * heads_width : hidden_width + (c + 1) * heads_width]
            for c in range(3)
        ]
    )

    grad_ins = [
        (first_grad, (STREAMS - 1, LANES, width), wide_map),
        (last_grad, (LANES, width), lambda i, p: (i, 0)),
        streams_in,
        stats_in,
        gain_in,
    ]
    block_grad_in = (block_grad, (LANES, width), lambda i, p: (i, 0))
    sums, norm_part = call(
        functools.partial(sums_kernel, width_all),
        (token_steps,),
        ins=grad_ins + [hist_in, block_grad_in],
        outs=[
            ((48, tokens), F32, (48, LANES), row_map),
            ((2 * STREAMS, width), F32, (2 * STREAMS, width), const(0, 0)),
        ],
        name="sums",
    )
    dp_bits = axis_bits("dp")
    sums = sums + swap(sums, "tensor", tensor_bits[0])
    norm_part = norm_part + swap(norm_part, "dp", dp_bits[0])
    for bit in next_bits[2:]:
        next_sum = next_sum + swap(next_sum, "dp", bit)
    sums, norm_part, next_sum = lax.optimization_barrier((sums, norm_part, next_sum))
    for bit in tensor_bits[1:]:
        sums = sums + swap(sums, "tensor", bit)
    norm_part = norm_part + swap(norm_part, "dp", dp_bits[1])
    sums, norm_part = lax.optimization_barrier((sums, norm_part))
    pairs = STREAMS * ENTRIES
    feature_sums = sums[pairs : pairs + 2 * STREAMS]
    (history_grad,) = call(
        functools.partial(history_kernel, width_all),
        (token_steps,),
        ins=grad_ins
        + [(feature_sums, (2 * STREAMS, LANES), row_map), coef_in, block_grad_in],
        outs=[((ENTRIES, tokens, width), F32, (ENTRIES, LANES, width), wide_map)],
        name="history",
    )
    center = stats[:STREAMS] / width_all
    spread = lax.rsqrt(stats[STREAMS:] / width_all - center * center + ln_eps)
    mix_grad = (
        sums[:pairs].reshape(STREAMS, ENTRIES, tokens)
        - (spread * feature_sums[:STREAMS] / width_all)[:, None]
        * fixed_sums[None, pairs : pairs + ENTRIES]
        - (spread * feature_sums[STREAMS:] / width_all)[:, None]
        * fixed_sums[:pairs].reshape(STREAMS, ENTRIES, tokens)
    ).reshape(pairs, tokens)

    for bit in dp_bits[2:]:
        norm_part = norm_part + swap(norm_part, "dp", bit)
    norm_whole = lax.dynamic_update_slice_in_dim(
        jnp.zeros((2 * STREAMS, width_all), F32), norm_part, tensor_place * width, 1
    )
    norm_whole = butterfly_sum(norm_whole, "tensor")
    norm_whole = lax.dynamic_slice_in_dim(norm_whole, dp_place * share, share, 1)
    next_proj_grad = next_sum
    return (
        block_own,
        next_mix,
        history_grad,
        mix_grad,
        qkv_grad,
        out_grad,
        up_grad,
        down_grad,
        norm_whole[:STREAMS],
        norm_whole[STREAMS:],
        mix_proj_grad,
        next_proj_grad,
    )


def solution(mesh):
    placed = (
        P(None, "dp", "tensor"),
        P(None, "dp"),
        P("dp"),
        P(),
        P("dp", "tensor"),
        P(None, "dp"),
        P(None, "dp", "tensor"),
        P("tensor", "dp"),
        P("dp", "tensor"),
        P("tensor", "dp"),
        P(None, "dp"),
        P(None, "dp"),
        P("dp", None),
        P(),
    )
    return jax.shard_map(
        per_device,
        mesh=mesh,
        in_specs=placed,
        out_specs=(
            P("dp", "tensor"),
            P(None, "dp"),
            P(None, "dp", "tensor"),
            P(None, "dp"),
            P(None, "dp", "tensor"),
            P("tensor", "dp"),
            P("dp", "tensor"),
            P("tensor", "dp"),
            P(None, "dp"),
            P(None, "dp"),
            P("dp", None),
            P(),
        ),
        check_vma=False,
    )
```

```python
import functools

import jax
import jax.numpy as jnp
import numpy as np
from jax import lax
from jax.experimental import pallas as pl
from jax.experimental.pallas import tpu as pltpu
from jax.sharding import PartitionSpec as P

HEAD_DIM = 128
ROT = 32
STREAMS = 4
ENTRIES = 9
LENGTH = 1024
LANES = 128

ln_eps = 1e-05
rms_eps = 1e-06
big_negative = -1e30
root_half = 0.7071067811865476
inv_root_tau = 0.3989422804014327
F32 = jnp.float32
BF16 = jnp.bfloat16
VMEM_BYTES = 56 * 1024 * 1024

NN = (((1,), (0,)), ((), ()))
NT = (((1,), (1,)), ((), ()))
TN = (((0,), (0,)), ((), ()))


def mul(left, right, dims=NN):
    return lax.dot_general(left, right, dims, preferred_element_type=F32)


def kernel_call(body, grid, place, ins, outs, name, flops=0, scratch=()):
    moved = sum(a.size * a.dtype.itemsize for a, _, _ in ins)
    moved += sum(int(np.prod(s)) * jnp.dtype(d).itemsize for s, d, _, _ in outs)
    call = pl.pallas_call(
        body,
        out_shape=[jax.ShapeDtypeStruct(s, d) for s, d, _, _ in outs],
        grid_spec=pltpu.PrefetchScalarGridSpec(
            num_scalar_prefetch=1,
            grid=grid,
            in_specs=[pl.BlockSpec(b, m) for _, b, m in ins],
            out_specs=[pl.BlockSpec(b, m) for _, _, b, m in outs],
            scratch_shapes=[pltpu.VMEM(shape, dtype) for shape, dtype in scratch],
        ),
        compiler_params=pltpu.CompilerParams(
            vmem_limit_bytes=VMEM_BYTES,
            dimension_semantics=("arbitrary",) * len(grid),
        ),
        cost_estimate=pl.CostEstimate(
            flops=int(flops), bytes_accessed=int(moved), transcendentals=0
        ),
        name=name,
    )
    return call(place, *[a for a, _, _ in ins])


def const(*zeros):
    return lambda *_: zeros


def group_parts(refs, shape):
    groups, spot = [], 0
    for parts in shape:
        groups.append(refs[spot : spot + parts])
        spot += parts
    return groups, refs[spot:]


def joined(parts):
    if len(parts) == 1:
        return parts[0][...]
    return jnp.concatenate([part[...] for part in parts], 0)


def normal_parts(x):
    size = jnp.abs(x) * root_half
    lower = 1.0 + 0.3275911 * size
    t = 1.0 / lower
    poly = t * (
        0.254829592
        + t * (-0.284496736 + t * (1.421413741 + t * (-1.453152027 + t * 1.061405429)))
    )
    bell = jnp.exp(-0.5 * x * x)
    tail = 0.5 * poly * bell
    cumulative = jnp.where(x < 0, tail, 1.0 - tail)
    return cumulative, bell * inv_root_tau


def lanes_to_rows(columns, rows):
    lane = lax.broadcasted_iota(jnp.int32, (columns[0].shape[0], LANES), 1)
    wide = jnp.zeros((columns[0].shape[0], LANES), F32)
    for number, column in enumerate(columns):
        wide = jnp.where(lane == number, column, wide)
    return wide.T[:rows]


def mix_kernel(place, hist, coef, streams, stats):
    totals = [None] * STREAMS
    for e in range(ENTRIES):
        entry = hist[e].astype(F32)
        for c in range(STREAMS):
            k = c * ENTRIES + e
            term = coef[:, k : k + 1] * entry
            totals[c] = term if totals[c] is None else totals[c] + term
    columns = []
    for c in range(STREAMS):
        streams[c] = totals[c]
        columns.append(jnp.sum(totals[c], axis=1, keepdims=True))
    for c in range(STREAMS):
        columns.append(jnp.sum(totals[c] * totals[c], axis=1, keepdims=True))
    stats[...] = lanes_to_rows(columns, 2 * STREAMS)


def rows_to_lanes(rows):
    tall = jnp.concatenate([rows, jnp.zeros((LANES - rows.shape[0], LANES), F32)], 0)
    return tall.T


def center_and_spread(stats, width_all):
    turned = rows_to_lanes(stats)
    centers, spreads = [], []
    for c in range(STREAMS):
        center = turned[:, c : c + 1] / width_all
        square = turned[:, STREAMS + c : STREAMS + c + 1] / width_all
        centers.append(center)
        spreads.append(lax.rsqrt(square - center * center + ln_eps))
    return centers, spreads


def norm_kernel(width_all, place, streams, stats, gain, bias, first, last):
    centers, spreads = center_and_spread(stats[...], width_all)
    for c in range(STREAMS):
        unit = (streams[c] - centers[c]) * spreads[c]
        normed = (unit * gain[c : c + 1] + bias[c : c + 1]).astype(BF16)
        if c < STREAMS - 1:
            first[c] = normed
        else:
            last[...] = normed


def spread_kernel(width_all, place, streams, stats, hist, out):
    centers, spreads = center_and_spread(stats[...], width_all)
    units = [(streams[c] - centers[c]) * spreads[c] for c in range(STREAMS)]
    columns = []
    entries = [hist[e].astype(F32) for e in range(ENTRIES)]
    for c in range(STREAMS):
        for e in range(ENTRIES):
            columns.append(jnp.sum(units[c] * entries[e], axis=1, keepdims=True))
    for e in range(ENTRIES):
        columns.append(jnp.sum(entries[e], axis=1, keepdims=True))
    out[...] = lanes_to_rows(columns, out.shape[0])


def turn(x, cosine, ahead, behind):
    half = ROT // 2
    return x * cosine + pltpu.roll(x, half, 1) * ahead + pltpu.roll(x, LANES - half, 1) * behind


def qkv_kernel(shape, place, *refs):
    pieces, refs = group_parts(refs, shape)
    count = len(shape)
    weights, (cosine, ahead, behind, out) = refs[:count], refs[count:]
    total = mul(joined(pieces[0]), weights[0][...])
    for r in range(1, count):
        total += mul(joined(pieces[r]), weights[r][...])
    c = pl.program_id(0)

    @pl.when(c < 2)
    def _():
        for h in range(total.shape[1] // HEAD_DIM):
            spot = slice(h * HEAD_DIM, (h + 1) * HEAD_DIM)
            turned = turn(total[:, spot], cosine[...], ahead[...], behind[...])
            out[:, spot] = turned.astype(BF16)

    @pl.when(c == 2)
    def _():
        out[...] = total.astype(BF16)


ROWS = 256


def attend_kernel(place, q, k, v, out):
    scale = HEAD_DIM**-0.5
    for number in range(q.shape[0] // ROWS):
        start, stop = number * ROWS, (number + 1) * ROWS
        scores = mul(q[start:stop], k[:stop], NT) * scale
        row = lax.broadcasted_iota(jnp.int32, scores.shape, 0) + start
        col = lax.broadcasted_iota(jnp.int32, scores.shape, 1)
        scores = jnp.where(col <= row, scores, big_negative)
        summit = jnp.max(scores, axis=1, keepdims=True)
        exponent = jnp.exp(scores - summit)
        part = jnp.sum(exponent, axis=1, keepdims=True)
        probs = (exponent * (1.0 / part)).astype(BF16)
        out[start:stop] = mul(probs, v[:stop]).astype(BF16)


def attend_back_kernel(place, q, k, v, grad, cosine, ahead, behind, out, dk, dv):
    scale = HEAD_DIM**-0.5
    dk[...] = jnp.zeros_like(dk)
    dv[...] = jnp.zeros_like(dv)
    for number in range(q.shape[0] // ROWS):
        start, stop = number * ROWS, (number + 1) * ROWS
        here = slice(start, stop)
        scores = mul(k[:stop], q[here], NT) * scale
        row = lax.broadcasted_iota(jnp.int32, scores.shape, 0)
        col = lax.broadcasted_iota(jnp.int32, scores.shape, 1) + start
        scores = jnp.where(row <= col, scores, big_negative)
        summit = jnp.max(scores, axis=0, keepdims=True)
        exponent = jnp.exp(scores - summit)
        part = jnp.sum(exponent, axis=0, keepdims=True)
        probs = exponent * (1.0 / part)
        prob_grad = mul(v[:stop], grad[here], NT)
        dv[:stop] += mul(probs.astype(BF16), grad[here])
        center = jnp.sum(probs * prob_grad, axis=0, keepdims=True)
        score_grad = (probs * (prob_grad - center)).astype(BF16)
        dk[:stop] += mul(score_grad, q[here])
        query_grad = mul(score_grad, k[:stop], TN) * scale
        out[0, here] = turn(
            query_grad, cosine[here], -ahead[here], -behind[here]
        ).astype(BF16)
    out[1] = turn(dk[...] * scale, cosine[...], -ahead[...], -behind[...]).astype(BF16)
    out[2] = dv[...].astype(BF16)


def part_rows(parts, start, rows):
    for part in parts:
        if start < part.shape[0]:
            return part[start : start + rows]
        start -= part.shape[0]


def up_kernel(shape, place, *refs):
    pieces, refs = group_parts(refs, shape)
    count = len(shape)
    weights, (hidden, slope) = refs[:count], refs[count:]
    for m in range(hidden.shape[0] // ROWS):
        here = slice(m * ROWS, (m + 1) * ROWS)
        total = mul(part_rows(pieces[0], m * ROWS, ROWS), weights[0][...])
        for r in range(1, count):
            total += mul(part_rows(pieces[r], m * ROWS, ROWS), weights[r][...])
        cumulative, density = normal_parts(total)
        hidden[here] = (total * cumulative).astype(BF16)
        slope[here] = (cumulative + total * density).astype(BF16)


def down_kernel(place, hidden, attended, down, out, branch):
    for m in range(hidden.shape[0] // ROWS):
        here = slice(m * ROWS, (m + 1) * ROWS)
        branch[here] = (
            mul(hidden[here], down[...]) + mul(attended[here], out[...])
        ).astype(BF16)


def spans(pieces, rows):
    ins = []
    for parts in pieces:
        before = 0
        for part in parts:
            steps = part.shape[0] // rows

            def block_map(i, p, before=before, steps=steps):
                return (jnp.clip(i - before, 0, steps - 1), 0)

            ins.append((part, (rows, part.shape[1]), block_map))
            before += steps
    return ins


def pick(parts, steps):
    value, before = parts[0][...], 0
    for number in range(1, len(parts)):
        before += steps[number - 1]
        value = jnp.where(pl.program_id(0) < before, value, parts[number][...])
    return value


def middle_kernel(block_steps, cot_steps, width_all, place, *refs):
    block, refs = group_parts(refs, [len(steps) for steps in block_steps])
    cot, refs = group_parts(refs, [len(steps) for steps in cot_steps])
    count = len(block)
    block = [pick(parts, steps) for parts, steps in zip(block, block_steps)]
    cot = [pick(parts, steps) for parts, steps in zip(cot, cot_steps)]
    weights = refs[:count]
    next_weight, seed, factor = refs[count : 3 + count]
    branch_grad, block_grad, next_mix, next_part, mix_part = refs[3 + count :]
    width = block[0].shape[1]

    @pl.when(pl.program_id(0) == 0)
    def _():
        next_part[...] = jnp.zeros_like(next_part)
        mix_part[...] = jnp.zeros_like(mix_part)

    raw = mul(block[0], weights[0][...])
    for r in range(1, count):
        raw += mul(block[r], weights[r][...])
    square = 0.0
    for r in range(count):
        wide = block[r].astype(F32)
        square += jnp.sum(wide * wide, axis=1, keepdims=True)
    root_inv = lax.rsqrt(square / width_all + rms_eps)
    pre_mix = raw * root_inv
    cumulative, density = normal_parts(pre_mix)
    mix_hidden = (pre_mix * cumulative).astype(BF16)
    next_mix[...] = mul(next_weight[...], mix_hidden, (((0,), (1,)), ((), ())))
    next_part[...] += mul(mix_hidden, seed[...], TN)
    hidden_grad = mul(seed[...], next_weight[...], NT)
    pre_grad = (hidden_grad * (cumulative + pre_mix * density)).astype(BF16)
    inner = jnp.sum(pre_grad.astype(F32) * raw, axis=1, keepdims=True) / width_all
    coef = root_inv * root_inv * root_inv * inner
    for r in range(count):
        offset = pl.multiple_of((place[0] ^ r) * width, LANES)
        wide = block[r].astype(F32)
        scaled = (wide * root_inv).astype(BF16)
        mix_part[:, pl.ds(offset, width)] += mul(pre_grad, scaled, TN)
        scaled_grad = mul(pre_grad, weights[r][...], NT)
        total = (
            root_inv * scaled_grad - wide * coef + cot[r].astype(F32) * factor[...]
        )
        branch_grad[:, pl.ds(offset, width)] = total.astype(BF16)
        if r == 0:
            block_grad[...] = total


def down_grad_kernel(hidden_steps, place, hidden, attended, branch_grad, out):
    def work(left):
        turned = left.T
        for m in range(out.shape[1] // 512):
            here = slice(m * 512, (m + 1) * 512)
            out[:, here] = mul(turned, branch_grad[:, here]).astype(BF16)

    j = pl.program_id(0)

    @pl.when(j < hidden_steps)
    def _():
        work(hidden[...])

    @pl.when(j == hidden_steps)
    def _():
        work(attended[...])


def hidden_grad_kernel(place, branch_grad, weight, slope, hidden_grad):
    for m in range(branch_grad.shape[0] // ROWS):
        here = slice(m * ROWS, (m + 1) * ROWS)
        total = mul(branch_grad[here], weight[...], NT)
        hidden_grad[here] = (total * slope[here].astype(F32)).astype(BF16)


def back_kernel(place, grad, weight, out):
    for m in range(grad.shape[0] // ROWS):
        here = slice(m * ROWS, (m + 1) * ROWS)
        out[here] = mul(grad[here], weight[...], NT).astype(BF16)


def weight_grad_kernel(shape, hidden_steps, place, *refs):
    last, refs = group_parts(refs, shape)
    first, refs = group_parts(refs, shape)
    hidden_grad, lin_grad, out, turned = refs
    j = pl.program_id(0)
    width = turned.shape[1]

    def store(k, total):
        offset = pl.multiple_of((place[0] ^ k) * width, width)
        out[pl.ds(offset, width), :] = total.astype(BF16)

    @pl.when(j == 0)
    def _():
        for k in range(len(shape)):
            turned[k] = joined(last[k]).T

    @pl.when(j < hidden_steps)
    def _():
        for k in range(len(shape)):
            store(k, mul(turned[k], hidden_grad[...]))

    @pl.when(j >= hidden_steps)
    def _():
        for k in range(len(shape)):
            store(k, mul(joined(first[k]), lin_grad[...], TN))


def sums_kernel(
    width_all, place, first, last, streams, stats, gain, hist, block_grad, out, norm_part
):
    @pl.when(pl.program_id(0) == 0)
    def _():
        norm_part[...] = jnp.zeros_like(norm_part)

    centers, spreads = center_and_spread(stats[...], width_all)
    terms, plain, other = [], [], []
    for c in range(STREAMS):
        unit = (streams[c] - centers[c]) * spreads[c]
        grad = first[c] if c < STREAMS - 1 else last[...]
        times = grad * unit
        norm_part[c : c + 1] += jnp.sum(times, axis=0, keepdims=True)
        norm_part[STREAMS + c : STREAMS + c + 1] += jnp.sum(grad, axis=0, keepdims=True)
        scaled = grad * gain[c : c + 1]
        plain.append(jnp.sum(scaled, axis=1, keepdims=True))
        other.append(jnp.sum(scaled * unit, axis=1, keepdims=True))
        term = scaled * spreads[c]
        terms.append(term + block_grad[...] if c == STREAMS - 1 else term)
    columns = [None] * (STREAMS * ENTRIES)
    for e in range(ENTRIES):
        entry = hist[e].astype(F32)
        for c in range(STREAMS):
            columns[c * ENTRIES + e] = jnp.sum(terms[c] * entry, axis=1, keepdims=True)
    out[...] = lanes_to_rows(columns + plain + other, out.shape[0])


def history_kernel(
    width_all, place, first, last, streams, stats, gain, sums, coef, block_grad, out
):
    centers, spreads = center_and_spread(stats[...], width_all)
    turned = rows_to_lanes(sums[...])
    grads = []
    for c in range(STREAMS):
        unit = (streams[c] - centers[c]) * spreads[c]
        grad = first[c] if c < STREAMS - 1 else last[...]
        plain = turned[:, c : c + 1] / width_all
        other = turned[:, STREAMS + c : STREAMS + c + 1] / width_all
        value = spreads[c] * (grad * gain[c : c + 1] - plain - unit * other)
        grads.append(value + block_grad[...] if c == STREAMS - 1 else value)
    for e in range(ENTRIES):
        total = coef[:, e : e + 1] * grads[0]
        for c in range(1, STREAMS):
            k = c * ENTRIES + e
            total += coef[:, k : k + 1] * grads[c]
        out[e] = total


def swap(values, axis, bit):
    count = lax.axis_size(axis)
    return lax.ppermute(values, axis, [(i, i ^ bit) for i in range(count)])


def after(value, *earlier):
    return lax.optimization_barrier((value, earlier))[0]


def axis_bits(axis):
    count = lax.axis_size(axis)
    return [1 << b for b in range(count.bit_length() - 1)]


def butterfly_sum(values, axis):
    for bit in axis_bits(axis):
        values = values + swap(values, axis, bit)
    return values


def gather_start(own):
    bits = axis_bits("tensor")
    if len(bits) == 2:
        return own, [swap(own, "tensor", bit) for bit in bits]
    return own, []


def gather_finish(state):
    own, arrived = state
    bits = axis_bits("tensor")
    half = own.shape[-2] // 2
    if len(bits) == 2:
        one, two = arrived
        top = swap(one[..., :half, :], "tensor", 2)
        bottom = swap(two[..., half:, :], "tensor", 1)
        return [[own], [one], [two], [top, bottom]]
    halves = []
    for part, order in ((own[..., :half, :], bits), (own[..., half:, :], bits[::-1])):
        held = {0: part}
        for bit in order:
            keys = list(held)
            got = swap(jnp.stack([held[k] for k in keys]), "tensor", bit)
            for number, k in enumerate(keys):
                held[k ^ bit] = got[number]
        halves.append(held)
    return [[halves[0][k], halves[1][k]] for k in sorted(halves[0])]


def gather_pieces(own):
    return gather_finish(gather_start(own))


def scatter_start(pieces):
    half = pieces.shape[-2] // 2
    bits = axis_bits("tensor")
    states = []
    for number, order in enumerate((bits, bits[::-1])):
        rows = pieces[..., number * half : (number + 1) * half, :]
        held = {k: rows[k] for k in range(pieces.shape[0])}
        states.append([held, *scatter_send(held, order[0])])
    return states


def scatter_send(held, bit):
    sent = [k for k in held if k & bit]
    return sent, swap(jnp.stack([held[k] for k in sent]).astype(BF16), "tensor", bit), bit


def scatter_add(held, sent, got, bit):
    for spot, k in enumerate(sent):
        held[k ^ bit] = held[k ^ bit].astype(F32) + got[spot].astype(F32)
        del held[k]


def scatter_arrived(states):
    return [state[2] for state in states]


def together(states):
    arrived = lax.optimization_barrier(tuple(scatter_arrived(states)))
    for state, got in zip(states, arrived):
        state[2] = got
    return states


def scatter_second(states):
    bits = axis_bits("tensor")
    later = []
    for (held, sent, got, first), order in zip(states, (bits, bits[::-1])):
        held = dict(held)
        scatter_add(held, sent, got, first)
        for bit in order[1:-1]:
            sent, got, _ = scatter_send(held, bit)
            scatter_add(held, sent, got, bit)
        later.append([held, *scatter_send(held, order[-1])])
    return later


def scatter_end(states):
    sums = []
    for held, sent, got, bit in states:
        held = dict(held)
        scatter_add(held, sent, got, bit)
        sums.append(held[0])
    return jnp.concatenate(sums, -2)


def per_device(
    history,
    mix_in,
    group_ids,
    group_weight,
    block_cotangent,
    mix_cotangent,
    qkv_weight,
    out_weight,
    up_weight,
    down_weight,
    norm_gain,
    norm_bias,
    mix_weight,
    next_weight,
):
    count = lax.axis_size("tensor")
    tensor_place = lax.axis_index("tensor")
    dp_place = lax.axis_index("dp")
    tokens, width = history.shape[1:]
    width_all = width * count
    share = norm_gain.shape[1]
    mix_out = mix_weight.shape[1]
    heads_width = qkv_weight.shape[2]
    heads = heads_width // HEAD_DIM
    hidden_width = up_weight.shape[1]
    hidden_steps = hidden_width // heads_width
    place = jnp.stack([tensor_place, dp_place]).astype(jnp.int32)
    call = functools.partial(kernel_call, place=place)

    def other(r, *rest):
        return lambda *g: (g[-1][0] ^ r,) + rest

    cot_state = gather_start(block_cotangent)

    smalls = jnp.concatenate([norm_gain.T, norm_bias.T, mix_weight], 1)
    smalls = lax.all_gather(smalls, "dp", axis=0, tiled=True)
    mix_full = smalls[:, 2 * STREAMS :]
    norm_own = lax.dynamic_slice_in_dim(
        smalls[:, : 2 * STREAMS].astype(F32), tensor_place * width, width, 0
    ).T
    gain_own, bias_own = norm_own[:STREAMS], norm_own[STREAMS:]
    wide_full = lax.all_gather(
        jnp.concatenate([up_weight, *qkv_weight], 1), "dp", axis=0, tiled=True
    )
    both_full = lax.all_gather(
        jnp.concatenate([down_weight, out_weight], 0), "dp", axis=1, tiled=True
    )

    coef = mix_in.T
    token_steps = tokens // LANES
    hist_in = (history, (ENTRIES, LANES, width), lambda i, p: (0, i, 0))
    coef_in = (coef, (LANES, coef.shape[1]), lambda i, p: (i, 0))
    wide_map = lambda i, p: (0, i, 0)
    row_map = lambda i, p: (0, i)
    streams, stats = call(
        mix_kernel,
        (token_steps,),
        ins=[hist_in, coef_in],
        outs=[
            ((STREAMS, tokens, width), F32, (STREAMS, LANES, width), wide_map),
            ((2 * STREAMS, tokens), F32, (2 * STREAMS, LANES), row_map),
        ],
        name="mix",
        flops=2 * STREAMS * history.size,
    )
    stats = butterfly_sum(after(stats, *cot_state[1]), "tensor")
    cot_pieces = gather_finish(cot_state)
    streams_in = (streams, (STREAMS, LANES, width), wide_map)
    stats_in = (stats, (2 * STREAMS, LANES), row_map)
    gain_in = (gain_own, (STREAMS, width), const(0, 0))
    normed_first, normed_last = call(
        functools.partial(norm_kernel, width_all),
        (token_steps,),
        ins=[streams_in, stats_in, gain_in, (bias_own, (STREAMS, width), const(0, 0))],
        outs=[
            ((STREAMS - 1, tokens, width), BF16, (STREAMS - 1, LANES, width), wide_map),
            ((tokens, width), BF16, (LANES, width), lambda i, p: (i, 0)),
        ],
        name="norm",
    )
    streams_in = (after(streams, normed_last), *streams_in[1:])
    (fixed_part,) = call(
        functools.partial(spread_kernel, width_all),
        (token_steps,),
        ins=[streams_in, stats_in, hist_in],
        outs=[((48, tokens), F32, (48, LANES), row_map)],
        name="spread",
    )

    first_own, first_arrived = gather_start(normed_first)
    first_arrived = [after(arrived, fixed_part) for arrived in first_arrived]
    first_pieces = gather_finish((first_own, first_arrived))
    last_own, last_arrived = gather_start(
        after(normed_last, *[part for parts in first_pieces[1:] for part in parts])
    )

    places = (jnp.arange(tokens, dtype=jnp.int32) % LENGTH).astype(F32)
    freqs = jnp.power(10000.0, -jnp.arange(0, ROT, 2).astype(F32) / ROT)
    angles = places[:, None] * freqs[None, :]
    cosine, sine = jnp.cos(angles), jnp.sin(angles)
    rest = jnp.zeros((tokens, HEAD_DIM - ROT), F32)
    blank = jnp.zeros_like(sine)
    tables = [
        jnp.concatenate([cosine, cosine, rest + 1.0], 1),
        jnp.concatenate([blank, sine, rest], 1),
        jnp.concatenate([-sine, blank, rest], 1),
    ]
    table_ins = [(t, (tokens, HEAD_DIM), const(0, 0)) for t in tables]

    (qkv,) = call(
        functools.partial(qkv_kernel, [len(parts) for parts in first_pieces]),
        (3,),
        ins=[
            (part, (None, *part.shape[1:]), lambda c, p: (c, 0, 0))
            for parts in first_pieces
            for part in parts
        ]
        + [
            (wide_full, (width, heads_width), lambda c, p, r=r: (p[0] ^ r, hidden_steps + c))
            for r in range(count)
        ]
        + table_ins,
        outs=[((3, tokens, heads_width), BF16, (None, tokens, heads_width), lambda c, p: (c, 0, 0))],
        name="qkv",
        flops=6 * tokens * width_all * heads_width,
    )
    head_ins = [
        (qkv, (None, tokens, HEAD_DIM), lambda h, p, c=c: (c, 0, h)) for c in range(3)
    ]
    (attended,) = call(
        attend_kernel,
        (heads,),
        ins=head_ins,
        outs=[((tokens, heads_width), BF16, (tokens, HEAD_DIM), lambda h, p: (0, h))],
        name="attend",
        flops=4 * tokens * tokens * heads_width,
    )
    last_pieces = gather_finish((last_own, [after(arrived, qkv) for arrived in last_arrived]))
    last_pieces[0] = [after(part, attended) for part in last_pieces[0]]
    step = min(512, hidden_width)
    hidden, slope = call(
        functools.partial(up_kernel, [len(parts) for parts in last_pieces]),
        (hidden_width // step,),
        ins=[(part, part.shape, const(0, 0)) for parts in last_pieces for part in parts]
        + [(wide_full, (width, step), lambda j, p, r=r: (p[0] ^ r, j)) for r in range(count)],
        outs=[((tokens, hidden_width), BF16, (tokens, step), lambda j, p: (0, j))] * 2,
        name="up",
        flops=2 * tokens * width_all * hidden_width,
    )
    member = (group_ids[:, None] == jnp.arange(group_weight.shape[0])[None, :]).astype(F32)
    seq_scale = jnp.sum(member * group_weight[None, :], axis=1)
    seed = (mix_cotangent * jnp.repeat(seq_scale, LENGTH)[None, :]).T.astype(BF16)
    factor = jnp.repeat(seq_scale, LENGTH)[:, None]
    seed, factor, mix_full = lax.optimization_barrier((seed, factor, mix_full))
    hidden = after(hidden, seed, factor, mix_full, cot_pieces)
    chunks = 1
    rows = tokens // chunks
    block_owns, block_states, held = [], [], hidden
    for number in range(chunks):
        (branch_pieces,) = call(
            down_kernel,
            (count,),
            ins=[
                (held, (rows, hidden_width), const(number, 0)),
                (attended, (rows, heads_width), const(number, 0)),
                (both_full, (hidden_width, width), lambda r, p: (0, p[0] ^ r)),
                (both_full, (heads_width, width), lambda r, p: (hidden_steps, p[0] ^ r)),
            ],
            outs=[((count, rows, width), BF16, (None, rows, width), lambda r, p: (r, 0, 0))],
            name="down",
            flops=2 * rows * width_all * (hidden_width + heads_width),
        )
        held = after(held, branch_pieces)
        block_states.append(scatter_start(branch_pieces))
    for number in range(chunks):
        residual = streams[STREAMS - 1, number * rows : (number + 1) * rows]
        if number:
            residual = after(residual, *block_states[number - 1][1])
        total = residual + scatter_end(together(scatter_second(together(block_states[number]))))
        block_owns.append(lax.optimization_barrier(total.astype(BF16)))
        block_states[number] = gather_start(block_owns[number])
    block_chunks = [gather_finish(state) for state in block_states]
    block_own = jnp.concatenate(block_owns, 0)
    block_pieces = [[part for chunk in block_chunks for part in chunk[r]] for r in range(count)]

    mid = min(256, tokens)
    branch_grad, block_grad, next_mix, next_part, mix_part = call(
        functools.partial(
            middle_kernel,
            [[part.shape[0] // mid for part in parts] for parts in block_pieces],
            [[part.shape[0] // mid for part in parts] for parts in cot_pieces],
            width_all,
        ),
        (tokens // mid,),
        ins=spans(block_pieces, mid)
        + spans(cot_pieces, mid)
        + [(mix_full, (width, mix_out), other(r, 0)) for r in range(count)]
        + [
            (next_weight, next_weight.shape, const(0, 0)),
            (seed, (mid, mix_out), lambda i, p: (i, 0)),
            (factor, (mid, 1), lambda i, p: (i, 0)),
        ],
        outs=[
            ((tokens, width_all), BF16, (mid, width_all), lambda i, p: (i, 0)),
            ((tokens, width), F32, (mid, width), lambda i, p: (i, 0)),
            ((mix_out, tokens), F32, (mix_out, mid), row_map),
            ((mix_out, mix_out), F32, (mix_out, mix_out), const(0, 0)),
            ((mix_out, width_all), F32, (mix_out, width_all), const(0, 0)),
        ],
        name="middle",
        flops=6 * tokens * width_all * mix_out,
    )

    last_step = hidden_steps - 1
    mix_rows = -(-mix_out // 16) * 16
    branch_in = (branch_grad, (tokens, width_all), const(0, 0))
    (both_part,) = call(
        functools.partial(down_grad_kernel, hidden_steps),
        (hidden_steps + 1,),
        ins=[
            (hidden, (tokens, heads_width), lambda j, p: (0, jnp.minimum(j, last_step))),
            (attended, (tokens, heads_width), const(0, 0)),
            branch_in,
        ],
        outs=[
            (
                (hidden_width + heads_width + mix_rows, width_all),
                BF16,
                (heads_width, width_all),
                lambda j, p: (j, 0),
            )
        ],
        name="down_grad",
        flops=2 * tokens * width_all * (hidden_width + heads_width),
    )
    both_part = lax.dynamic_update_slice_in_dim(
        both_part,
        jnp.pad(mix_part, ((0, mix_rows - mix_out), (0, 0))).astype(BF16),
        hidden_width + heads_width,
        0,
    )
    branch_grad = after(branch_grad, both_part)
    branch_in = (branch_grad, (tokens, width_all), const(0, 0))
    tensor_bits = axis_bits("tensor")
    (attended_grad,) = call(
        back_kernel,
        (tokens // ROWS,),
        ins=[
            (branch_grad, (ROWS, width_all), lambda i, p: (i, 0)),
            (both_full, (heads_width, width_all), const(hidden_steps, 0)),
        ],
        outs=[((tokens, heads_width), BF16, (ROWS, heads_width), lambda i, p: (i, 0))],
        name="attended_grad",
        flops=2 * tokens * width_all * heads_width,
    )
    lin_grads = pl.pallas_call(
        attend_back_kernel,
        out_shape=jax.ShapeDtypeStruct((3, tokens, heads_width), BF16),
        grid_spec=pltpu.PrefetchScalarGridSpec(
            num_scalar_prefetch=1,
            grid=(heads,),
            in_specs=[pl.BlockSpec(b, m) for _, b, m in head_ins]
            + [pl.BlockSpec((tokens, HEAD_DIM), lambda h, p: (0, h))]
            + [pl.BlockSpec(b, m) for _, b, m in table_ins],
            out_specs=pl.BlockSpec((3, tokens, HEAD_DIM), lambda h, p: (0, 0, h)),
            scratch_shapes=[pltpu.VMEM((tokens, HEAD_DIM), F32)] * 2,
        ),
        compiler_params=pltpu.CompilerParams(vmem_limit_bytes=VMEM_BYTES),
        cost_estimate=pl.CostEstimate(
            flops=10 * tokens * tokens * heads_width,
            bytes_accessed=8 * tokens * heads_width * 2,
            transcendentals=heads * tokens * tokens,
        ),
        name="attend_back",
    )(place, qkv, qkv, qkv, attended_grad, *tables)
    def qkv_back(grads, begin, end):
        return call(
            back_kernel,
            (end - begin, count),
            ins=[
                (grads, (None, tokens, heads_width), lambda c, r, p: (c + begin, 0, 0)),
                (
                    wide_full,
                    (width, heads_width),
                    lambda c, r, p: (p[0] ^ r, hidden_steps + c + begin),
                ),
            ],
            outs=[
                (
                    (count, end - begin, tokens, width),
                    BF16,
                    (None, None, tokens, width),
                    lambda c, r, p: (r, c, 0, 0),
                )
            ],
            name="qkv_back",
            flops=2 * (end - begin) * tokens * width_all * heads_width,
        )[0]

    grads_a = qkv_back(lin_grads, 0, 1)
    states_a = scatter_start(grads_a)
    lin_grads = after(lin_grads, grads_a)
    grads_b = qkv_back(lin_grads, 1, 3)
    states_b = scatter_start(grads_b)
    branch_grad = after(branch_grad, grads_b)
    branch_in = (branch_grad, (tokens, width_all), const(0, 0))
    (hidden_grad,) = call(
        hidden_grad_kernel,
        (hidden_steps,),
        ins=[
            branch_in,
            (both_full, (heads_width, width_all), lambda j, p: (j, 0)),
            (slope, (tokens, heads_width), lambda j, p: (0, j)),
        ],
        outs=[((tokens, hidden_width), BF16, (tokens, heads_width), lambda j, p: (0, j))],
        name="hidden_grad",
        flops=2 * tokens * width_all * hidden_width,
    )
    hidden_grad = after(hidden_grad, *scatter_arrived(states_a))
    (last_grads,) = call(
        back_kernel,
        (count,),
        ins=[
            (hidden_grad, (tokens, hidden_width), const(0, 0)),
            (wide_full, (width, hidden_width), lambda r, p: (p[0] ^ r, 0)),
        ],
        outs=[((count, tokens, width), BF16, (None, tokens, width), lambda r, p: (r, 0, 0))],
        name="up_back",
        flops=2 * tokens * width_all * hidden_width,
    )
    last_states = scatter_start(last_grads)
    next_bits = axis_bits("dp")
    fixed_got = swap(after(fixed_part, hidden_grad), "tensor", tensor_bits[0])
    next_got = swap(after(next_part, hidden_grad), "dp", next_bits[0])
    hidden_grad = after(hidden_grad, last_grads)
    all_steps = hidden_steps + 3
    lin_step = lambda j: jnp.maximum(j - hidden_steps, 0)
    (wide_part,) = call(
        functools.partial(
            weight_grad_kernel, [len(parts) for parts in last_pieces], hidden_steps
        ),
        (all_steps,),
        ins=[(part, part.shape, const(0, 0)) for parts in last_pieces for part in parts]
        + [
            (part, (None, *part.shape[1:]), lambda j, p: (lin_step(j), 0, 0))
            for parts in first_pieces
            for part in parts
        ]
        + [
            (
                hidden_grad,
                (tokens, heads_width),
                lambda j, p: (0, jnp.minimum(j, hidden_steps - 1)),
            ),
            (lin_grads, (None, tokens, heads_width), lambda j, p: (lin_step(j), 0, 0)),
        ],
        outs=[
            (
                (width_all, all_steps * heads_width),
                BF16,
                (width_all, heads_width),
                lambda j, p: (0, j),
            )
        ],
        name="weight_grad",
        flops=2 * tokens * width_all * (hidden_width + 3 * heads_width),
        scratch=[((count, width, tokens), BF16)],
    )
    wide_part = after(
        wide_part,
        fixed_got,
        next_got,
        *scatter_arrived(states_b),
        *scatter_arrived(last_states),
    )
    fixed_sums = fixed_part + fixed_got
    for bit in tensor_bits[1:]:
        fixed_sums = fixed_sums + swap(fixed_sums, "tensor", bit)
    next_sum = next_part + next_got
    next_sum = next_sum + swap(next_sum, "dp", next_bits[1])
    together(states_b + last_states)
    later = [scatter_second(states) for states in (states_a, states_b, last_states)]
    together([state for states in later for state in states] + [[None, None, next_sum]])
    first_grad = jnp.concatenate([scatter_end(later[0]), scatter_end(later[1])], 0)
    last_grad = scatter_end(later[2])
    both_grad = lax.psum_scatter(both_part, "dp", scatter_dimension=1, tiled=True).astype(F32)
    out_end = hidden_width + heads_width
    down_grad, out_grad = both_grad[:hidden_width], both_grad[hidden_width:out_end]
    mix_proj_grad = both_grad[out_end : out_end + mix_out].T
    wide_grad = lax.psum_scatter(wide_part, "dp", scatter_dimension=0, tiled=True).astype(F32)
    up_grad = wide_grad[:, :hidden_width]
    qkv_grad = jnp.stack(
        [
            wide_grad[:, hidden_width + c * heads_width : hidden_width + (c + 1) * heads_width]
            for c in range(3)
        ]
    )

    grad_ins = [
        (first_grad, (STREAMS - 1, LANES, width), wide_map),
        (last_grad, (LANES, width), lambda i, p: (i, 0)),
        streams_in,
        stats_in,
        gain_in,
    ]
    block_grad_in = (block_grad, (LANES, width), lambda i, p: (i, 0))
    sums, norm_part = call(
        functools.partial(sums_kernel, width_all),
        (token_steps,),
        ins=grad_ins + [hist_in, block_grad_in],
        outs=[
            ((48, tokens), F32, (48, LANES), row_map),
            ((2 * STREAMS, width), F32, (2 * STREAMS, width), const(0, 0)),
        ],
        name="sums",
    )
    dp_bits = axis_bits("dp")
    sums = sums + swap(sums, "tensor", tensor_bits[0])
    norm_part = norm_part + swap(norm_part, "dp", dp_bits[0])
    for bit in next_bits[2:]:
        next_sum = next_sum + swap(next_sum, "dp", bit)
    sums, norm_part, next_sum = lax.optimization_barrier((sums, norm_part, next_sum))
    for bit in tensor_bits[1:]:
        sums = sums + swap(sums, "tensor", bit)
    norm_part = norm_part + swap(norm_part, "dp", dp_bits[1])
    sums, norm_part = lax.optimization_barrier((sums, norm_part))
    pairs = STREAMS * ENTRIES
    feature_sums = sums[pairs : pairs + 2 * STREAMS]
    (history_grad,) = call(
        functools.partial(history_kernel, width_all),
        (token_steps,),
        ins=grad_ins
        + [(feature_sums, (2 * STREAMS, LANES), row_map), coef_in, block_grad_in],
        outs=[((ENTRIES, tokens, width), F32, (ENTRIES, LANES, width), wide_map)],
        name="history",
    )
    center = stats[:STREAMS] / width_all
    spread = lax.rsqrt(stats[STREAMS:] / width_all - center * center + ln_eps)
    mix_grad = (
        sums[:pairs].reshape(STREAMS, ENTRIES, tokens)
        - (spread * feature_sums[:STREAMS] / width_all)[:, None]
        * fixed_sums[None, pairs : pairs + ENTRIES]
        - (spread * feature_sums[STREAMS:] / width_all)[:, None]
        * fixed_sums[:pairs].reshape(STREAMS, ENTRIES, tokens)
    ).reshape(pairs, tokens)

    for bit in dp_bits[2:]:
        norm_part = norm_part + swap(norm_part, "dp", bit)
    norm_whole = lax.dynamic_update_slice_in_dim(
        jnp.zeros((2 * STREAMS, width_all), F32), norm_part, tensor_place * width, 1
    )
    norm_whole = butterfly_sum(norm_whole, "tensor")
    norm_whole = lax.dynamic_slice_in_dim(norm_whole, dp_place * share, share, 1)
    next_proj_grad = next_sum
    return (
        block_own,
        next_mix,
        history_grad,
        mix_grad,
        qkv_grad,
        out_grad,
        up_grad,
        down_grad,
        norm_whole[:STREAMS],
        norm_whole[STREAMS:],
        mix_proj_grad,
        next_proj_grad,
    )


def solution(mesh):
    placed = (
        P(None, "dp", "tensor"),
        P(None, "dp"),
        P("dp"),
        P(),
        P("dp", "tensor"),
        P(None, "dp"),
        P(None, "dp", "tensor"),
        P("tensor", "dp"),
        P("dp", "tensor"),
        P("tensor", "dp"),
        P(None, "dp"),
        P(None, "dp"),
        P("dp", None),
        P(),
    )
    return jax.shard_map(
        per_device,
        mesh=mesh,
        in_specs=placed,
        out_specs=(
            P("dp", "tensor"),
            P(None, "dp"),
            P(None, "dp", "tensor"),
            P(None, "dp"),
            P(None, "dp", "tensor"),
            P("tensor", "dp"),
            P("dp", "tensor"),
            P("tensor", "dp"),
            P(None, "dp"),
            P(None, "dp"),
            P("dp", None),
            P(),
        ),
        check_vma=False,
    )
```

```python
import functools

import jax
import jax.numpy as jnp
import numpy as np
from jax import lax
from jax.experimental import pallas as pl
from jax.experimental.pallas import tpu as pltpu
from jax.sharding import PartitionSpec as P

HEAD_DIM = 128
ROT = 32
STREAMS = 4
ENTRIES = 9
LENGTH = 1024
LANES = 128

ln_eps = 1e-05
rms_eps = 1e-06
big_negative = -1e30
root_half = 0.7071067811865476
inv_root_tau = 0.3989422804014327
F32 = jnp.float32
BF16 = jnp.bfloat16
VMEM_BYTES = 56 * 1024 * 1024

NN = (((1,), (0,)), ((), ()))
NT = (((1,), (1,)), ((), ()))
TN = (((0,), (0,)), ((), ()))


def mul(left, right, dims=NN):
    return lax.dot_general(left, right, dims, preferred_element_type=F32)


def kernel_call(body, grid, place, ins, outs, name, flops=0, scratch=()):
    moved = sum(a.size * a.dtype.itemsize for a, _, _ in ins)
    moved += sum(int(np.prod(s)) * jnp.dtype(d).itemsize for s, d, _, _ in outs)
    call = pl.pallas_call(
        body,
        out_shape=[jax.ShapeDtypeStruct(s, d) for s, d, _, _ in outs],
        grid_spec=pltpu.PrefetchScalarGridSpec(
            num_scalar_prefetch=1,
            grid=grid,
            in_specs=[pl.BlockSpec(b, m) for _, b, m in ins],
            out_specs=[pl.BlockSpec(b, m) for _, _, b, m in outs],
            scratch_shapes=[pltpu.VMEM(shape, dtype) for shape, dtype in scratch],
        ),
        compiler_params=pltpu.CompilerParams(
            vmem_limit_bytes=VMEM_BYTES,
            dimension_semantics=("arbitrary",) * len(grid),
        ),
        cost_estimate=pl.CostEstimate(
            flops=int(flops), bytes_accessed=int(moved), transcendentals=0
        ),
        name=name,
    )
    return call(place, *[a for a, _, _ in ins])


def const(*zeros):
    return lambda *_: zeros


def group_parts(refs, shape):
    groups, spot = [], 0
    for parts in shape:
        groups.append(refs[spot : spot + parts])
        spot += parts
    return groups, refs[spot:]


def joined(parts):
    if len(parts) == 1:
        return parts[0][...]
    return jnp.concatenate([part[...] for part in parts], 0)


def normal_parts(x):
    size = jnp.abs(x) * root_half
    lower = 1.0 + 0.3275911 * size
    t = 1.0 / lower
    poly = t * (
        0.254829592
        + t * (-0.284496736 + t * (1.421413741 + t * (-1.453152027 + t * 1.061405429)))
    )
    bell = jnp.exp(-0.5 * x * x)
    tail = 0.5 * poly * bell
    cumulative = jnp.where(x < 0, tail, 1.0 - tail)
    return cumulative, bell * inv_root_tau


def lanes_to_rows(columns, rows):
    lane = lax.broadcasted_iota(jnp.int32, (columns[0].shape[0], LANES), 1)
    wide = jnp.zeros((columns[0].shape[0], LANES), F32)
    for number, column in enumerate(columns):
        wide = jnp.where(lane == number, column, wide)
    return wide.T[:rows]


def mix_kernel(place, hist, coef, streams, stats):
    totals = [None] * STREAMS
    for e in range(ENTRIES):
        entry = hist[e].astype(F32)
        for c in range(STREAMS):
            k = c * ENTRIES + e
            term = coef[:, k : k + 1] * entry
            totals[c] = term if totals[c] is None else totals[c] + term
    columns = []
    for c in range(STREAMS):
        streams[c] = totals[c]
        columns.append(jnp.sum(totals[c], axis=1, keepdims=True))
    for c in range(STREAMS):
        columns.append(jnp.sum(totals[c] * totals[c], axis=1, keepdims=True))
    stats[...] = lanes_to_rows(columns, 2 * STREAMS)


def rows_to_lanes(rows):
    tall = jnp.concatenate([rows, jnp.zeros((LANES - rows.shape[0], LANES), F32)], 0)
    return tall.T


def center_and_spread(stats, width_all):
    turned = rows_to_lanes(stats)
    centers, spreads = [], []
    for c in range(STREAMS):
        center = turned[:, c : c + 1] / width_all
        square = turned[:, STREAMS + c : STREAMS + c + 1] / width_all
        centers.append(center)
        spreads.append(lax.rsqrt(square - center * center + ln_eps))
    return centers, spreads


def norm_kernel(width_all, place, streams, stats, gain, bias, first, last):
    centers, spreads = center_and_spread(stats[...], width_all)
    for c in range(STREAMS):
        unit = (streams[c] - centers[c]) * spreads[c]
        normed = (unit * gain[c : c + 1] + bias[c : c + 1]).astype(BF16)
        if c < STREAMS - 1:
            first[c] = normed
        else:
            last[...] = normed


def spread_kernel(width_all, place, streams, stats, hist, out):
    centers, spreads = center_and_spread(stats[...], width_all)
    units = [(streams[c] - centers[c]) * spreads[c] for c in range(STREAMS)]
    columns = []
    entries = [hist[e].astype(F32) for e in range(ENTRIES)]
    for c in range(STREAMS):
        for e in range(ENTRIES):
            columns.append(jnp.sum(units[c] * entries[e], axis=1, keepdims=True))
    for e in range(ENTRIES):
        columns.append(jnp.sum(entries[e], axis=1, keepdims=True))
    out[...] = lanes_to_rows(columns, out.shape[0])


def turn(x, cosine, ahead, behind):
    half = ROT // 2
    return x * cosine + pltpu.roll(x, half, 1) * ahead + pltpu.roll(x, LANES - half, 1) * behind


def qkv_kernel(shape, place, *refs):
    pieces, refs = group_parts(refs, shape)
    count = len(shape)
    weights, (cosine, ahead, behind, out) = refs[:count], refs[count:]
    total = mul(joined(pieces[0]), weights[0][...])
    for r in range(1, count):
        total += mul(joined(pieces[r]), weights[r][...])
    c = pl.program_id(0)

    @pl.when(c < 2)
    def _():
        for h in range(total.shape[1] // HEAD_DIM):
            spot = slice(h * HEAD_DIM, (h + 1) * HEAD_DIM)
            turned = turn(total[:, spot], cosine[...], ahead[...], behind[...])
            out[:, spot] = turned.astype(BF16)

    @pl.when(c == 2)
    def _():
        out[...] = total.astype(BF16)


ROWS = 256


def attend_kernel(place, q, k, v, out):
    scale = HEAD_DIM**-0.5
    for number in range(q.shape[0] // ROWS):
        start, stop = number * ROWS, (number + 1) * ROWS
        scores = mul(q[start:stop], k[:stop], NT) * scale
        row = lax.broadcasted_iota(jnp.int32, scores.shape, 0) + start
        col = lax.broadcasted_iota(jnp.int32, scores.shape, 1)
        scores = jnp.where(col <= row, scores, big_negative)
        summit = jnp.max(scores, axis=1, keepdims=True)
        exponent = jnp.exp(scores - summit)
        part = jnp.sum(exponent, axis=1, keepdims=True)
        probs = (exponent * (1.0 / part)).astype(BF16)
        out[start:stop] = mul(probs, v[:stop]).astype(BF16)


def attend_back_kernel(place, q, k, v, grad, cosine, ahead, behind, out, dk, dv):
    scale = HEAD_DIM**-0.5
    dk[...] = jnp.zeros_like(dk)
    dv[...] = jnp.zeros_like(dv)
    for number in range(q.shape[0] // ROWS):
        start, stop = number * ROWS, (number + 1) * ROWS
        here = slice(start, stop)
        scores = mul(k[:stop], q[here], NT) * scale
        row = lax.broadcasted_iota(jnp.int32, scores.shape, 0)
        col = lax.broadcasted_iota(jnp.int32, scores.shape, 1) + start
        scores = jnp.where(row <= col, scores, big_negative)
        summit = jnp.max(scores, axis=0, keepdims=True)
        exponent = jnp.exp(scores - summit)
        part = jnp.sum(exponent, axis=0, keepdims=True)
        probs = exponent * (1.0 / part)
        prob_grad = mul(v[:stop], grad[here], NT)
        dv[:stop] += mul(probs.astype(BF16), grad[here])
        center = jnp.sum(probs * prob_grad, axis=0, keepdims=True)
        score_grad = (probs * (prob_grad - center)).astype(BF16)
        dk[:stop] += mul(score_grad, q[here])
        query_grad = mul(score_grad, k[:stop], TN) * scale
        out[0, here] = turn(
            query_grad, cosine[here], -ahead[here], -behind[here]
        ).astype(BF16)
    out[1] = turn(dk[...] * scale, cosine[...], -ahead[...], -behind[...]).astype(BF16)
    out[2] = dv[...].astype(BF16)


def part_rows(parts, start, rows):
    for part in parts:
        if start < part.shape[0]:
            return part[start : start + rows]
        start -= part.shape[0]


def up_kernel(shape, place, *refs):
    pieces, refs = group_parts(refs, shape)
    count = len(shape)
    weights, (hidden, slope) = refs[:count], refs[count:]
    for m in range(hidden.shape[0] // ROWS):
        here = slice(m * ROWS, (m + 1) * ROWS)
        total = mul(part_rows(pieces[0], m * ROWS, ROWS), weights[0][...])
        for r in range(1, count):
            total += mul(part_rows(pieces[r], m * ROWS, ROWS), weights[r][...])
        cumulative, density = normal_parts(total)
        hidden[here] = (total * cumulative).astype(BF16)
        slope[here] = (cumulative + total * density).astype(BF16)


def down_kernel(place, hidden, attended, down, out, branch):
    for m in range(hidden.shape[0] // ROWS):
        here = slice(m * ROWS, (m + 1) * ROWS)
        branch[here] = (
            mul(hidden[here], down[...]) + mul(attended[here], out[...])
        ).astype(BF16)


def spans(pieces, rows):
    ins = []
    for parts in pieces:
        before = 0
        for part in parts:
            steps = part.shape[0] // rows

            def block_map(i, p, before=before, steps=steps):
                return (jnp.clip(i - before, 0, steps - 1), 0)

            ins.append((part, (rows, part.shape[1]), block_map))
            before += steps
    return ins


def pick(parts, steps):
    value, before = parts[0][...], 0
    for number in range(1, len(parts)):
        before += steps[number - 1]
        value = jnp.where(pl.program_id(0) < before, value, parts[number][...])
    return value


def middle_kernel(block_steps, cot_steps, width_all, place, *refs):
    block, refs = group_parts(refs, [len(steps) for steps in block_steps])
    cot, refs = group_parts(refs, [len(steps) for steps in cot_steps])
    count = len(block)
    block = [pick(parts, steps) for parts, steps in zip(block, block_steps)]
    cot = [pick(parts, steps) for parts, steps in zip(cot, cot_steps)]
    weights = refs[:count]
    next_weight, seed, factor = refs[count : 3 + count]
    branch_grad, block_grad, next_mix, next_part, mix_part = refs[3 + count :]
    width = block[0].shape[1]

    @pl.when(pl.program_id(0) == 0)
    def _():
        next_part[...] = jnp.zeros_like(next_part)
        mix_part[...] = jnp.zeros_like(mix_part)

    raw = mul(block[0], weights[0][...])
    for r in range(1, count):
        raw += mul(block[r], weights[r][...])
    square = 0.0
    for r in range(count):
        wide = block[r].astype(F32)
        square += jnp.sum(wide * wide, axis=1, keepdims=True)
    root_inv = lax.rsqrt(square / width_all + rms_eps)
    pre_mix = raw * root_inv
    cumulative, density = normal_parts(pre_mix)
    mix_hidden = (pre_mix * cumulative).astype(BF16)
    next_mix[...] = mul(next_weight[...], mix_hidden, (((0,), (1,)), ((), ())))
    next_part[...] += mul(mix_hidden, seed[...], TN)
    hidden_grad = mul(seed[...], next_weight[...], NT)
    pre_grad = (hidden_grad * (cumulative + pre_mix * density)).astype(BF16)
    inner = jnp.sum(pre_grad.astype(F32) * raw, axis=1, keepdims=True) / width_all
    coef = root_inv * root_inv * root_inv * inner
    for r in range(count):
        offset = pl.multiple_of((place[0] ^ r) * width, LANES)
        wide = block[r].astype(F32)
        scaled = (wide * root_inv).astype(BF16)
        mix_part[:, pl.ds(offset, width)] += mul(pre_grad, scaled, TN)
        scaled_grad = mul(pre_grad, weights[r][...], NT)
        total = (
            root_inv * scaled_grad - wide * coef + cot[r].astype(F32) * factor[...]
        )
        branch_grad[:, pl.ds(offset, width)] = total.astype(BF16)
        if r == 0:
            block_grad[...] = total


def down_grad_kernel(hidden_steps, place, hidden, attended, branch_grad, out):
    def work(left):
        turned = left.T
        for m in range(out.shape[1] // 512):
            here = slice(m * 512, (m + 1) * 512)
            out[:, here] = mul(turned, branch_grad[:, here]).astype(BF16)

    j = pl.program_id(0)

    @pl.when(j < hidden_steps)
    def _():
        work(hidden[...])

    @pl.when(j == hidden_steps)
    def _():
        work(attended[...])


def hidden_grad_kernel(place, branch_grad, weight, slope, hidden_grad):
    for m in range(branch_grad.shape[0] // ROWS):
        here = slice(m * ROWS, (m + 1) * ROWS)
        total = mul(branch_grad[here], weight[...], NT)
        hidden_grad[here] = (total * slope[here].astype(F32)).astype(BF16)


def back_kernel(place, grad, weight, out):
    for m in range(grad.shape[0] // ROWS):
        here = slice(m * ROWS, (m + 1) * ROWS)
        out[here] = mul(grad[here], weight[...], NT).astype(BF16)


def weight_grad_kernel(shape, hidden_steps, place, *refs):
    last, refs = group_parts(refs, shape)
    first, refs = group_parts(refs, shape)
    hidden_grad, lin_grad, out, turned = refs
    j = pl.program_id(0)
    width = turned.shape[1]

    def store(k, total):
        offset = pl.multiple_of((place[0] ^ k) * width, width)
        out[pl.ds(offset, width), :] = total.astype(BF16)

    @pl.when(j == 0)
    def _():
        for k in range(len(shape)):
            turned[k] = joined(last[k]).T

    @pl.when(j < hidden_steps)
    def _():
        for k in range(len(shape)):
            store(k, mul(turned[k], hidden_grad[...]))

    @pl.when(j >= hidden_steps)
    def _():
        for k in range(len(shape)):
            store(k, mul(joined(first[k]), lin_grad[...], TN))


def sums_kernel(
    width_all, place, first, last, streams, stats, gain, hist, block_grad, out, norm_part
):
    @pl.when(pl.program_id(0) == 0)
    def _():
        norm_part[...] = jnp.zeros_like(norm_part)

    centers, spreads = center_and_spread(stats[...], width_all)
    terms, plain, other = [], [], []
    for c in range(STREAMS):
        unit = (streams[c] - centers[c]) * spreads[c]
        grad = first[c] if c < STREAMS - 1 else last[...]
        times = grad * unit
        norm_part[c : c + 1] += jnp.sum(times, axis=0, keepdims=True)
        norm_part[STREAMS + c : STREAMS + c + 1] += jnp.sum(grad, axis=0, keepdims=True)
        scaled = grad * gain[c : c + 1]
        plain.append(jnp.sum(scaled, axis=1, keepdims=True))
        other.append(jnp.sum(scaled * unit, axis=1, keepdims=True))
        term = scaled * spreads[c]
        terms.append(term + block_grad[...] if c == STREAMS - 1 else term)
    columns = [None] * (STREAMS * ENTRIES)
    for e in range(ENTRIES):
        entry = hist[e].astype(F32)
        for c in range(STREAMS):
            columns[c * ENTRIES + e] = jnp.sum(terms[c] * entry, axis=1, keepdims=True)
    out[...] = lanes_to_rows(columns + plain + other, out.shape[0])


def history_kernel(
    width_all, place, first, last, streams, stats, gain, sums, coef, block_grad, out
):
    centers, spreads = center_and_spread(stats[...], width_all)
    turned = rows_to_lanes(sums[...])
    grads = []
    for c in range(STREAMS):
        unit = (streams[c] - centers[c]) * spreads[c]
        grad = first[c] if c < STREAMS - 1 else last[...]
        plain = turned[:, c : c + 1] / width_all
        other = turned[:, STREAMS + c : STREAMS + c + 1] / width_all
        value = spreads[c] * (grad * gain[c : c + 1] - plain - unit * other)
        grads.append(value + block_grad[...] if c == STREAMS - 1 else value)
    for e in range(ENTRIES):
        total = coef[:, e : e + 1] * grads[0]
        for c in range(1, STREAMS):
            k = c * ENTRIES + e
            total += coef[:, k : k + 1] * grads[c]
        out[e] = total


def swap(values, axis, bit):
    count = lax.axis_size(axis)
    return lax.ppermute(values, axis, [(i, i ^ bit) for i in range(count)])


def after(value, *earlier):
    return lax.optimization_barrier((value, earlier))[0]


def axis_bits(axis):
    count = lax.axis_size(axis)
    return [1 << b for b in range(count.bit_length() - 1)]


def butterfly_sum(values, axis):
    for bit in axis_bits(axis):
        values = values + swap(values, axis, bit)
    return values


def gather_start(own):
    bits = axis_bits("tensor")
    if len(bits) == 2:
        return own, [swap(own, "tensor", bit) for bit in bits]
    return own, []


def gather_finish(state):
    own, arrived = state
    bits = axis_bits("tensor")
    half = own.shape[-2] // 2
    if len(bits) == 2:
        one, two = arrived
        top = swap(one[..., :half, :], "tensor", 2)
        bottom = swap(two[..., half:, :], "tensor", 1)
        return [[own], [one], [two], [top, bottom]]
    halves = []
    for part, order in ((own[..., :half, :], bits), (own[..., half:, :], bits[::-1])):
        held = {0: part}
        for bit in order:
            keys = list(held)
            got = swap(jnp.stack([held[k] for k in keys]), "tensor", bit)
            for number, k in enumerate(keys):
                held[k ^ bit] = got[number]
        halves.append(held)
    return [[halves[0][k], halves[1][k]] for k in sorted(halves[0])]


def gather_pieces(own):
    return gather_finish(gather_start(own))


def scatter_start(pieces):
    half = pieces.shape[-2] // 2
    bits = axis_bits("tensor")
    states = []
    for number, order in enumerate((bits, bits[::-1])):
        rows = pieces[..., number * half : (number + 1) * half, :]
        held = {k: rows[k] for k in range(pieces.shape[0])}
        states.append([held, *scatter_send(held, order[0])])
    return states


def scatter_send(held, bit):
    sent = [k for k in held if k & bit]
    return sent, swap(jnp.stack([held[k] for k in sent]).astype(BF16), "tensor", bit), bit


def scatter_add(held, sent, got, bit):
    for spot, k in enumerate(sent):
        held[k ^ bit] = held[k ^ bit].astype(F32) + got[spot].astype(F32)
        del held[k]


def scatter_arrived(states):
    return [state[2] for state in states]


def together(states):
    arrived = lax.optimization_barrier(tuple(scatter_arrived(states)))
    for state, got in zip(states, arrived):
        state[2] = got
    return states


def scatter_second(states):
    bits = axis_bits("tensor")
    later = []
    for (held, sent, got, first), order in zip(states, (bits, bits[::-1])):
        held = dict(held)
        scatter_add(held, sent, got, first)
        for bit in order[1:-1]:
            sent, got, _ = scatter_send(held, bit)
            scatter_add(held, sent, got, bit)
        later.append([held, *scatter_send(held, order[-1])])
    return later


def scatter_end(states):
    sums = []
    for held, sent, got, bit in states:
        held = dict(held)
        scatter_add(held, sent, got, bit)
        sums.append(held[0])
    return jnp.concatenate(sums, -2)


def per_device(
    history,
    mix_in,
    group_ids,
    group_weight,
    block_cotangent,
    mix_cotangent,
    qkv_weight,
    out_weight,
    up_weight,
    down_weight,
    norm_gain,
    norm_bias,
    mix_weight,
    next_weight,
):
    count = lax.axis_size("tensor")
    tensor_place = lax.axis_index("tensor")
    dp_place = lax.axis_index("dp")
    tokens, width = history.shape[1:]
    width_all = width * count
    share = norm_gain.shape[1]
    mix_out = mix_weight.shape[1]
    heads_width = qkv_weight.shape[2]
    heads = heads_width // HEAD_DIM
    hidden_width = up_weight.shape[1]
    hidden_steps = hidden_width // heads_width
    place = jnp.stack([tensor_place, dp_place]).astype(jnp.int32)
    call = functools.partial(kernel_call, place=place)

    def other(r, *rest):
        return lambda *g: (g[-1][0] ^ r,) + rest

    cot_state = gather_start(block_cotangent)

    smalls = jnp.concatenate([norm_gain.T, norm_bias.T, mix_weight], 1)
    smalls = lax.all_gather(smalls, "dp", axis=0, tiled=True)
    mix_full = smalls[:, 2 * STREAMS :]
    norm_own = lax.dynamic_slice_in_dim(
        smalls[:, : 2 * STREAMS].astype(F32), tensor_place * width, width, 0
    ).T
    gain_own, bias_own = norm_own[:STREAMS], norm_own[STREAMS:]
    wide_full = lax.all_gather(
        jnp.concatenate([up_weight, *qkv_weight], 1), "dp", axis=0, tiled=True
    )
    both_full = lax.all_gather(
        jnp.concatenate([down_weight, out_weight], 0), "dp", axis=1, tiled=True
    )

    coef = mix_in.T
    token_steps = tokens // LANES
    hist_in = (history, (ENTRIES, LANES, width), lambda i, p: (0, i, 0))
    coef_in = (coef, (LANES, coef.shape[1]), lambda i, p: (i, 0))
    wide_map = lambda i, p: (0, i, 0)
    row_map = lambda i, p: (0, i)
    streams, stats = call(
        mix_kernel,
        (token_steps,),
        ins=[hist_in, coef_in],
        outs=[
            ((STREAMS, tokens, width), F32, (STREAMS, LANES, width), wide_map),
            ((2 * STREAMS, tokens), F32, (2 * STREAMS, LANES), row_map),
        ],
        name="mix",
        flops=2 * STREAMS * history.size,
    )
    stats = butterfly_sum(after(stats, *cot_state[1]), "tensor")
    cot_pieces = gather_finish(cot_state)
    streams_in = (streams, (STREAMS, LANES, width), wide_map)
    stats_in = (stats, (2 * STREAMS, LANES), row_map)
    gain_in = (gain_own, (STREAMS, width), const(0, 0))
    normed_first, normed_last = call(
        functools.partial(norm_kernel, width_all),
        (token_steps,),
        ins=[streams_in, stats_in, gain_in, (bias_own, (STREAMS, width), const(0, 0))],
        outs=[
            ((STREAMS - 1, tokens, width), BF16, (STREAMS - 1, LANES, width), wide_map),
            ((tokens, width), BF16, (LANES, width), lambda i, p: (i, 0)),
        ],
        name="norm",
    )
    streams_in = (after(streams, normed_last), *streams_in[1:])
    (fixed_part,) = call(
        functools.partial(spread_kernel, width_all),
        (token_steps,),
        ins=[streams_in, stats_in, hist_in],
        outs=[((48, tokens), F32, (48, LANES), row_map)],
        name="spread",
    )

    first_own, first_arrived = gather_start(normed_first)
    first_arrived = [after(arrived, fixed_part) for arrived in first_arrived]
    first_pieces = gather_finish((first_own, first_arrived))
    last_own, last_arrived = gather_start(
        after(normed_last, *[part for parts in first_pieces[1:] for part in parts])
    )

    places = (jnp.arange(tokens, dtype=jnp.int32) % LENGTH).astype(F32)
    freqs = jnp.power(10000.0, -jnp.arange(0, ROT, 2).astype(F32) / ROT)
    angles = places[:, None] * freqs[None, :]
    cosine, sine = jnp.cos(angles), jnp.sin(angles)
    rest = jnp.zeros((tokens, HEAD_DIM - ROT), F32)
    blank = jnp.zeros_like(sine)
    tables = [
        jnp.concatenate([cosine, cosine, rest + 1.0], 1),
        jnp.concatenate([blank, sine, rest], 1),
        jnp.concatenate([-sine, blank, rest], 1),
    ]
    table_ins = [(t, (tokens, HEAD_DIM), const(0, 0)) for t in tables]

    (qkv,) = call(
        functools.partial(qkv_kernel, [len(parts) for parts in first_pieces]),
        (3,),
        ins=[
            (part, (None, *part.shape[1:]), lambda c, p: (c, 0, 0))
            for parts in first_pieces
            for part in parts
        ]
        + [
            (wide_full, (width, heads_width), lambda c, p, r=r: (p[0] ^ r, hidden_steps + c))
            for r in range(count)
        ]
        + table_ins,
        outs=[((3, tokens, heads_width), BF16, (None, tokens, heads_width), lambda c, p: (c, 0, 0))],
        name="qkv",
        flops=6 * tokens * width_all * heads_width,
    )
    head_ins = [
        (qkv, (None, tokens, HEAD_DIM), lambda h, p, c=c: (c, 0, h)) for c in range(3)
    ]
    (attended,) = call(
        attend_kernel,
        (heads,),
        ins=head_ins,
        outs=[((tokens, heads_width), BF16, (tokens, HEAD_DIM), lambda h, p: (0, h))],
        name="attend",
        flops=4 * tokens * tokens * heads_width,
    )
    last_pieces = gather_finish((last_own, [after(arrived, qkv) for arrived in last_arrived]))
    last_pieces[0] = [after(part, attended) for part in last_pieces[0]]
    step = min(512, hidden_width)
    hidden, slope = call(
        functools.partial(up_kernel, [len(parts) for parts in last_pieces]),
        (hidden_width // step,),
        ins=[(part, part.shape, const(0, 0)) for parts in last_pieces for part in parts]
        + [(wide_full, (width, step), lambda j, p, r=r: (p[0] ^ r, j)) for r in range(count)],
        outs=[((tokens, hidden_width), BF16, (tokens, step), lambda j, p: (0, j))] * 2,
        name="up",
        flops=2 * tokens * width_all * hidden_width,
    )
    member = (group_ids[:, None] == jnp.arange(group_weight.shape[0])[None, :]).astype(F32)
    seq_scale = jnp.sum(member * group_weight[None, :], axis=1)
    seed = (mix_cotangent * jnp.repeat(seq_scale, LENGTH)[None, :]).T.astype(BF16)
    factor = jnp.repeat(seq_scale, LENGTH)[:, None]
    seed, factor, mix_full = lax.optimization_barrier((seed, factor, mix_full))
    hidden = after(hidden, seed, factor, mix_full, cot_pieces)
    chunks = 1
    rows = tokens // chunks
    block_owns, block_states, held = [], [], hidden
    for number in range(chunks):
        (branch_pieces,) = call(
            down_kernel,
            (count,),
            ins=[
                (held, (rows, hidden_width), const(number, 0)),
                (attended, (rows, heads_width), const(number, 0)),
                (both_full, (hidden_width, width), lambda r, p: (0, p[0] ^ r)),
                (both_full, (heads_width, width), lambda r, p: (hidden_steps, p[0] ^ r)),
            ],
            outs=[((count, rows, width), BF16, (None, rows, width), lambda r, p: (r, 0, 0))],
            name="down",
            flops=2 * rows * width_all * (hidden_width + heads_width),
        )
        held = after(held, branch_pieces)
        block_states.append(scatter_start(branch_pieces))
    for number in range(chunks):
        residual = streams[STREAMS - 1, number * rows : (number + 1) * rows]
        if number:
            residual = after(residual, *block_states[number - 1][1])
        total = residual + scatter_end(together(scatter_second(together(block_states[number]))))
        block_owns.append(lax.optimization_barrier(total.astype(BF16)))
        block_states[number] = gather_start(block_owns[number])
    block_chunks = [gather_finish(state) for state in block_states]
    block_own = jnp.concatenate(block_owns, 0)
    block_pieces = [[part for chunk in block_chunks for part in chunk[r]] for r in range(count)]

    mid = min(256, tokens)
    branch_grad, block_grad, next_mix, next_part, mix_part = call(
        functools.partial(
            middle_kernel,
            [[part.shape[0] // mid for part in parts] for parts in block_pieces],
            [[part.shape[0] // mid for part in parts] for parts in cot_pieces],
            width_all,
        ),
        (tokens // mid,),
        ins=spans(block_pieces, mid)
        + spans(cot_pieces, mid)
        + [(mix_full, (width, mix_out), other(r, 0)) for r in range(count)]
        + [
            (next_weight, next_weight.shape, const(0, 0)),
            (seed, (mid, mix_out), lambda i, p: (i, 0)),
            (factor, (mid, 1), lambda i, p: (i, 0)),
        ],
        outs=[
            ((tokens, width_all), BF16, (mid, width_all), lambda i, p: (i, 0)),
            ((tokens, width), F32, (mid, width), lambda i, p: (i, 0)),
            ((mix_out, tokens), F32, (mix_out, mid), row_map),
            ((mix_out, mix_out), F32, (mix_out, mix_out), const(0, 0)),
            ((mix_out, width_all), F32, (mix_out, width_all), const(0, 0)),
        ],
        name="middle",
        flops=6 * tokens * width_all * mix_out,
    )

    last_step = hidden_steps - 1
    mix_rows = -(-mix_out // 16) * 16
    branch_in = (branch_grad, (tokens, width_all), const(0, 0))
    (both_part,) = call(
        functools.partial(down_grad_kernel, hidden_steps),
        (hidden_steps + 1,),
        ins=[
            (hidden, (tokens, heads_width), lambda j, p: (0, jnp.minimum(j, last_step))),
            (attended, (tokens, heads_width), const(0, 0)),
            branch_in,
        ],
        outs=[
            (
                (hidden_width + heads_width + mix_rows, width_all),
                BF16,
                (heads_width, width_all),
                lambda j, p: (j, 0),
            )
        ],
        name="down_grad",
        flops=2 * tokens * width_all * (hidden_width + heads_width),
    )
    both_part = lax.dynamic_update_slice_in_dim(
        both_part,
        jnp.pad(mix_part, ((0, mix_rows - mix_out), (0, 0))).astype(BF16),
        hidden_width + heads_width,
        0,
    )
    branch_grad = after(branch_grad, both_part)
    branch_in = (branch_grad, (tokens, width_all), const(0, 0))
    tensor_bits = axis_bits("tensor")
    (attended_grad,) = call(
        back_kernel,
        (tokens // ROWS,),
        ins=[
            (branch_grad, (ROWS, width_all), lambda i, p: (i, 0)),
            (both_full, (heads_width, width_all), const(hidden_steps, 0)),
        ],
        outs=[((tokens, heads_width), BF16, (ROWS, heads_width), lambda i, p: (i, 0))],
        name="attended_grad",
        flops=2 * tokens * width_all * heads_width,
    )
    lin_grads = pl.pallas_call(
        attend_back_kernel,
        out_shape=jax.ShapeDtypeStruct((3, tokens, heads_width), BF16),
        grid_spec=pltpu.PrefetchScalarGridSpec(
            num_scalar_prefetch=1,
            grid=(heads,),
            in_specs=[pl.BlockSpec(b, m) for _, b, m in head_ins]
            + [pl.BlockSpec((tokens, HEAD_DIM), lambda h, p: (0, h))]
            + [pl.BlockSpec(b, m) for _, b, m in table_ins],
            out_specs=pl.BlockSpec((3, tokens, HEAD_DIM), lambda h, p: (0, 0, h)),
            scratch_shapes=[pltpu.VMEM((tokens, HEAD_DIM), F32)] * 2,
        ),
        compiler_params=pltpu.CompilerParams(vmem_limit_bytes=VMEM_BYTES),
        cost_estimate=pl.CostEstimate(
            flops=10 * tokens * tokens * heads_width,
            bytes_accessed=8 * tokens * heads_width * 2,
            transcendentals=heads * tokens * tokens,
        ),
        name="attend_back",
    )(place, qkv, qkv, qkv, attended_grad, *tables)
    def qkv_back(grads, begin, end):
        return call(
            back_kernel,
            (end - begin, count),
            ins=[
                (grads, (None, tokens, heads_width), lambda c, r, p: (c + begin, 0, 0)),
                (
                    wide_full,
                    (width, heads_width),
                    lambda c, r, p: (p[0] ^ r, hidden_steps + c + begin),
                ),
            ],
            outs=[
                (
                    (count, end - begin, tokens, width),
                    BF16,
                    (None, None, tokens, width),
                    lambda c, r, p: (r, c, 0, 0),
                )
            ],
            name="qkv_back",
            flops=2 * (end - begin) * tokens * width_all * heads_width,
        )[0]

    grads_a = qkv_back(lin_grads, 0, 1)
    states_a = scatter_start(grads_a)
    lin_grads = after(lin_grads, grads_a)
    grads_b = qkv_back(lin_grads, 1, 3)
    states_b = scatter_start(grads_b)
    branch_grad = after(branch_grad, grads_b)
    branch_in = (branch_grad, (tokens, width_all), const(0, 0))
    (hidden_grad,) = call(
        hidden_grad_kernel,
        (hidden_steps,),
        ins=[
            branch_in,
            (both_full, (heads_width, width_all), lambda j, p: (j, 0)),
            (slope, (tokens, heads_width), lambda j, p: (0, j)),
        ],
        outs=[((tokens, hidden_width), BF16, (tokens, heads_width), lambda j, p: (0, j))],
        name="hidden_grad",
        flops=2 * tokens * width_all * hidden_width,
    )
    hidden_grad = after(hidden_grad, *scatter_arrived(states_a))
    (last_grads,) = call(
        back_kernel,
        (count,),
        ins=[
            (hidden_grad, (tokens, hidden_width), const(0, 0)),
            (wide_full, (width, hidden_width), lambda r, p: (p[0] ^ r, 0)),
        ],
        outs=[((count, tokens, width), BF16, (None, tokens, width), lambda r, p: (r, 0, 0))],
        name="up_back",
        flops=2 * tokens * width_all * hidden_width,
    )
    last_states = scatter_start(last_grads)
    next_bits = axis_bits("dp")
    fixed_got = swap(after(fixed_part, hidden_grad), "tensor", tensor_bits[0])
    next_got = swap(after(next_part, hidden_grad), "dp", next_bits[0])
    hidden_grad = after(hidden_grad, last_grads)
    all_steps = hidden_steps + 3
    lin_step = lambda j: jnp.maximum(j - hidden_steps, 0)
    (wide_part,) = call(
        functools.partial(
            weight_grad_kernel, [len(parts) for parts in last_pieces], hidden_steps
        ),
        (all_steps,),
        ins=[(part, part.shape, const(0, 0)) for parts in last_pieces for part in parts]
        + [
            (part, (None, *part.shape[1:]), lambda j, p: (lin_step(j), 0, 0))
            for parts in first_pieces
            for part in parts
        ]
        + [
            (
                hidden_grad,
                (tokens, heads_width),
                lambda j, p: (0, jnp.minimum(j, hidden_steps - 1)),
            ),
            (lin_grads, (None, tokens, heads_width), lambda j, p: (lin_step(j), 0, 0)),
        ],
        outs=[
            (
                (width_all, all_steps * heads_width),
                BF16,
                (width_all, heads_width),
                lambda j, p: (0, j),
            )
        ],
        name="weight_grad",
        flops=2 * tokens * width_all * (hidden_width + 3 * heads_width),
        scratch=[((count, width, tokens), BF16)],
    )
    wide_part = after(
        wide_part,
        *scatter_arrived(states_b),
        *scatter_arrived(last_states),
    )
    fixed_sums = fixed_part + fixed_got
    for bit in tensor_bits[1:]:
        fixed_sums = fixed_sums + swap(fixed_sums, "tensor", bit)
    next_sum = next_part + next_got
    next_sum = next_sum + swap(next_sum, "dp", next_bits[1])
    together(states_b + last_states)
    later = [scatter_second(states) for states in (states_a, states_b, last_states)]
    together([state for states in later for state in states] + [[None, None, next_sum]])
    first_grad = jnp.concatenate([scatter_end(later[0]), scatter_end(later[1])], 0)
    last_grad = scatter_end(later[2])
    both_grad = lax.psum_scatter(both_part, "dp", scatter_dimension=1, tiled=True).astype(F32)
    out_end = hidden_width + heads_width
    down_grad, out_grad = both_grad[:hidden_width], both_grad[hidden_width:out_end]
    mix_proj_grad = both_grad[out_end : out_end + mix_out].T
    wide_grad = lax.psum_scatter(wide_part, "dp", scatter_dimension=0, tiled=True).astype(F32)
    up_grad = wide_grad[:, :hidden_width]
    qkv_grad = jnp.stack(
        [
            wide_grad[:, hidden_width + c * heads_width : hidden_width + (c + 1) * heads_width]
            for c in range(3)
        ]
    )

    grad_ins = [
        (first_grad, (STREAMS - 1, LANES, width), wide_map),
        (last_grad, (LANES, width), lambda i, p: (i, 0)),
        streams_in,
        stats_in,
        gain_in,
    ]
    block_grad_in = (block_grad, (LANES, width), lambda i, p: (i, 0))
    sums, norm_part = call(
        functools.partial(sums_kernel, width_all),
        (token_steps,),
        ins=grad_ins + [hist_in, block_grad_in],
        outs=[
            ((48, tokens), F32, (48, LANES), row_map),
            ((2 * STREAMS, width), F32, (2 * STREAMS, width), const(0, 0)),
        ],
        name="sums",
    )
    dp_bits = axis_bits("dp")
    sums = sums + swap(sums, "tensor", tensor_bits[0])
    norm_part = norm_part + swap(norm_part, "dp", dp_bits[0])
    for bit in next_bits[2:]:
        next_sum = next_sum + swap(next_sum, "dp", bit)
    sums, norm_part, next_sum = lax.optimization_barrier((sums, norm_part, next_sum))
    for bit in tensor_bits[1:]:
        sums = sums + swap(sums, "tensor", bit)
    norm_part = norm_part + swap(norm_part, "dp", dp_bits[1])
    sums, norm_part = lax.optimization_barrier((sums, norm_part))
    pairs = STREAMS * ENTRIES
    feature_sums = sums[pairs : pairs + 2 * STREAMS]
    (history_grad,) = call(
        functools.partial(history_kernel, width_all),
        (token_steps,),
        ins=grad_ins
        + [(feature_sums, (2 * STREAMS, LANES), row_map), coef_in, block_grad_in],
        outs=[((ENTRIES, tokens, width), F32, (ENTRIES, LANES, width), wide_map)],
        name="history",
    )
    center = stats[:STREAMS] / width_all
    spread = lax.rsqrt(stats[STREAMS:] / width_all - center * center + ln_eps)
    mix_grad = (
        sums[:pairs].reshape(STREAMS, ENTRIES, tokens)
        - (spread * feature_sums[:STREAMS] / width_all)[:, None]
        * fixed_sums[None, pairs : pairs + ENTRIES]
        - (spread * feature_sums[STREAMS:] / width_all)[:, None]
        * fixed_sums[:pairs].reshape(STREAMS, ENTRIES, tokens)
    ).reshape(pairs, tokens)

    for bit in dp_bits[2:]:
        norm_part = norm_part + swap(norm_part, "dp", bit)
    norm_whole = lax.dynamic_update_slice_in_dim(
        jnp.zeros((2 * STREAMS, width_all), F32), norm_part, tensor_place * width, 1
    )
    norm_whole = butterfly_sum(norm_whole, "tensor")
    norm_whole = lax.dynamic_slice_in_dim(norm_whole, dp_place * share, share, 1)
    next_proj_grad = next_sum
    return (
        block_own,
        next_mix,
        history_grad,
        mix_grad,
        qkv_grad,
        out_grad,
        up_grad,
        down_grad,
        norm_whole[:STREAMS],
        norm_whole[STREAMS:],
        mix_proj_grad,
        next_proj_grad,
    )


def solution(mesh):
    placed = (
        P(None, "dp", "tensor"),
        P(None, "dp"),
        P("dp"),
        P(),
        P("dp", "tensor"),
        P(None, "dp"),
        P(None, "dp", "tensor"),
        P("tensor", "dp"),
        P("dp", "tensor"),
        P("tensor", "dp"),
        P(None, "dp"),
        P(None, "dp"),
        P("dp", None),
        P(),
    )
    return jax.shard_map(
        per_device,
        mesh=mesh,
        in_specs=placed,
        out_specs=(
            P("dp", "tensor"),
            P(None, "dp"),
            P(None, "dp", "tensor"),
            P(None, "dp"),
            P(None, "dp", "tensor"),
            P("tensor", "dp"),
            P("dp", "tensor"),
            P("tensor", "dp"),
            P(None, "dp"),
            P(None, "dp"),
            P("dp", None),
            P(),
        ),
        check_vma=False,
    )
```
